256 devices in a mesh: cond: 4 (over z_hi), px: 64 (over z_lo, x, y, core).
Axes of the slice: x: 4, y: 4, z: 8 (z_hi: 4, z_lo: 2; z = z_hi * 2 + z_lo), core: 2. Of those that a mesh axis runs over, the one named last changes fastest.
Arguments:
- mask_level: float32 [8192, 8192], P('px'), may hold values from -6 to 6
- socs_kernels: float32 [4, 12, 2, 256, 256], P('cond'), may hold values from -3 to 3
- band_cutoff: int32 [4, 12], P('cond'), may hold values from 64 to 128
- kernel_weight: float32 [4, 12], P('cond'), may hold values from 0.05 to 1
- dose_scale: float32 [4], P('cond'), may hold values from 0.7 to 1.4
- shape_corner: int32 [256, 2], replicated, may hold values from 0 to 2047
- shape_extent: int32 [256, 2], replicated, may hold values from 32 to 160
Outputs:
- mask_gradient: float32 [8192, 8192], P('px', 'cond')
The draws below stay inside these ranges and needn't reach their ends.
All inputs are finite; a program needn't handle non-finite values.
Results may differ from the reference program's by a relative error of at most 0.00011.
Values sent between devices are 32-bit elements; how exact they have to be, the bound alone decides.
No kernel may reach another device: no remote copies, remote signals or barrier semaphores. Data moves between devices by JAX's collectives and lax.ppermute only.
A program may use at most 192 MiB of HBM per device.

```python
import math
import jax
import jax.numpy as jnp
from jax import lax

GRID = 8192
IMAGE = 2048
BAND = 256
KERN = 12
RECTS = 256
COND = 4
N_COND = 4


def touch_ends(entries, rng, least, high):
    longest = entries.shape.index(max(entries.shape))
    spots = []
    for shift in (0, 1):
        where = [jax.random.randint(jax.random.fold_in(rng, axis), (), 0, length) for axis, length in enumerate(entries.shape)]
        where[longest] = (where[longest] + shift) % entries.shape[longest]
        spots.append(tuple(where))
    return entries.at[spots[0]].set(least).at[spots[1]].set(high)


def steps_of(stream_key, shape, shards, low, high):
    gain, own = 1.0, jax.random.fold_in(stream_key, 6)
    for position, parts in shards:
        draws = jnp.exp(jax.random.uniform(jax.random.fold_in(own, position), (parts,), jnp.float32, low / len(shards), high / len(shards)))
        gain = gain * jnp.repeat(draws, shape[position] // parts).reshape([-1 if axis == position else 1 for axis in range(len(shape))])
    return gain


def scatter_about(own_key, extent, spread, bound, shards=(), kind=jnp.bfloat16):
    gain = steps_of(own_key, extent, shards, -0.22, 0.18) if shards else 1.0
    values = jax.random.normal(own_key, extent, jnp.float32) * spread * gain
    return jnp.minimum(jnp.maximum(values, -bound), bound).astype(kind)


def setup_inputs(seed: int = 0) -> dict:
    splits = jax.random.split(jax.random.key(seed), 8)
    mask_level = scatter_about(splits[0], (GRID, GRID), 1.0, 6.0, ((0, 64),), jnp.float32)
    socs_kernels = scatter_about(splits[1], (COND, KERN, 2, BAND, BAND), 0.5, 3.0, ((0, 4),), jnp.float32)
    band_cutoff = touch_ends(jax.random.randint(splits[2], (COND, KERN), BAND // 4, BAND // 2 + 1), jax.random.fold_in(splits[2], 1), BAND // 4, (BAND // 2 + 1) - 1).astype(jnp.int32)
    kernel_weight = jnp.clip(jnp.exp(math.log(1.0) - 2.9957323 * jax.random.uniform(splits[3], (COND, KERN), jnp.float32) ** steps_of(splits[3], (COND, KERN), ((0, 4),), -0.2, 0.2)), 0.05, 1.0)
    dose_scale = jnp.clip(0.7 + 0.7 * jax.random.uniform(splits[4], (COND,), jnp.float32) ** steps_of(splits[4], (COND,), ((0, 4),), -0.2, 0.2), 0.7, 1.4)
    shape_corner = touch_ends(jax.random.randint(splits[5], (RECTS, 2), 0, IMAGE), jax.random.fold_in(splits[5], 1), 0, IMAGE - 1).astype(jnp.int32)
    shape_extent = touch_ends(jax.random.randint(splits[6], (RECTS, 2), IMAGE // 64, IMAGE * 5 // 64 + 1), jax.random.fold_in(splits[6], 1), IMAGE // 64, (IMAGE * 5 // 64 + 1) - 1).astype(jnp.int32)
    return dict(mask_level=mask_level, socs_kernels=socs_kernels, band_cutoff=band_cutoff, kernel_weight=kernel_weight, dose_scale=dose_scale, shape_corner=shape_corner, shape_extent=shape_extent)


highest = lax.Precision.HIGHEST
steepness = 6.0
threshold = 0.3

def band_index(length, band):
    return ((jnp.arange(band, dtype=jnp.int32) - band // 2) % length).astype(jnp.int32)

def rasterize(shape_corner, shape_extent):
    places = jnp.arange(IMAGE, dtype=jnp.int32)[None, :]
    rows_in = ((places >= shape_corner[:, 0:1]) & (places < shape_corner[:, 0:1] + shape_extent[:, 0:1])).astype(jnp.float32)
    cols_in = ((places >= shape_corner[:, 1:2]) & (places < shape_corner[:, 1:2] + shape_extent[:, 1:2])).astype(jnp.float32)
    coverage = jnp.dot(rows_in.T, cols_in, precision=highest, preferred_element_type=jnp.float32)
    return jnp.minimum(coverage, 1.0)

def reference(mask_level, socs_kernels, band_cutoff, kernel_weight, dose_scale, shape_corner, shape_extent):
    target = rasterize(shape_corner, shape_extent)
    offsets = jnp.arange(BAND, dtype=jnp.int32) - BAND // 2
    radius_sq = offsets[:, None] * offsets[None, :] * 0 + offsets[:, None] * offsets[:, None] + offsets[None, :] * offsets[None, :]
    inside = radius_sq[None, None] <= (band_cutoff * band_cutoff)[:, :, None, None]
    kernel_re = jnp.where(inside, socs_kernels[:, :, 0], 0.0)
    kernel_im = jnp.where(inside, socs_kernels[:, :, 1], 0.0)
    index_grid = band_index(GRID, BAND)
    index_image = band_index(IMAGE, BAND)

    def objective(levels):
        transmit = jnp.tanh(levels)
        spectrum_full = jnp.fft.fft2(transmit)
        spectrum = jnp.take(jnp.take(spectrum_full, index_grid, axis=0), index_grid, axis=1) / GRID
        loss_sum = jnp.zeros((), transmit.dtype)
        for condition in range(N_COND):

            def add_kernel(intensity, items):
                part_re, part_im, weight = items
                product = (part_re + 1j * part_im) * spectrum
                padded_grid = jnp.zeros((IMAGE, IMAGE), product.dtype)
                padded_grid = padded_grid.at[index_image[:, None], index_image[None, :]].set(product)
                aerial = jnp.fft.ifft2(padded_grid) * (IMAGE * IMAGE / BAND)
                return (intensity + weight * (aerial.real * aerial.real + aerial.imag * aerial.imag), None)
            start_int = jnp.zeros((IMAGE, IMAGE), jnp.float32)
            intensity, unused = lax.scan(add_kernel, start_int, (kernel_re[condition], kernel_im[condition], kernel_weight[condition]))
            resist = jax.nn.sigmoid(steepness * (dose_scale[condition] * intensity - threshold))
            differ = resist - target
            loss_sum = loss_sum + jnp.sum(differ * differ)
        return loss_sum * (GRID / BAND)
    return jax.grad(objective)(mask_level)
```

```python
import functools
import math

import jax
import jax.numpy as jnp
import numpy as np
from jax import lax
from jax.experimental import pallas as pl
from jax.experimental.pallas import tpu as pltpu
from jax.sharding import PartitionSpec as P

IMAGE = 2048
LANES = 128
steepness = 6.0
threshold = 0.3
f32 = jnp.float32
bf16 = jnp.bfloat16


def basis_slots(band):
    half = band // 2
    slots = np.arange(band)
    is_sin = (slots >= half) & (slots < band - 1)
    freq = np.where(slots < half, slots, np.where(is_sin, slots - (half - 1), half))
    return freq, is_sin


def basis_tables(band, width):
    freq, is_sin = basis_slots(band)
    fine = 2.0 * np.pi * ((np.arange(LANES)[:, None] * freq[None]) % width) / width
    big = 2.0 * np.pi * ((LANES * np.arange(width // LANES)[:, None] * freq[None]) % width) / width
    first = np.where(is_sin, np.sin(big), np.cos(big))
    second = np.where(is_sin, np.cos(big), -np.sin(big))
    edge = np.sin(2.0 * np.pi * ((np.arange(LANES) * (band // 2)) % width) / width)
    tables = (first, second, np.cos(fine), np.sin(fine))
    return tuple(table.astype(np.float32) for table in tables), edge.astype(np.float32)


def fold_table(band):
    half = band // 2
    both = np.zeros((2 * band, band), np.float32)
    for place in range(band):
        freq = place - half
        size = abs(freq)
        both[place, size if size < half else band - 1] = 1.0
        if 0 < size < half:
            both[band + place, half - 1 + size] = -1.0 if freq > 0 else 1.0
    return both


def wave(places, band, period):
    offsets = np.arange(band) - band // 2
    angle = 2.0 * np.pi * ((places[:, None] * offsets[None, :]) % period) / period
    return np.cos(angle), np.sin(angle)


def resample_table(band, image):
    coarse = 2 * band
    period = 2 * image
    base = np.arange(period)
    row = np.ones(period)
    for freq in range(1, band):
        row += 2.0 * np.cos(2.0 * np.pi * ((base * freq) % period) / period)
    row /= coarse
    place = (2 * np.arange(band) + 1) * (image // coarse)
    columns = 2 * np.arange(image)
    plus = row[(columns[None, :] - place[:, None]) % period]
    minus = row[(columns[None, :] + place[:, None]) % period]
    return np.concatenate([plus, minus], axis=0)


def halves(table):
    table = np.asarray(table, np.float32)
    top = table.astype(bf16)
    rest = (table - top.astype(np.float32)).astype(bf16)
    return top, rest


def split(value):
    top = value.astype(bf16)
    return top, (value - top.astype(f32)).astype(bf16)


def dot(left, right, left_dim=1, right_dim=0):
    return lax.dot_general(
        left, right, (((left_dim,), (right_dim,)), ((), ())), preferred_element_type=f32
    )


def dot_split(left, right, left_dim=1, right_dim=0):
    go = functools.partial(dot, left_dim=left_dim, right_dim=right_dim)
    return go(left[0], right[0]) + (go(left[1], right[0]) + go(left[0], right[1]))


def basis_rows(tables, start, blocks):
    first, second, fine_cos, fine_sin = tables
    parts = []
    for block in range(blocks):
        a = first[pl.ds(start + block, 1), :]
        b = second[pl.ds(start + block, 1), :]
        parts.append(a * fine_cos[...] + b * fine_sin[...])
    return parts[0] if blocks == 1 else jnp.concatenate(parts, axis=0)


def put(array, row, column, value):
    rows = lax.broadcasted_iota(jnp.int32, array.shape, 0)
    columns = lax.broadcasted_iota(jnp.int32, array.shape, 1)
    return jnp.where((rows == row) & (columns == column), value, array)


def store_pieces(out, array):
    band = array.shape[1]
    pieces = [array[:, place : place + LANES] for place in range(0, band, LANES)]
    flat = pieces[0] if len(pieces) == 1 else jnp.concatenate(pieces, axis=0)
    out[...] = flat.reshape(out.shape)


def load_pieces(ref, band):
    flat = ref[...].reshape(band * band // LANES, LANES)
    pieces = [flat[place : place + band] for place in range(0, flat.shape[0], band)]
    return pieces[0] if len(pieces) == 1 else jnp.concatenate(pieces, axis=1)


def mask_kernel(where, mask, first, second, fine_cos, fine_sin, edge_row, edge_col, out, total, side):
    step = pl.program_id(0)
    band = total.shape[1]
    blocks = mask.shape[1] // LANES
    tables = (first, second, fine_cos, fine_sin)

    @pl.when(step == 0)
    def _():
        total[...] = jnp.zeros_like(total)
        side[...] = jnp.zeros_like(side)

    transmit = jnp.tanh(mask[...])
    start = where[0] * (blocks * pl.num_programs(0)) + step * blocks
    columns = split(basis_rows(tables, start, blocks))
    total[...] += dot_split(split(transmit), columns)
    side[...] += jnp.sum(transmit, axis=0, keepdims=True)

    @pl.when(step == pl.num_programs(0) - 1)
    def _():
        row_part = total[...]
        rows = split(basis_rows(tables, where[1], 1))
        packed = dot_split(rows, split(row_part), 0, 0)
        edge_u = jnp.sum(edge_col[...] * row_part[:, 0:1])
        edge_v = jnp.sum(edge_row[...] * side[...])
        packed = put(put(packed, band - 1, 1, edge_u), 1, band - 1, edge_v)
        store_pieces(out, packed)


def target_kernel(where, corner, extent, corner_row, extent_row, out):
    rows_here, image = out.shape
    count = corner.shape[0]
    top = corner_row[0:1, :]
    rows = where[1] * rows_here + lax.broadcasted_iota(jnp.int32, (rows_here, count), 0)
    rows_in = (rows >= top) & (rows < top + extent_row[0:1, :])
    rows_in = jnp.where(rows_in, 1.0, 0.0).astype(bf16)
    left = corner[:, 1:2]
    right = left + extent[:, 1:2]
    step = min(512, image)
    for place in range(0, image, step):
        columns = place + lax.broadcasted_iota(jnp.int32, (count, step), 1)
        cols_in = jnp.where((columns >= left) & (columns < right), 1.0, 0.0).astype(bf16)
        out[:, place : place + step] = jnp.minimum(dot(rows_in, cols_in), 1.0)


def field_kernel(
    where,
    cutoff,
    weight,
    dose,
    packed,
    kernels,
    both,
    both_t,
    y_big,
    y_fine,
    x_hi,
    x_lo,
    up_hi,
    up_lo,
    target,
    out,
    kern,
    radius,
    spec,
    y_rows,
    y_cols,
    prod_hi,
    prod_lo,
    wide_hi,
    wide_lo,
    deep_hi,
    deep_lo,
    cs,
    gain,
    back,
    gs,
    sems,
    *,
    width,
):
    count, _, band, _ = kern.shape
    rows_here, image = target.shape
    half = band // 2
    total_rows = count * rows_here
    part = 64

    def copy(place):
        return pltpu.make_async_copy(kernels.at[0, place], kern.at[place], sems.at[place])

    for place in range(count):
        copy(place).start()

    big_cos = y_big[0, pl.ds(where[1], 1), :]
    big_sin = y_big[1, pl.ds(where[1], 1), :]
    cos_y = (big_cos * y_fine[0] - big_sin * y_fine[1]) * (1.0 / band)
    sin_y = (big_sin * y_fine[0] + big_cos * y_fine[1]) * (1.0 / band)
    table = jnp.concatenate(
        [
            jnp.concatenate([cos_y, 0.0 - sin_y], axis=1),
            jnp.concatenate([sin_y, cos_y], axis=1),
        ],
        axis=0,
    )
    table_hi, table_lo = split(table)
    y_rows[...] = jnp.concatenate([table_hi, table_lo], axis=0)
    table_hi, table_lo = table_hi.astype(f32), table_lo.astype(f32)
    stacked = jnp.concatenate([table_hi, table_hi, table_lo], axis=0)
    y_cols[...] = jnp.transpose(stacked).astype(bf16)
    fu = lax.broadcasted_iota(jnp.int32, (band, band), 0) - half
    fv = lax.broadcasted_iota(jnp.int32, (band, band), 1) - half
    radius[...] = fu * fu + fv * fv
    gs[...] = jnp.zeros_like(gs)

    box = load_pieces(packed, band)
    edge_u = box[band - 1 : band, 1:2] * (1.0 / width)
    edge_v = box[1:2, band - 1 : band] * (1.0 / width)
    box_hi, box_lo = split(box * (1.0 / width))
    opened = dot(both[...], box_hi) + dot(both[...], box_lo)
    box_hi, box_lo = split(opened)
    opened = dot(box_hi, both[...], 1, 1) + dot(box_lo, both[...], 1, 1)
    spec_im = opened[band:, :band] + opened[:band, band:]
    spec[0] = opened[:band, :band] - opened[band:, band:]
    at_u = (fu == -half) & (fv == 0)
    at_v = (fu == 0) & (fv == -half)
    spec[1] = spec_im + jnp.where(at_u, edge_u, 0.0) + jnp.where(at_v, edge_v, 0.0)

    def forward(place, carry):
        copy(place).wait()
        limit = cutoff[0, place]
        limit = limit * limit
        for start in range(0, band, part):
            here = pl.ds(start, part)
            inside = radius[here, :] <= limit
            k_re = jnp.where(inside, kern[place, 0, here, :], 0.0)
            k_im = jnp.where(inside, kern[place, 1, here, :], 0.0)
            kern[place, 0, here, :] = k_re
            kern[place, 1, here, :] = k_im
            s_re = spec[0, here, :]
            s_im = spec[1, here, :]
            re_hi, re_lo = split(k_re * s_re - k_im * s_im)
            im_hi, im_lo = split(k_re * s_im + k_im * s_re)
            prod_hi[here, :] = re_hi
            prod_lo[here, :] = re_lo
            there = pl.ds(band + start, part)
            prod_hi[there, :] = im_hi
            prod_lo[there, :] = im_lo
        main = dot(y_rows[...], prod_hi[...])
        rest = dot(y_rows[: 2 * rows_here, :], prod_lo[...])
        value = main[: 2 * rows_here] + (main[2 * rows_here :] + rest)
        hi, lo = split(value)
        here = pl.ds(pl.multiple_of(place * rows_here, rows_here), rows_here)
        there = pl.ds(pl.multiple_of(total_rows + place * rows_here, rows_here), rows_here)
        wide_hi[here, :] = hi[:rows_here]
        wide_lo[here, :] = lo[:rows_here]
        wide_hi[there, :] = hi[rows_here:]
        wide_lo[there, :] = lo[rows_here:]
        return carry

    lax.fori_loop(0, count, forward, 0)

    cs[...] = dot_split((wide_hi[...], wide_lo[...]), (x_hi[...], x_lo[...]))

    def fields(place):
        here = pl.ds(pl.multiple_of(place * rows_here, rows_here), rows_here)
        there = pl.ds(pl.multiple_of(total_rows + place * rows_here, rows_here), rows_here)
        c_re = cs[here, :band]
        s_re = cs[here, band:]
        c_im = cs[there, :band]
        s_im = cs[there, band:]
        return (c_re - s_im, c_im + s_re, c_re + s_im, c_im - s_re), here, there

    def add_power(place, carry):
        plus, minus = carry
        (p_re, p_im, m_re, m_im), _, _ = fields(place)
        scale = weight[0, place]
        return (
            plus + scale * (p_re * p_re + p_im * p_im),
            minus + scale * (m_re * m_re + m_im * m_im),
        )

    zero = jnp.zeros((rows_here, band), f32)
    plus, minus = lax.fori_loop(0, count, add_power, (zero, zero))
    power_hi, power_lo = split(jnp.concatenate([plus, minus], axis=1))
    power = jnp.concatenate([power_hi, power_lo], axis=0)
    dose_here = dose[0]
    scale = 2.0 * (width / band) * steepness * dose_here
    step = min(512, image)
    for place in range(0, image, step):
        here = pl.ds(place, step)
        main = dot(power, up_hi[:, here])
        rest = dot(power_hi, up_lo[:, here])
        intensity = main[:rows_here] + (main[rows_here:] + rest)
        level = steepness * (dose_here * intensity - threshold)
        resist = 1.0 / (1.0 + jnp.exp(0.0 - level))
        slope = scale * (resist - target[:, here]) * resist * (1.0 - resist)
        hi, lo = split(slope)
        gain[:rows_here, here] = hi
        gain[rows_here:, here] = lo
    main = dot(gain[...], up_hi[...], 1, 1)
    rest = dot(gain[:rows_here, :], up_lo[...], 1, 1)
    slope = 2.0 * (main[:rows_here] + (main[rows_here:] + rest))
    slope_plus = slope[:, :band]
    slope_minus = slope[:, band:]

    def pull(place, carry):
        (p_re, p_im, m_re, m_im), here, there = fields(place)
        scale = weight[0, place]
        plus = scale * slope_plus
        minus = scale * slope_minus
        p_re, p_im, m_re, m_im = plus * p_re, plus * p_im, minus * m_re, minus * m_im
        for rows, columns, value in (
            (here, slice(0, band), p_re + m_re),
            (here, slice(band, 2 * band), p_im - m_im),
            (there, slice(0, band), p_im + m_im),
            (there, slice(band, 2 * band), m_re - p_re),
        ):
            hi, lo = split(value)
            deep_hi[rows, columns] = hi
            deep_lo[rows, columns] = lo
        return carry

    lax.fori_loop(0, count, pull, 0)
    back[...] = dot_split((deep_hi[...], deep_lo[...]), (x_hi[...], x_lo[...]), 1, 1)

    def gather(place, carry):
        here = pl.ds(pl.multiple_of(place * rows_here, rows_here), rows_here)
        there = pl.ds(pl.multiple_of(total_rows + place * rows_here, rows_here), rows_here)
        hi, lo = split(jnp.concatenate([back[here, :], back[there, :]], axis=0))
        grad = dot(y_cols[...], jnp.concatenate([hi, lo, hi], axis=0))
        for start in range(0, band, part):
            here = pl.ds(start, part)
            k_re = kern[place, 0, here, :]
            k_im = kern[place, 1, here, :]
            g_re = grad[start : start + part]
            g_im = grad[band + start : band + start + part]
            gs[0, here, :] += k_re * g_re + k_im * g_im
            gs[1, here, :] += k_re * g_im - k_im * g_re
        return carry

    lax.fori_loop(0, count, gather, 0)
    g_re = gs[0]
    g_im = gs[1]
    edge_u = g_im[0:1, half : half + 1]
    edge_v = g_im[half : half + 1, 0:1]
    re_hi, re_lo = split(g_re)
    im_hi, im_lo = split(g_im)
    even, odd = both_t[:, :band], both_t[:, band:]
    left = dot(even, re_hi) + dot(even, re_lo) + dot(odd, im_hi) + dot(odd, im_lo)
    right = dot(even, im_hi) + dot(even, im_lo) - dot(odd, re_hi) - dot(odd, re_lo)
    l_hi, l_lo = split(left)
    r_hi, r_lo = split(right)
    even, odd = both[:band, :], both[band:, :]
    folded = dot(l_hi, even) + dot(l_lo, even) + dot(r_hi, odd) + dot(r_lo, odd)
    store_pieces(out, put(put(folded, band - 1, 1, edge_u), 1, band - 1, edge_v))


def spread_kernel(
    where, mask, packed, first, second, fine_cos, fine_sin, edge_row, edge_col, out, rows_hi, rows_lo, side
):
    step = pl.program_id(0)
    band = rows_hi.shape[1]
    blocks = mask.shape[1] // LANES
    tables = (first, second, fine_cos, fine_sin)
    width = first.shape[0] * LANES

    @pl.when(step == 0)
    def _():
        box = load_pieces(packed, band) * (1.0 / width)
        edge_u = box[band - 1 : band, 1:2]
        edge_v = box[1:2, band - 1 : band]
        box = put(put(box, band - 1, 1, 0.0), 1, band - 1, 0.0)
        mixed = dot_split(split(basis_rows(tables, where[1], 1)), split(box))
        hi, lo = split(mixed)
        rows_hi[: mixed.shape[0], :] = hi
        rows_hi[mixed.shape[0] :, :] = lo
        rows_lo[...] = edge_u * edge_col[...]
        side[...] = edge_v * edge_row[...]

    transmit = jnp.tanh(mask[...])
    start = where[0] * (blocks * pl.num_programs(0)) + step * blocks
    columns_hi, columns_lo = split(basis_rows(tables, start, blocks))
    count = mask.shape[0]
    main = dot(rows_hi[...], columns_hi, 1, 1)
    rest = dot(rows_hi[:count, :], columns_lo, 1, 1)
    grad = main[:count] + (main[count:] + rest) + rows_lo[...] + side[...]
    out[...] = grad * (1.0 - transmit * transmit)


def params():
    return pltpu.CompilerParams(vmem_limit_bytes=48 * 1024 * 1024)


def whole(array):
    rank = len(array.shape)
    return pl.BlockSpec(array.shape, lambda *_: (0,) * rank)


def local(
    mask_level, socs_kernels, band_cutoff, kernel_weight, dose_scale, shape_corner, shape_extent
):
    rows_here, width = mask_level.shape
    count = socs_kernels.shape[1]
    band = socs_kernels.shape[3]
    pencils = lax.axis_size("px")
    conds = lax.axis_size("cond")
    image_rows = IMAGE // pencils
    cols_here = width // conds
    where = jnp.stack([lax.axis_index("cond"), lax.axis_index("px")]).astype(jnp.int32)
    pieces = (pencils, band * band // LANES // pencils, LANES)

    tables, edge = basis_tables(band, width)
    chunk = min(512, cols_here)
    steps = cols_here // chunk
    edge_row = np.tile(edge, chunk // LANES)[None, :]
    edge_col = edge[:, None]
    consts = (*tables, edge_row, edge_col)

    mask_spec = pl.BlockSpec((rows_here, chunk), lambda i, w: (0, w[0] * steps + i))
    packed = pl.pallas_call(
        mask_kernel,
        out_shape=jax.ShapeDtypeStruct(pieces, f32),
        grid_spec=pltpu.PrefetchScalarGridSpec(
            num_scalar_prefetch=1,
            grid=(steps,),
            in_specs=[mask_spec, *(whole(table) for table in consts)],
            out_specs=pl.BlockSpec(pieces, lambda *_: (0, 0, 0)),
            scratch_shapes=[pltpu.VMEM((rows_here, band), f32), pltpu.VMEM((1, chunk), f32)],
        ),
        compiler_params=params(),
        name="mask_rows",
    )(where, mask_level, *consts)

    smem = pl.BlockSpec(memory_space=pltpu.SMEM)
    vmem = pl.BlockSpec(memory_space=pltpu.VMEM)
    target = pl.pallas_call(
        target_kernel,
        out_shape=jax.ShapeDtypeStruct((image_rows, IMAGE), f32),
        in_specs=[smem, vmem, vmem, vmem, vmem],
        out_specs=vmem,
        compiler_params=params(),
        name="target_rows",
    )(where, shape_corner, shape_extent, shape_corner.T, shape_extent.T)

    packed = exchange(packed)

    both = fold_table(band)
    y_big = np.stack(wave(image_rows * np.arange(pencils), band, IMAGE)).astype(np.float32)
    y_fine = np.stack(wave(np.arange(image_rows), band, IMAGE)).astype(np.float32)
    x_cos, x_sin = wave(2 * np.arange(band) + 1, band, 4 * band)
    x_hi, x_lo = halves(np.concatenate([x_cos.T, x_sin.T], axis=1))
    up_hi, up_lo = halves(resample_table(band, IMAGE))
    deep = 2 * count * image_rows
    folded = pl.pallas_call(
        functools.partial(field_kernel, width=width),
        out_shape=jax.ShapeDtypeStruct(pieces, f32),
        in_specs=[smem] * 4 + [vmem, pl.BlockSpec(memory_space=pl.ANY)] + [vmem] * 9,
        out_specs=vmem,
        scratch_shapes=[
            pltpu.VMEM((count, 2, band, band), f32),
            pltpu.VMEM((band, band), jnp.int32),
            pltpu.VMEM((2, band, band), f32),
            pltpu.VMEM((4 * image_rows, 2 * band), bf16),
            pltpu.VMEM((2 * band, 6 * image_rows), bf16),
            pltpu.VMEM((2 * band, band), bf16),
            pltpu.VMEM((2 * band, band), bf16),
            pltpu.VMEM((deep, band), bf16),
            pltpu.VMEM((deep, band), bf16),
            pltpu.VMEM((deep, 2 * band), bf16),
            pltpu.VMEM((deep, 2 * band), bf16),
            pltpu.VMEM((deep, 2 * band), f32),
            pltpu.VMEM((2 * image_rows, IMAGE), bf16),
            pltpu.VMEM((deep, band), f32),
            pltpu.VMEM((2, band, band), f32),
            pltpu.SemaphoreType.DMA((count,)),
        ],
        compiler_params=params(),
        name="image_rows",
    )(
        where,
        band_cutoff,
        kernel_weight,
        dose_scale,
        packed,
        socs_kernels,
        both.astype(bf16),
        both.T.astype(bf16),
        y_big,
        y_fine,
        x_hi,
        x_lo,
        up_hi,
        up_lo,
        target,
    )

    folded = exchange(folded)

    return pl.pallas_call(
        spread_kernel,
        out_shape=jax.ShapeDtypeStruct((rows_here, cols_here), f32),
        grid_spec=pltpu.PrefetchScalarGridSpec(
            num_scalar_prefetch=1,
            grid=(steps,),
            in_specs=[
                mask_spec,
                pl.BlockSpec(pieces, lambda *_: (0, 0, 0)),
                *(whole(table) for table in consts),
            ],
            out_specs=pl.BlockSpec((rows_here, chunk), lambda i, w: (0, i)),
            scratch_shapes=[
                pltpu.VMEM((2 * rows_here, band), bf16),
                pltpu.VMEM((rows_here, 1), f32),
                pltpu.VMEM((1, chunk), f32),
            ],
        ),
        compiler_params=params(),
        name="mask_gradient",
    )(where, mask_level, folded, *consts)


def exchange(packed):
    conds = lax.axis_size("cond")
    arrived = lax.all_to_all(packed, "px", split_axis=0, concat_axis=0, tiled=True)
    piece = jnp.sum(arrived, axis=0)
    others = [
        lax.ppermute(piece, "cond", [(i, (i + d) % conds) for i in range(conds)])
        for d in range(1, conds)
    ]
    piece = functools.reduce(jnp.add, others, piece)
    outgoing = jnp.broadcast_to(piece[None], packed.shape)
    return lax.all_to_all(outgoing, "px", split_axis=0, concat_axis=0, tiled=True)


def solution(mesh):
    in_specs = (
        P("px", None),
        P("cond", None, None, None, None),
        P("cond", None),
        P("cond", None),
        P("cond"),
        P(),
        P(),
    )
    out_specs = P("px", "cond")
    return jax.shard_map(local, mesh=mesh, in_specs=in_specs, out_specs=out_specs, check_vma=False)
```

```python
import functools
import math

import jax
import jax.numpy as jnp
import numpy as np
from jax import lax
from jax.experimental import pallas as pl
from jax.experimental.pallas import tpu as pltpu
from jax.sharding import PartitionSpec as P

IMAGE = 2048
LANES = 128
SLOTS = 2
steepness = 6.0
threshold = 0.3
f32 = jnp.float32
bf16 = jnp.bfloat16


def basis_slots(band):
    half = band // 2
    slots = np.arange(band)
    is_sin = (slots >= half) & (slots < band - 1)
    freq = np.where(slots < half, slots, np.where(is_sin, slots - (half - 1), half))
    return freq, is_sin


def basis_tables(band, width):
    freq, is_sin = basis_slots(band)
    fine = 2.0 * np.pi * ((np.arange(LANES)[:, None] * freq[None]) % width) / width
    big = 2.0 * np.pi * ((LANES * np.arange(width // LANES)[:, None] * freq[None]) % width) / width
    first = np.where(is_sin, np.sin(big), np.cos(big))
    second = np.where(is_sin, np.cos(big), -np.sin(big))
    edge = np.sin(2.0 * np.pi * ((np.arange(LANES) * (band // 2)) % width) / width)
    table = np.concatenate([np.cos(fine), np.sin(fine), first, second], axis=0)
    return table.astype(np.float32), edge.astype(np.float32)


def fold_table(band):
    half = band // 2
    both = np.zeros((2 * band, band), np.float32)
    for place in range(band):
        freq = place - half
        size = abs(freq)
        both[place, size if size < half else band - 1] = 1.0
        if 0 < size < half:
            both[band + place, half - 1 + size] = -1.0 if freq > 0 else 1.0
    return both


def wave(places, band, period):
    offsets = np.arange(band) - band // 2
    angle = 2.0 * np.pi * ((places[:, None] * offsets[None, :]) % period) / period
    return np.cos(angle), np.sin(angle)


def resample_table(band, image):
    coarse = 2 * band
    period = 2 * image
    base = np.arange(period)
    row = np.ones(period)
    for freq in range(1, band):
        row += 2.0 * np.cos(2.0 * np.pi * ((base * freq) % period) / period)
    row /= coarse
    place = (2 * np.arange(band) + 1) * (image // coarse)
    columns = 2 * np.arange(image)
    plus = row[(columns[None, :] - place[:, None]) % period]
    minus = row[(columns[None, :] + place[:, None]) % period]
    return np.concatenate([plus, minus], axis=0)


def halves(table):
    table = np.asarray(table, np.float32)
    top = table.astype(bf16)
    rest = (table - top.astype(np.float32)).astype(bf16)
    return top, rest


def split(value):
    top = value.astype(bf16)
    return top, (value - top.astype(f32)).astype(bf16)


def dot(left, right, left_dim=1, right_dim=0):
    return lax.dot_general(
        left, right, (((left_dim,), (right_dim,)), ((), ())), preferred_element_type=f32
    )


def dot_split(left, right, left_dim=1, right_dim=0):
    go = functools.partial(dot, left_dim=left_dim, right_dim=right_dim)
    return go(left[0], right[0]) + (go(left[1], right[0]) + go(left[0], right[1]))


def basis_rows(table, start, blocks):
    places = (table.shape[0] - 2 * LANES) // 2
    parts = []
    for block in range(blocks):
        a = table[pl.ds(2 * LANES + start + block, 1), :]
        b = table[pl.ds(2 * LANES + places + start + block, 1), :]
        parts.append(a * table[:LANES, :] + b * table[LANES : 2 * LANES, :])
    return parts[0] if blocks == 1 else jnp.concatenate(parts, axis=0)


def put(array, row, column, value):
    rows = lax.broadcasted_iota(jnp.int32, array.shape, 0)
    columns = lax.broadcasted_iota(jnp.int32, array.shape, 1)
    return jnp.where((rows == row) & (columns == column), value, array)


def store_pieces(out, array):
    band = array.shape[1]
    pieces = [array[:, place : place + LANES] for place in range(0, band, LANES)]
    flat = pieces[0] if len(pieces) == 1 else jnp.concatenate(pieces, axis=0)
    out[...] = flat.reshape(out.shape)


def load_pieces(ref, band):
    flat = ref[...].reshape(band * band // LANES, LANES)
    pieces = [flat[place : place + band] for place in range(0, flat.shape[0], band)]
    return pieces[0] if len(pieces) == 1 else jnp.concatenate(pieces, axis=1)


def mask_kernel(where, mask_hbm, table_hbm, edge_row, edge_col, out, mask, table, total, sems):
    count, rows_here, chunk = mask.shape
    band = total.shape[1]
    blocks = chunk // LANES

    def copy(place):
        columns = pl.ds(place * chunk, chunk)
        return pltpu.make_async_copy(mask_hbm.at[:, columns], mask.at[place], sems.at[place])

    copy_table = pltpu.make_async_copy(table_hbm, table, sems.at[count])
    copy(0).start()
    copy_table.start()
    for place in range(1, count):
        copy(place).start()
    copy_table.wait()
    side = jnp.zeros((1, LANES), f32)
    for place in range(count):
        copy(place).wait()
        transmit = jnp.tanh(mask[place])
        columns = split(basis_rows(table, place * blocks, blocks))
        value = dot_split(split(transmit), columns)
        if place == 0:
            total[...] = value
        else:
            total[...] += value
        line = jnp.sum(transmit, axis=0, keepdims=True)
        for start in range(0, chunk, LANES):
            side += line[:, start : start + LANES]
    row_part = total[...]
    rows = split(basis_rows(table, where[1], 1))
    packed = dot_split(rows, split(row_part), 0, 0)
    edge_u = jnp.sum(edge_col[...] * row_part[:, 0:1])
    edge_v = jnp.sum(edge_row[...] * side)
    packed = put(put(packed, band - 1, 1, edge_u), 1, band - 1, edge_v)
    store_pieces(out, packed)


def prepare_kernel(
    where,
    cutoff,
    corner,
    extent,
    corner_row,
    extent_row,
    y_big,
    y_fine,
    after,
    kernels,
    mask_hbm,
    table_hbm,
    target,
    kern,
    y_rows,
    y_cols,
    rows_hi,
    rows_lo,
    cols_hi,
    cols_lo,
    slope,
    table,
    sems,
):
    count, _, band, _ = kern.shape
    rows_here, image = target.shape
    cols_here = slope.shape[1]
    blocks = cols_here // LANES
    half = band // 2
    mine = pl.ds(pl.multiple_of(where[0] * cols_here, cols_here), cols_here)
    copy_table = pltpu.make_async_copy(table_hbm, table, sems.at[count])
    copy_mask = pltpu.make_async_copy(mask_hbm.at[:, mine], slope, sems.at[count + 1])

    def copy(place):
        return pltpu.make_async_copy(kernels.at[0, place], kern.at[place], sems.at[place])

    copy_table.start()
    copy_mask.start()
    for place in range(count):
        copy(place).start()

    rects = corner.shape[0]
    top = corner_row[0:1, :]
    rows = where[1] * rows_here + lax.broadcasted_iota(jnp.int32, (rows_here, rects), 0)
    rows_in = (rows >= top) & (rows < top + extent_row[0:1, :])
    rows_in = jnp.where(rows_in, 1.0, 0.0).astype(bf16)
    left = corner[:, 1:2]
    right = left + extent[:, 1:2]
    step = min(512, image)
    for place in range(0, image, step):
        columns = place + lax.broadcasted_iota(jnp.int32, (rects, step), 1)
        cols_in = jnp.where((columns >= left) & (columns < right), 1.0, 0.0).astype(bf16)
        target[:, place : place + step] = jnp.minimum(dot(rows_in, cols_in), 1.0)

    big_cos = y_big[0, pl.ds(where[1], 1), :]
    big_sin = y_big[1, pl.ds(where[1], 1), :]
    cos_y = (big_cos * y_fine[0] - big_sin * y_fine[1]) * (1.0 / band)
    sin_y = (big_sin * y_fine[0] + big_cos * y_fine[1]) * (1.0 / band)
    waves = jnp.concatenate(
        [
            jnp.concatenate([cos_y, 0.0 - sin_y], axis=1),
            jnp.concatenate([sin_y, cos_y], axis=1),
        ],
        axis=0,
    )
    waves_hi, waves_lo = split(waves)
    y_rows[...] = jnp.concatenate([waves_hi, waves_lo], axis=0)
    waves_hi, waves_lo = waves_hi.astype(f32), waves_lo.astype(f32)
    stacked = jnp.concatenate([waves_hi, waves_hi, waves_lo], axis=0)
    y_cols[...] = jnp.transpose(stacked).astype(bf16)

    copy_table.wait()
    hi, lo = split(basis_rows(table, where[1], 1))
    rows_hi[...] = hi
    rows_lo[...] = lo
    for block in range(blocks):
        here = pl.ds(block * LANES, LANES)
        hi, lo = split(basis_rows(table, where[0] * blocks + block, 1))
        cols_hi[here, :] = hi
        cols_lo[here, :] = lo
    copy_mask.wait()
    for start in range(0, cols_here, LANES):
        here = pl.ds(start, LANES)
        transmit = jnp.tanh(slope[:, here])
        slope[:, here] = 1.0 - transmit * transmit

    part = 64
    for start in range(0, band, part):
        here = pl.ds(start, part)
        fu = start - half + lax.broadcasted_iota(jnp.int32, (part, band), 0)
        fv = lax.broadcasted_iota(jnp.int32, (part, band), 1) - half
        radius = fu * fu + fv * fv
        for place in range(count):
            if start == 0:
                copy(place).wait()
            inside = radius <= cutoff[0, place] * cutoff[0, place]
            kern[place, 0, here, :] = jnp.where(inside, kern[place, 0, here, :], 0.0)
            kern[place, 1, here, :] = jnp.where(inside, kern[place, 1, here, :], 0.0)


def field_kernel(
    weight,
    dose,
    packed,
    kern,
    both,
    both_t,
    x_hi,
    x_lo,
    up_hi,
    up_lo,
    target,
    y_rows,
    y_cols,
    out,
    spec,
    prod_hi,
    prod_lo,
    wide_hi,
    wide_lo,
    deep_hi,
    deep_lo,
    cs,
    gain,
    back,
    gs,
    *,
    width,
):
    count, _, band, _ = kern.shape
    rows_here, image = target.shape
    half = band // 2
    total_rows = count * rows_here
    part = 64
    fu = lax.broadcasted_iota(jnp.int32, (band, band), 0) - half
    fv = lax.broadcasted_iota(jnp.int32, (band, band), 1) - half

    box = load_pieces(packed, band)
    edge_u = box[band - 1 : band, 1:2] * (1.0 / width)
    edge_v = box[1:2, band - 1 : band] * (1.0 / width)
    box_hi, box_lo = split(box * (1.0 / width))
    opened = dot(both[...], box_hi) + dot(both[...], box_lo)
    box_hi, box_lo = split(opened)
    opened = dot(box_hi, both[...], 1, 1) + dot(box_lo, both[...], 1, 1)
    spec_im = opened[band:, :band] + opened[:band, band:]
    spec[0] = opened[:band, :band] - opened[band:, band:]
    at_u = (fu == -half) & (fv == 0)
    at_v = (fu == 0) & (fv == -half)
    spec[1] = spec_im + jnp.where(at_u, edge_u, 0.0) + jnp.where(at_v, edge_v, 0.0)

    for place in range(count):
        slot = place % prod_hi.shape[0]
        for start in range(0, band, part):
            here = pl.ds(start, part)
            there = pl.ds(band + start, part)
            k_re = kern[place, 0, here, :]
            k_im = kern[place, 1, here, :]
            s_re = spec[0, here, :]
            s_im = spec[1, here, :]
            re_hi, re_lo = split(k_re * s_re - k_im * s_im)
            im_hi, im_lo = split(k_re * s_im + k_im * s_re)
            prod_hi[slot, here, :] = re_hi
            prod_lo[slot, here, :] = re_lo
            prod_hi[slot, there, :] = im_hi
            prod_lo[slot, there, :] = im_lo
        main = dot(y_rows[...], prod_hi[slot])
        rest = dot(y_rows[: 2 * rows_here, :], prod_lo[slot])
        hi, lo = split(main[: 2 * rows_here] + (main[2 * rows_here :] + rest))
        here = pl.ds(place * rows_here, rows_here)
        there = pl.ds(total_rows + place * rows_here, rows_here)
        wide_hi[here, :] = hi[:rows_here]
        wide_lo[here, :] = lo[:rows_here]
        wide_hi[there, :] = hi[rows_here:]
        wide_lo[there, :] = lo[rows_here:]

    cs[...] = dot_split((wide_hi[...], wide_lo[...]), (x_hi[...], x_lo[...]))

    def fields(place):
        here = pl.ds(place * rows_here, rows_here)
        there = pl.ds(total_rows + place * rows_here, rows_here)
        c_re = cs[here, :band]
        s_re = cs[here, band:]
        c_im = cs[there, :band]
        s_im = cs[there, band:]
        return (c_re - s_im, c_im + s_re, c_re + s_im, c_im - s_re), here, there

    plus = jnp.zeros((rows_here, band), f32)
    minus = jnp.zeros((rows_here, band), f32)
    for place in range(count):
        (p_re, p_im, m_re, m_im), _, _ = fields(place)
        scale = weight[0, place]
        plus += scale * (p_re * p_re + p_im * p_im)
        minus += scale * (m_re * m_re + m_im * m_im)
    power_hi, power_lo = split(jnp.concatenate([plus, minus], axis=1))
    power = jnp.concatenate([power_hi, power_lo], axis=0)
    dose_here = dose[0]
    scale = 2.0 * (width / band) * steepness * dose_here
    step = min(512, image)
    for place in range(0, image, step):
        here = pl.ds(place, step)
        main = dot(power, up_hi[:, here])
        rest = dot(power_hi, up_lo[:, here])
        intensity = main[:rows_here] + (main[rows_here:] + rest)
        level = steepness * (dose_here * intensity - threshold)
        resist = 1.0 / (1.0 + jnp.exp(0.0 - level))
        slope = scale * (resist - target[:, here]) * resist * (1.0 - resist)
        hi, lo = split(slope)
        gain[:rows_here, here] = hi
        gain[rows_here:, here] = lo
    main = dot(gain[...], up_hi[...], 1, 1)
    rest = dot(gain[:rows_here, :], up_lo[...], 1, 1)
    slope = 2.0 * (main[:rows_here] + (main[rows_here:] + rest))
    slope_plus = slope[:, :band]
    slope_minus = slope[:, band:]

    for place in range(count):
        (p_re, p_im, m_re, m_im), here, there = fields(place)
        scale = weight[0, place]
        plus = scale * slope_plus
        minus = scale * slope_minus
        p_re, p_im, m_re, m_im = plus * p_re, plus * p_im, minus * m_re, minus * m_im
        for rows, columns, value in (
            (here, slice(0, band), p_re + m_re),
            (here, slice(band, 2 * band), p_im - m_im),
            (there, slice(0, band), p_im + m_im),
            (there, slice(band, 2 * band), m_re - p_re),
        ):
            hi, lo = split(value)
            deep_hi[rows, columns] = hi
            deep_lo[rows, columns] = lo
    back[...] = dot_split((deep_hi[...], deep_lo[...]), (x_hi[...], x_lo[...]), 1, 1)

    for place in range(count):
        here = pl.ds(place * rows_here, rows_here)
        there = pl.ds(total_rows + place * rows_here, rows_here)
        hi, lo = split(jnp.concatenate([back[here, :], back[there, :]], axis=0))
        grad = dot(y_cols[...], jnp.concatenate([hi, lo, hi], axis=0))
        for start in range(0, band, part):
            here = pl.ds(start, part)
            k_re = kern[place, 0, here, :]
            k_im = kern[place, 1, here, :]
            g_re = grad[start : start + part]
            g_im = grad[band + start : band + start + part]
            if place == 0:
                gs[0, here, :] = k_re * g_re + k_im * g_im
                gs[1, here, :] = k_re * g_im - k_im * g_re
            else:
                gs[0, here, :] += k_re * g_re + k_im * g_im
                gs[1, here, :] += k_re * g_im - k_im * g_re
    g_re = gs[0]
    g_im = gs[1]
    edge_u = g_im[0:1, half : half + 1]
    edge_v = g_im[half : half + 1, 0:1]
    re_hi, re_lo = split(g_re)
    im_hi, im_lo = split(g_im)
    even, odd = both_t[:, :band], both_t[:, band:]
    left = dot(even, re_hi) + dot(even, re_lo) + dot(odd, im_hi) + dot(odd, im_lo)
    right = dot(even, im_hi) + dot(even, im_lo) - dot(odd, re_hi) - dot(odd, re_lo)
    l_hi, l_lo = split(left)
    r_hi, r_lo = split(right)
    even, odd = both[:band, :], both[band:, :]
    folded = dot(l_hi, even) + dot(l_lo, even) + dot(r_hi, odd) + dot(r_lo, odd)
    store_pieces(out, put(put(folded, band - 1, 1, edge_u), 1, band - 1, edge_v))


def spread_kernel(packed, slope, rows_hi, rows_lo, cols_hi, cols_lo, edge_row, edge_col, out, *, width):
    band = rows_hi.shape[1]
    count, cols_here = out.shape
    box = load_pieces(packed, band) * (1.0 / width)
    edge_u = box[band - 1 : band, 1:2]
    edge_v = box[1:2, band - 1 : band]
    box = put(put(box, band - 1, 1, 0.0), 1, band - 1, 0.0)
    mixed_hi, mixed_lo = split(dot_split((rows_hi[...], rows_lo[...]), split(box)))
    mixed = jnp.concatenate([mixed_hi, mixed_lo], axis=0)
    side = edge_u * edge_col[...] + edge_v * edge_row[...]
    step = min(512, cols_here)
    for start in range(0, cols_here, step):
        here = pl.ds(start, step)
        main = dot(mixed, cols_hi[here, :], 1, 1)
        rest = dot(mixed_hi, cols_lo[here, :], 1, 1)
        grad = main[:count] + (main[count:] + rest)
        for inner in range(0, step, LANES):
            there = pl.ds(start + inner, LANES)
            out[:, there] = (grad[:, inner : inner + LANES] + side) * slope[:, there]


def params(mebibytes):
    return pltpu.CompilerParams(vmem_limit_bytes=mebibytes * 1024 * 1024)


smem = pl.BlockSpec(memory_space=pltpu.SMEM)
vmem = pl.BlockSpec(memory_space=pltpu.VMEM)
anywhere = pl.BlockSpec(memory_space=pl.ANY)


def call_mask(where, mask_level, table, edge, pieces):
    rows_here, width = mask_level.shape
    band = table.shape[1]
    chunk = min(1024, width)
    steps = width // chunk
    return pl.pallas_call(
        mask_kernel,
        out_shape=jax.ShapeDtypeStruct(pieces, f32),
        in_specs=[smem, anywhere, anywhere, vmem, vmem],
        out_specs=vmem,
        scratch_shapes=[
            pltpu.VMEM((steps, rows_here, chunk), f32),
            pltpu.VMEM(table.shape, f32),
            pltpu.VMEM((rows_here, band), f32),
            pltpu.SemaphoreType.DMA((steps + 1,)),
        ],
        compiler_params=params(60),
        name="mask_rows",
    )(where, mask_level, table, edge[None, :], edge[:, None])


def call_prepare(where, band_cutoff, shape_corner, shape_extent, after, socs_kernels, mask_level, table, pencils, conds):
    rows_here, width = mask_level.shape
    _, count, _, band, _ = socs_kernels.shape
    image_rows = IMAGE // pencils
    cols_here = width // conds
    y_big = np.stack(wave(image_rows * np.arange(pencils), band, IMAGE)).astype(np.float32)
    y_fine = np.stack(wave(np.arange(image_rows), band, IMAGE)).astype(np.float32)
    shapes = [
        ((image_rows, IMAGE), f32),
        ((count, 2, band, band), f32),
        ((4 * image_rows, 2 * band), bf16),
        ((2 * band, 6 * image_rows), bf16),
        ((rows_here, band), bf16),
        ((rows_here, band), bf16),
        ((cols_here, band), bf16),
        ((cols_here, band), bf16),
        ((rows_here, cols_here), f32),
    ]
    return pl.pallas_call(
        prepare_kernel,
        out_shape=[jax.ShapeDtypeStruct(*shape) for shape in shapes],
        in_specs=[smem] * 2 + [vmem] * 6 + [anywhere] * 4,
        out_specs=[vmem] * len(shapes),
        scratch_shapes=[pltpu.VMEM(table.shape, f32), pltpu.SemaphoreType.DMA((count + 2,))],
        compiler_params=params(24),
        cost_estimate=pl.CostEstimate(flops=10**9, bytes_accessed=2 * 10**7, transcendentals=10**6),
        name="prepare",
    )(
        where,
        band_cutoff,
        shape_corner,
        shape_extent,
        shape_corner.T,
        shape_extent.T,
        y_big,
        y_fine,
        after,
        socs_kernels,
        mask_level,
        table,
    )


def call_field(kernel_weight, dose_scale, packed, kern, target, y_rows, y_cols, width):
    count, _, band, _ = kern.shape
    image_rows = target.shape[0]
    both = fold_table(band)
    x_cos, x_sin = wave(2 * np.arange(band) + 1, band, 4 * band)
    x_hi, x_lo = halves(np.concatenate([x_cos.T, x_sin.T], axis=1))
    up_hi, up_lo = halves(resample_table(band, IMAGE))
    deep = 2 * count * image_rows
    return pl.pallas_call(
        functools.partial(field_kernel, width=width),
        out_shape=jax.ShapeDtypeStruct(packed.shape, f32),
        in_specs=[smem] * 2 + [vmem] * 11,
        out_specs=vmem,
        scratch_shapes=[
            pltpu.VMEM((2, band, band), f32),
            pltpu.VMEM((SLOTS, 2 * band, band), bf16),
            pltpu.VMEM((SLOTS, 2 * band, band), bf16),
            pltpu.VMEM((deep, band), bf16),
            pltpu.VMEM((deep, band), bf16),
            pltpu.VMEM((deep, 2 * band), bf16),
            pltpu.VMEM((deep, 2 * band), bf16),
            pltpu.VMEM((deep, 2 * band), f32),
            pltpu.VMEM((2 * image_rows, IMAGE), bf16),
            pltpu.VMEM((deep, band), f32),
            pltpu.VMEM((2, band, band), f32),
        ],
        compiler_params=params(28),
        name="image_rows",
    )(
        kernel_weight,
        dose_scale,
        packed,
        kern,
        both.astype(bf16),
        both.T.astype(bf16),
        x_hi,
        x_lo,
        up_hi,
        up_lo,
        target,
        y_rows,
        y_cols,
    )


def call_spread(folded, slope, rows_hi, rows_lo, cols_hi, cols_lo, edge, width):
    return pl.pallas_call(
        functools.partial(spread_kernel, width=width),
        out_shape=jax.ShapeDtypeStruct(slope.shape, f32),
        in_specs=[vmem] * 8,
        out_specs=vmem,
        compiler_params=params(24),
        name="mask_gradient",
    )(folded, slope, rows_hi, rows_lo, cols_hi, cols_lo, edge[None, :], edge[:, None])


def local(
    mask_level, socs_kernels, band_cutoff, kernel_weight, dose_scale, shape_corner, shape_extent
):
    width = mask_level.shape[1]
    band = socs_kernels.shape[3]
    pencils = lax.axis_size("px")
    conds = lax.axis_size("cond")
    where = jnp.stack([lax.axis_index("cond"), lax.axis_index("px")]).astype(jnp.int32)
    pieces = (pencils, band * band // LANES // pencils, LANES)
    table, edge = basis_tables(band, width)

    packed = call_mask(where, mask_level, table, edge, pieces)
    piece = collect(packed)
    prepared = call_prepare(
        where, band_cutoff, shape_corner, shape_extent, piece, socs_kernels, mask_level, table, pencils, conds
    )
    target, kern, y_rows, y_cols, rows_hi, rows_lo, cols_hi, cols_lo, slope = prepared
    packed = hand_out(piece, pieces)
    folded = call_field(kernel_weight, dose_scale, packed, kern, target, y_rows, y_cols, width)
    piece = collect(folded)
    others = [
        lax.ppermute(piece, "cond", [(i, (i + d) % conds) for i in range(conds)])
        for d in range(1, conds)
    ]
    piece = functools.reduce(jnp.add, others, piece)
    folded = hand_out(piece, pieces)
    return call_spread(folded, slope, rows_hi, rows_lo, cols_hi, cols_lo, edge, width)


def collect(packed):
    arrived = lax.all_to_all(packed, "px", split_axis=0, concat_axis=0, tiled=True)
    return jnp.sum(arrived, axis=0)


def hand_out(piece, pieces):
    outgoing = jnp.broadcast_to(piece[None], pieces)
    return lax.all_to_all(outgoing, "px", split_axis=0, concat_axis=0, tiled=True)


def solution(mesh):
    in_specs = (
        P("px", None),
        P("cond", None, None, None, None),
        P("cond", None),
        P("cond", None),
        P("cond"),
        P(),
        P(),
    )
    out_specs = P("px", "cond")
    return jax.shard_map(local, mesh=mesh, in_specs=in_specs, out_specs=out_specs, check_vma=False)
```

```python
import functools
import math

import jax
import jax.numpy as jnp
import numpy as np
from jax import lax
from jax.experimental import pallas as pl
from jax.experimental.pallas import tpu as pltpu
from jax.sharding import PartitionSpec as P

IMAGE = 2048
LANES = 128
SLOTS = 2
ROOM = 60
AHEAD = 4
steepness = 6.0
threshold = 0.3
f32 = jnp.float32
bf16 = jnp.bfloat16


def basis_slots(band):
    half = band // 2
    even = np.arange(0, half, 2)
    odd = np.arange(1, half, 2)
    freq = np.concatenate([even, even[1:], [half], odd, odd])
    is_sin = np.concatenate([0 * even, 1 + 0 * even[1:], [0], 0 * odd, 1 + 0 * odd]) > 0
    return freq, is_sin


def basis_tables(band, width):
    freq, is_sin = basis_slots(band)
    fine = 2.0 * np.pi * ((np.arange(LANES)[:, None] * freq[None]) % width) / width
    big = 2.0 * np.pi * ((LANES * np.arange(width // LANES)[:, None] * freq[None]) % width) / width
    first = np.where(is_sin, np.sin(big), np.cos(big))
    second = np.where(is_sin, np.cos(big), -np.sin(big))
    edge = np.sin(2.0 * np.pi * ((np.arange(LANES) * (band // 2)) % width) / width)
    edge = np.tile(edge, (8, band // LANES))
    table = np.concatenate([np.cos(fine), np.sin(fine), first, second, edge], axis=0)
    return table.astype(np.float32)


def fold_table(band):
    half = band // 2
    freq, is_sin = basis_slots(band)
    both = np.zeros((2 * band, band), np.float32)
    for slot in range(band):
        places = [half - freq[slot]] if freq[slot] == half else [half - freq[slot], half + freq[slot]]
        for place in places:
            if is_sin[slot]:
                both[band + place, slot] = -1.0 if place > half else 1.0
            else:
                both[place, slot] = 1.0
    return both


def wave(places, band, period):
    offsets = np.arange(band) - band // 2
    angle = 2.0 * np.pi * ((places[:, None] * offsets[None, :]) % period) / period
    return np.cos(angle), np.sin(angle)


def resample_table(band, image):
    assert image == 8 * band
    base = np.arange(image)
    row = np.ones(image)
    for freq in range(1, band):
        row += 2.0 * np.cos(2.0 * np.pi * ((base * freq) % image) / image)
    row /= 2 * band
    place = 4 * np.arange(band)[:, None] + 2
    odd = 2 * np.arange(2 * band)[None, :] + 1
    near, far = row[(odd - place) % image], row[(odd + place) % image]
    fourth = 4 * np.arange(2 * band)[None, :]
    direct = [row[(fourth - place) % image], row[(fourth + place) % image]]
    return np.concatenate([(near + far) / 2, (near - far) / 2, *direct], axis=0)


def column_runs(band, image):
    return (
        (0, band, 2, 4),
        (band, band, image - 2, -4),
        (2 * band, 2 * band, 1, 2),
        (4 * band, 2 * band, image - 1, -2),
        (6 * band, 2 * band, 0, 4),
    )


def halves(table):
    table = np.asarray(table, np.float32)
    top = table.astype(bf16)
    rest = (table - top.astype(np.float32)).astype(bf16)
    return top, rest


def split(value):
    top = value.astype(bf16)
    return top, (value - top.astype(f32)).astype(bf16)


def dot(left, right, left_dim=1, right_dim=0):
    return lax.dot_general(
        left, right, (((left_dim,), (right_dim,)), ((), ())), preferred_element_type=f32
    )


def dot_split(left, right, left_dim=1, right_dim=0):
    go = functools.partial(dot, left_dim=left_dim, right_dim=right_dim)
    return go(left[0], right[0]) + (go(left[1], right[0]) + go(left[0], right[1]))


def basis_rows(table, start, blocks):
    places = (table.shape[0] - 2 * LANES - 8) // 2
    parts = []
    for block in range(blocks):
        a = table[pl.ds(2 * LANES + start + block, 1), :]
        b = table[pl.ds(2 * LANES + places + start + block, 1), :]
        parts.append(a * table[:LANES, :] + b * table[LANES : 2 * LANES, :])
    return parts[0] if blocks == 1 else jnp.concatenate(parts, axis=0)


def edges(table):
    last = table.shape[0] - 8
    half = table.shape[1] // 2
    return table[last : last + 1, :LANES], table[LANES : 2 * LANES, half - 1 : half]


def put(array, row, column, value):
    rows = lax.broadcasted_iota(jnp.int32, array.shape, 0)
    columns = lax.broadcasted_iota(jnp.int32, array.shape, 1)
    return jnp.where((rows == row) & (columns == column), value, array)


def store_pieces(out, array):
    band = array.shape[1]
    pieces = [array[:, place : place + LANES] for place in range(0, band, LANES)]
    flat = pieces[0] if len(pieces) == 1 else jnp.concatenate(pieces, axis=0)
    out[...] = flat.reshape(out.shape)


def load_pieces(ref, band):
    flat = ref[...].reshape(band * band // LANES, LANES)
    pieces = [flat[place : place + band] for place in range(0, flat.shape[0], band)]
    return pieces[0] if len(pieces) == 1 else jnp.concatenate(pieces, axis=1)


def mask_kernel(mask_hbm, table_hbm, out, mask, table, even, odd, sems):
    count, rows_here, chunk = mask.shape
    band = even.shape[1] // 2 * 2
    half = band // 2
    blocks = chunk // LANES
    pairs = count // 2
    order = [place + side * pairs for place in range(pairs) for side in range(2)]

    def copy(place):
        columns = pl.ds(place * chunk, chunk)
        return pltpu.make_async_copy(mask_hbm.at[:, columns], mask.at[place], sems.at[place])

    copy_table = pltpu.make_async_copy(table_hbm, table, sems.at[count])
    copy(order[0]).start()
    copy(order[1]).start()
    copy_table.start()
    for place in order[2:AHEAD]:
        copy(place).start()
    copy_table.wait()
    line = jnp.zeros((1, LANES), f32)
    for place in range(pairs):
        copy(place).wait()
        copy(place + pairs).wait()
        for ahead in order[2 * place + AHEAD : 2 * place + AHEAD + 2]:
            copy(ahead).start()
        near = jnp.tanh(mask[place])
        far = jnp.tanh(mask[place + pairs])
        hi, lo = split(basis_rows(table, place * blocks, blocks))
        for total, value, columns in (
            (even, near + far, slice(0, half)),
            (odd, near - far, slice(half, band)),
        ):
            weights = jnp.concatenate([hi[:, columns], lo[:, columns]], axis=1)
            product = dot(jnp.concatenate(split(value), axis=0), weights)
            if place == 0:
                total[...] = product
            else:
                total[...] += product
        both_sum = jnp.sum(near + far, axis=0, keepdims=True)
        for start in range(0, chunk, LANES):
            line += both_sum[:, start : start + LANES]
    parts = []
    for total in (even, odd):
        part = total[:rows_here, :] + total[rows_here:, :]
        parts.append(part[:, :half] + part[:, half:])
    row_part = jnp.concatenate(parts, axis=1)
    rows = split(basis_rows(table, lax.axis_index("px"), 1))
    packed = dot_split(rows, split(row_part), 0, 0)
    edge_row, edge_col = edges(table)
    edge_u = jnp.sum(edge_col * row_part[:, 0:1])
    edge_v = jnp.sum(edge_row * line)
    packed = put(put(packed, half - 1, 1, edge_u), 1, half - 1, edge_v)
    store_pieces(out, packed)


def prepare_kernel(
    corner,
    extent,
    y_big,
    y_fine,
    table,
    after,
    mask_hbm,
    target,
    y_rows,
    y_cols,
    rows,
    cols,
    slope,
    sem,
):
    band = table.shape[1]
    rows_here, image = target.shape
    cols_here = slope.shape[1]
    blocks = cols_here // LANES
    place_px = lax.axis_index("px")
    place_cond = lax.axis_index("cond")
    mine = pl.ds(pl.multiple_of(place_cond * cols_here, cols_here), cols_here)
    copy_mask = pltpu.make_async_copy(mask_hbm.at[:, mine], slope, sem)
    copy_mask.start()

    rects = corner.shape[1]
    top = corner[0:1, :]
    bottom = top + extent[0:1, :]
    left = corner[1:2, :]
    right = left + extent[1:2, :]
    places = place_px * rows_here + lax.broadcasted_iota(jnp.int32, (rows_here, rects), 0)
    rows_in = jnp.where((places >= top) & (places < bottom), 1.0, 0.0).astype(bf16)
    for start, count, first, stride in column_runs(band, image):
        places = first + stride * lax.broadcasted_iota(jnp.int32, (count, rects), 0)
        cols_in = jnp.where((places >= left) & (places < right), 1.0, 0.0).astype(bf16)
        target[:, start : start + count] = jnp.minimum(dot(rows_in, cols_in, 1, 1), 1.0)

    big_cos = y_big[0, pl.ds(place_px, 1), :]
    big_sin = y_big[1, pl.ds(place_px, 1), :]
    cos_y = (big_cos * y_fine[0] - big_sin * y_fine[1]) * (1.0 / band)
    sin_y = (big_sin * y_fine[0] + big_cos * y_fine[1]) * (1.0 / band)
    waves = jnp.concatenate(
        [
            jnp.concatenate([cos_y, 0.0 - sin_y], axis=1),
            jnp.concatenate([sin_y, cos_y], axis=1),
        ],
        axis=0,
    )
    waves_hi, waves_lo = split(waves)
    y_rows[...] = jnp.concatenate([waves_hi, waves_lo], axis=0)
    waves_hi, waves_lo = waves_hi.astype(f32), waves_lo.astype(f32)
    stacked = jnp.concatenate([waves_hi, waves_hi, waves_lo], axis=0)
    y_cols[...] = jnp.transpose(stacked).astype(bf16)

    hi, lo = split(basis_rows(table, place_px, 1))
    rows[0] = hi
    rows[1] = lo
    for block in range(blocks):
        here = pl.ds(block * LANES, LANES)
        hi, lo = split(basis_rows(table, place_cond * blocks + block, 1))
        cols[0, here, :] = hi
        cols[1, here, :] = lo
    copy_mask.wait()
    for start in range(0, cols_here, LANES):
        here = pl.ds(start, LANES)
        transmit = jnp.tanh(slope[:, here])
        slope[:, here] = 1.0 - transmit * transmit


def field_kernel(
    cutoff_hbm,
    weight_hbm,
    dose_hbm,
    packed_hbm,
    both_hbm,
    y_rows_hbm,
    kernels,
    x_hbm,
    up_hbm,
    target_hbm,
    y_cols_hbm,
    both_t_hbm,
    out,
    cutoff,
    weight,
    dose,
    packed,
    both,
    y_rows,
    kern,
    x_wave,
    up,
    target,
    y_cols,
    both_t,
    spec,
    radius,
    prod_hi,
    prod_lo,
    wide_hi,
    wide_lo,
    deep_hi,
    deep_lo,
    cs,
    back,
    gs,
    sems,
    kern_sems,
    *,
    width,
):
    count, _, band, _ = kern.shape
    rows_here, image = target.shape
    half = band // 2
    total_rows = count * rows_here
    part = 64
    pairs = (
        (packed_hbm, packed),
        (cutoff_hbm, cutoff),
        (weight_hbm, weight),
        (dose_hbm, dose),
        (both_hbm, both),
        (y_rows_hbm, y_rows),
        (x_hbm, x_wave),
        (up_hbm, up),
        (target_hbm, target),
        (y_cols_hbm, y_cols),
        (both_t_hbm, both_t),
    )
    copies = [pltpu.make_async_copy(*pair, sems.at[place]) for place, pair in enumerate(pairs)]
    copy_x, copy_up, copy_target, copy_y_cols, copy_both_t = copies[6:]

    def copy(place):
        return pltpu.make_async_copy(kernels.at[0, place], kern.at[place], kern_sems.at[place])

    for early in copies[:6]:
        early.start()
    later = [copy(place) for place in range(count)] + copies[6:]
    for item in later[:AHEAD]:
        item.start()
    fu = lax.broadcasted_iota(jnp.int32, (band, band), 0) - half
    fv = lax.broadcasted_iota(jnp.int32, (band, band), 1) - half
    radius[...] = fu * fu + fv * fv
    for early in copies[:6]:
        early.wait()

    box = load_pieces(packed, band)
    edge_u = box[half - 1 : half, 1:2] * (1.0 / width)
    edge_v = box[1:2, half - 1 : half] * (1.0 / width)
    box_hi, box_lo = split(box * (1.0 / width))
    opened = dot(both[...], box_hi) + dot(both[...], box_lo)
    box_hi, box_lo = split(opened)
    opened = dot(box_hi, both[...], 1, 1) + dot(box_lo, both[...], 1, 1)
    spec_im = opened[band:, :band] + opened[:band, band:]
    spec[0] = opened[:band, :band] - opened[band:, band:]
    at_u = (fu == -half) & (fv == 0)
    at_v = (fu == 0) & (fv == -half)
    spec[1] = spec_im + jnp.where(at_u, edge_u, 0.0) + jnp.where(at_v, edge_v, 0.0)

    for place in range(count):
        copy(place).wait()
        if place + AHEAD < len(later):
            later[place + AHEAD].start()
        limit = cutoff[0, place] * cutoff[0, place]
        slot = place % prod_hi.shape[0]
        for start in range(0, band, part):
            here = pl.ds(start, part)
            there = pl.ds(band + start, part)
            inside = radius[here, :] <= limit
            k_re = jnp.where(inside, kern[place, 0, here, :], 0.0)
            k_im = jnp.where(inside, kern[place, 1, here, :], 0.0)
            kern[place, 0, here, :] = k_re
            kern[place, 1, here, :] = k_im
            s_re = spec[0, here, :]
            s_im = spec[1, here, :]
            re_hi, re_lo = split(k_re * s_re - k_im * s_im)
            im_hi, im_lo = split(k_re * s_im + k_im * s_re)
            prod_hi[slot, here, :] = re_hi
            prod_lo[slot, here, :] = re_lo
            prod_hi[slot, there, :] = im_hi
            prod_lo[slot, there, :] = im_lo
        main = dot(y_rows[...], prod_hi[slot])
        rest = dot(y_rows[: 2 * rows_here, :], prod_lo[slot])
        hi, lo = split(main[: 2 * rows_here] + (main[2 * rows_here :] + rest))
        here = pl.ds(place * rows_here, rows_here)
        there = pl.ds(total_rows + place * rows_here, rows_here)
        wide_hi[here, :] = hi[:rows_here]
        wide_lo[here, :] = lo[:rows_here]
        wide_hi[there, :] = hi[rows_here:]
        wide_lo[there, :] = lo[rows_here:]

    for item in later[count + AHEAD :]:
        item.start()
    copy_x.wait()
    cs[...] = dot_split((wide_hi[...], wide_lo[...]), (x_wave[0], x_wave[1]))

    def fields(place):
        here = pl.ds(place * rows_here, rows_here)
        there = pl.ds(total_rows + place * rows_here, rows_here)
        c_re = cs[here, :band]
        s_re = cs[here, band:]
        c_im = cs[there, :band]
        s_im = cs[there, band:]
        return (c_re - s_im, c_im + s_re, c_re + s_im, c_im - s_re), here, there

    plus = jnp.zeros((rows_here, band), f32)
    minus = jnp.zeros((rows_here, band), f32)
    for place in range(count):
        (p_re, p_im, m_re, m_im), _, _ = fields(place)
        scale = weight[0, place]
        plus += scale * (p_re * p_re + p_im * p_im)
        minus += scale * (m_re * m_re + m_im * m_im)
    dose_here = dose[0]
    scale = 2.0 * (width / band) * steepness * dose_here

    def slope_of(intensity, start):
        level = steepness * (dose_here * intensity - threshold)
        resist = 1.0 / (1.0 + jnp.exp(0.0 - level))
        aim = target[:, start : start + intensity.shape[1]]
        return scale * (resist - aim) * resist * (1.0 - resist)

    def resample(value, rows, transposed):
        hi, lo = split(value)
        dim = 1 if transposed else 0
        main = dot(jnp.concatenate([hi, lo], axis=0), up[0, rows, :], 1, dim)
        rest = dot(hi, up[1, rows, :], 1, dim)
        return main[:rows_here] + (main[rows_here:] + rest)

    sums, gaps, whole_rows = slice(0, band), slice(band, 2 * band), slice(2 * band, 4 * band)
    copy_up.wait()
    copy_target.wait()
    sum_part = resample(plus + minus, sums, False)
    gap_part = resample(plus - minus, gaps, False)
    fourth = resample(jnp.concatenate([plus, minus], axis=1), whole_rows, False)
    slope_plus = slope_of(plus, 0)
    slope_minus = slope_of(minus, band)
    right = slope_of(sum_part + gap_part, 2 * band)
    left = slope_of(sum_part - gap_part, 4 * band)
    fourth = resample(slope_of(fourth, 6 * band), whole_rows, True)
    sum_part = resample(right + left, sums, True)
    gap_part = resample(right - left, gaps, True)
    slope_plus = 2.0 * (slope_plus + (sum_part + gap_part) + fourth[:, :band])
    slope_minus = 2.0 * (slope_minus + (sum_part - gap_part) + fourth[:, band:])

    for place in range(count):
        (p_re, p_im, m_re, m_im), here, there = fields(place)
        scale = weight[0, place]
        plus = scale * slope_plus
        minus = scale * slope_minus
        p_re, p_im, m_re, m_im = plus * p_re, plus * p_im, minus * m_re, minus * m_im
        for rows, columns, value in (
            (here, slice(0, band), p_re + m_re),
            (here, slice(band, 2 * band), p_im - m_im),
            (there, slice(0, band), p_im + m_im),
            (there, slice(band, 2 * band), m_re - p_re),
        ):
            hi, lo = split(value)
            deep_hi[rows, columns] = hi
            deep_lo[rows, columns] = lo
    back[...] = dot_split((deep_hi[...], deep_lo[...]), (x_wave[0], x_wave[1]), 1, 1)

    copy_y_cols.wait()
    copy_both_t.wait()
    for place in range(count):
        here = pl.ds(place * rows_here, rows_here)
        there = pl.ds(total_rows + place * rows_here, rows_here)
        hi, lo = split(jnp.concatenate([back[here, :], back[there, :]], axis=0))
        grad = dot(y_cols[...], jnp.concatenate([hi, lo, hi], axis=0))
        for start in range(0, band, part):
            here = pl.ds(start, part)
            k_re = kern[place, 0, here, :]
            k_im = kern[place, 1, here, :]
            g_re = grad[start : start + part]
            g_im = grad[band + start : band + start + part]
            if place == 0:
                gs[0, here, :] = k_re * g_re + k_im * g_im
                gs[1, here, :] = k_re * g_im - k_im * g_re
            else:
                gs[0, here, :] += k_re * g_re + k_im * g_im
                gs[1, here, :] += k_re * g_im - k_im * g_re
    g_re = gs[0]
    g_im = gs[1]
    edge_u = g_im[0:1, half : half + 1]
    edge_v = g_im[half : half + 1, 0:1]
    re_hi, re_lo = split(g_re)
    im_hi, im_lo = split(g_im)
    even, odd = both_t[:, :band], both_t[:, band:]
    left = dot(even, re_hi) + dot(even, re_lo) + dot(odd, im_hi) + dot(odd, im_lo)
    right = dot(even, im_hi) + dot(even, im_lo) - dot(odd, re_hi) - dot(odd, re_lo)
    l_hi, l_lo = split(left)
    r_hi, r_lo = split(right)
    even, odd = both[:band, :], both[band:, :]
    folded = dot(l_hi, even) + dot(l_lo, even) + dot(r_hi, odd) + dot(r_lo, odd)
    store_pieces(out, put(put(folded, half - 1, 1, edge_u), 1, half - 1, edge_v))


def spread_kernel(
    packed_hbm,
    rows_hbm,
    table_hbm,
    cols_hbm,
    slope_hbm,
    out_hbm,
    packed,
    rows,
    table,
    cols,
    slope,
    out,
    sems,
    in_sems,
    out_sems,
    *,
    width,
):
    band = rows.shape[2]
    half = band // 2
    steps, count, step = out.shape

    def copy_in(place):
        here = pl.ds(place * step, step)
        return (
            pltpu.make_async_copy(cols_hbm.at[:, here, :], cols.at[place], in_sems.at[2 * place]),
            pltpu.make_async_copy(slope_hbm.at[:, here], slope.at[place], in_sems.at[2 * place + 1]),
        )

    def copy_out(place):
        here = pl.ds(place * step, step)
        return pltpu.make_async_copy(out.at[place], out_hbm.at[:, here], out_sems.at[place])

    pairs = ((packed_hbm, packed), (rows_hbm, rows), (table_hbm, table))
    early = [pltpu.make_async_copy(*pair, sems.at[place]) for place, pair in enumerate(pairs)]
    for copy in early:
        copy.start()
    for copy in copy_in(0):
        copy.start()
    for copy in early:
        copy.wait()
    for place in range(1, steps):
        for copy in copy_in(place):
            copy.start()
    box = load_pieces(packed, band) * (1.0 / width)
    edge_u = box[half - 1 : half, 1:2]
    edge_v = box[1:2, half - 1 : half]
    box = put(put(box, half - 1, 1, 0.0), 1, half - 1, 0.0)
    mixed_hi, mixed_lo = split(dot_split((rows[0], rows[1]), split(box)))
    mixed = jnp.concatenate([mixed_hi, mixed_lo], axis=0)
    edge_row, edge_col = edges(table)
    side = edge_u * edge_col + edge_v * edge_row
    for place in range(steps):
        for copy in copy_in(place):
            copy.wait()
        main = dot(mixed, cols[place, 0], 1, 1)
        rest = dot(mixed_hi, cols[place, 1], 1, 1)
        grad = main[:count] + (main[count:] + rest)
        for inner in range(0, step, LANES):
            there = pl.ds(inner, LANES)
            out[place, :, there] = (grad[:, inner : inner + LANES] + side) * slope[place, :, there]
        copy_out(place).start()
    for place in range(steps):
        copy_out(place).wait()


def params(mebibytes):
    return pltpu.CompilerParams(vmem_limit_bytes=mebibytes * 1024 * 1024)


vmem = pl.BlockSpec(memory_space=pltpu.VMEM)
anywhere = pl.BlockSpec(memory_space=pl.ANY)


def call_mask(mask_level, table, pieces):
    rows_here, width = mask_level.shape
    band = table.shape[1]
    chunk = min(512, width // 4)
    steps = width // chunk
    return pl.pallas_call(
        mask_kernel,
        out_shape=jax.ShapeDtypeStruct(pieces, f32),
        in_specs=[anywhere, anywhere],
        out_specs=vmem,
        scratch_shapes=[
            pltpu.VMEM((steps, rows_here, chunk), f32),
            pltpu.VMEM(table.shape, f32),
            pltpu.VMEM((2 * rows_here, band), f32),
            pltpu.VMEM((2 * rows_here, band), f32),
            pltpu.SemaphoreType.DMA((steps + 1,)),
        ],
        compiler_params=params(ROOM),
        name="mask_rows",
    )(mask_level, table)


def call_prepare(shape_corner, shape_extent, after, mask_level, table, band, pencils, conds):
    rows_here, width = mask_level.shape
    image_rows = IMAGE // pencils
    cols_here = width // conds
    y_big = np.stack(wave(image_rows * np.arange(pencils), band, IMAGE)).astype(np.float32)
    y_fine = np.stack(wave(np.arange(image_rows), band, IMAGE)).astype(np.float32)
    shapes = [
        ((image_rows, IMAGE), f32),
        ((4 * image_rows, 2 * band), bf16),
        ((2 * band, 6 * image_rows), bf16),
        ((2, rows_here, band), bf16),
        ((2, cols_here, band), bf16),
        ((rows_here, cols_here), f32),
    ]
    return pl.pallas_call(
        prepare_kernel,
        out_shape=[jax.ShapeDtypeStruct(*shape) for shape in shapes],
        in_specs=[vmem] * 5 + [anywhere] * 2,
        out_specs=[vmem] * len(shapes),
        scratch_shapes=[pltpu.SemaphoreType.DMA],
        compiler_params=params(ROOM),
        cost_estimate=pl.CostEstimate(flops=10**9, bytes_accessed=2 * 10**7, transcendentals=10**6),
        name="prepare",
    )(shape_corner.T, shape_extent.T, y_big, y_fine, table, after, mask_level)


def call_field(
    band_cutoff, kernel_weight, dose_scale, packed, socs_kernels, target, y_rows, y_cols, width
):
    _, count, _, band, _ = socs_kernels.shape
    image_rows = target.shape[0]
    both = fold_table(band)
    x_cos, x_sin = wave(2 * np.arange(band) + 1, band, 4 * band)
    x_wave = np.stack(halves(np.concatenate([x_cos.T, x_sin.T], axis=1)))
    up = np.stack(halves(resample_table(band, IMAGE)))
    deep = 2 * count * image_rows
    return pl.pallas_call(
        functools.partial(field_kernel, width=width),
        out_shape=jax.ShapeDtypeStruct(packed.shape, f32),
        in_specs=[anywhere] * 12,
        out_specs=vmem,
        scratch_shapes=[
            pltpu.SMEM(band_cutoff.shape, jnp.int32),
            pltpu.SMEM(kernel_weight.shape, f32),
            pltpu.SMEM(dose_scale.shape, f32),
            pltpu.VMEM(packed.shape, f32),
            pltpu.VMEM(both.shape, bf16),
            pltpu.VMEM(y_rows.shape, bf16),
            pltpu.VMEM((count, 2, band, band), f32),
            pltpu.VMEM(x_wave.shape, bf16),
            pltpu.VMEM(up.shape, bf16),
            pltpu.VMEM(target.shape, f32),
            pltpu.VMEM(y_cols.shape, bf16),
            pltpu.VMEM(both.T.shape, bf16),
            pltpu.VMEM((2, band, band), f32),
            pltpu.VMEM((band, band), jnp.int32),
            pltpu.VMEM((SLOTS, 2 * band, band), bf16),
            pltpu.VMEM((SLOTS, 2 * band, band), bf16),
            pltpu.VMEM((deep, band), bf16),
            pltpu.VMEM((deep, band), bf16),
            pltpu.VMEM((deep, 2 * band), bf16),
            pltpu.VMEM((deep, 2 * band), bf16),
            pltpu.VMEM((deep, 2 * band), f32),
            pltpu.VMEM((deep, band), f32),
            pltpu.VMEM((2, band, band), f32),
            pltpu.SemaphoreType.DMA((11,)),
            pltpu.SemaphoreType.DMA((count,)),
        ],
        compiler_params=params(ROOM),
        name="image_rows",
    )(
        band_cutoff,
        kernel_weight,
        dose_scale,
        packed,
        both.astype(bf16),
        y_rows,
        socs_kernels,
        x_wave,
        up,
        target,
        y_cols,
        both.T.astype(bf16),
    )


def call_spread(folded, slope, rows, cols, table, width):
    count, cols_here = slope.shape
    band = rows.shape[2]
    step = min(512, cols_here)
    steps = cols_here // step
    return pl.pallas_call(
        functools.partial(spread_kernel, width=width),
        out_shape=jax.ShapeDtypeStruct(slope.shape, f32),
        in_specs=[anywhere] * 5,
        out_specs=anywhere,
        scratch_shapes=[
            pltpu.VMEM(folded.shape, f32),
            pltpu.VMEM(rows.shape, bf16),
            pltpu.VMEM(table.shape, f32),
            pltpu.VMEM((steps, 2, step, band), bf16),
            pltpu.VMEM((steps, count, step), f32),
            pltpu.VMEM((steps, count, step), f32),
            pltpu.SemaphoreType.DMA((3,)),
            pltpu.SemaphoreType.DMA((2 * steps,)),
            pltpu.SemaphoreType.DMA((steps,)),
        ],
        compiler_params=params(ROOM),
        name="mask_gradient",
    )(folded, rows, table, cols, slope)


def local(
    mask_level, socs_kernels, band_cutoff, kernel_weight, dose_scale, shape_corner, shape_extent
):
    width = mask_level.shape[1]
    band = socs_kernels.shape[3]
    pencils = lax.axis_size("px")
    conds = lax.axis_size("cond")
    pieces = (pencils, band * band // LANES // pencils, LANES)
    table = basis_tables(band, width)

    packed = call_mask(mask_level, table, pieces)
    piece = collect(packed)
    target, y_rows, y_cols, rows, cols, slope = call_prepare(
        shape_corner, shape_extent, piece, mask_level, table, band, pencils, conds
    )
    packed = hand_out(piece, pieces)
    folded = call_field(
        band_cutoff, kernel_weight, dose_scale, packed, socs_kernels, target, y_rows, y_cols, width
    )
    piece = collect(folded)
    others = [
        lax.ppermute(piece, "cond", [(i, (i + d) % conds) for i in range(conds)])
        for d in range(1, conds)
    ]
    piece = functools.reduce(jnp.add, others, piece)
    folded = hand_out(piece, pieces)
    return call_spread(folded, slope, rows, cols, table, width)


def collect(packed):
    arrived = lax.all_to_all(packed, "px", split_axis=0, concat_axis=0, tiled=True)
    return jnp.sum(arrived, axis=0)


def hand_out(piece, pieces):
    outgoing = jnp.broadcast_to(piece[None], pieces)
    return lax.all_to_all(outgoing, "px", split_axis=0, concat_axis=0, tiled=True)


def solution(mesh):
    in_specs = (
        P("px", None),
        P("cond", None, None, None, None),
        P("cond", None),
        P("cond", None),
        P("cond"),
        P(),
        P(),
    )
    out_specs = P("px", "cond")
    return jax.shard_map(local, mesh=mesh, in_specs=in_specs, out_specs=out_specs, check_vma=False)
```

```python
import functools
import math

import jax
import jax.numpy as jnp
import numpy as np
from jax import lax
from jax.experimental import pallas as pl
from jax.experimental.pallas import tpu as pltpu
from jax.sharding import PartitionSpec as P

IMAGE = 2048
LANES = 128
SLOTS = 2
ROOM = 60
AHEAD = 4
steepness = 6.0
threshold = 0.3
f32 = jnp.float32
bf16 = jnp.bfloat16


def basis_slots(band):
    half = band // 2
    even = np.arange(0, half, 2)
    odd = np.arange(1, half, 2)
    freq = np.concatenate([even, even[1:], [half], odd, odd])
    is_sin = np.concatenate([0 * even, 1 + 0 * even[1:], [0], 0 * odd, 1 + 0 * odd]) > 0
    return freq, is_sin


def basis_tables(band, width):
    freq, is_sin = basis_slots(band)
    fine = 2.0 * np.pi * ((np.arange(LANES)[:, None] * freq[None]) % width) / width
    big = 2.0 * np.pi * ((LANES * np.arange(width // LANES)[:, None] * freq[None]) % width) / width
    first = np.where(is_sin, np.sin(big), np.cos(big))
    second = np.where(is_sin, np.cos(big), -np.sin(big))
    edge = np.sin(2.0 * np.pi * ((np.arange(LANES) * (band // 2)) % width) / width)
    edge = np.tile(edge, (8, band // LANES))
    table = np.concatenate([np.cos(fine), np.sin(fine), first, second, edge], axis=0)
    return table.astype(np.float32)


def fold_table(band):
    half = band // 2
    freq, is_sin = basis_slots(band)
    both = np.zeros((2 * band, band), np.float32)
    for slot in range(band):
        places = [half - freq[slot]] if freq[slot] == half else [half - freq[slot], half + freq[slot]]
        for place in places:
            if is_sin[slot]:
                both[band + place, slot] = -1.0 if place > half else 1.0
            else:
                both[place, slot] = 1.0
    return both


def wave(places, band, period):
    offsets = np.arange(band) - band // 2
    angle = 2.0 * np.pi * ((places[:, None] * offsets[None, :]) % period) / period
    return np.cos(angle), np.sin(angle)


def resample_table(band, image):
    assert image == 8 * band
    base = np.arange(image)
    row = np.ones(image)
    for freq in range(1, band):
        row += 2.0 * np.cos(2.0 * np.pi * ((base * freq) % image) / image)
    row /= 2 * band
    place = 4 * np.arange(band)[:, None] + 2
    odd = 2 * np.arange(2 * band)[None, :] + 1
    near, far = row[(odd - place) % image], row[(odd + place) % image]
    fourth = 4 * np.arange(2 * band)[None, :]
    direct = [row[(fourth - place) % image], row[(fourth + place) % image]]
    return np.concatenate([(near + far) / 2, (near - far) / 2, *direct], axis=0)


def column_runs(band, image):
    return (
        (0, band, 2, 4),
        (band, band, image - 2, -4),
        (2 * band, 2 * band, 1, 2),
        (4 * band, 2 * band, image - 1, -2),
        (6 * band, 2 * band, 0, 4),
    )


def halves(table):
    table = np.asarray(table, np.float32)
    top = table.astype(bf16)
    rest = (table - top.astype(np.float32)).astype(bf16)
    return top, rest


def split(value):
    top = value.astype(bf16)
    return top, (value - top.astype(f32)).astype(bf16)


def dot(left, right, left_dim=1, right_dim=0):
    return lax.dot_general(
        left, right, (((left_dim,), (right_dim,)), ((), ())), preferred_element_type=f32
    )


def dot_split(left, right, left_dim=1, right_dim=0):
    go = functools.partial(dot, left_dim=left_dim, right_dim=right_dim)
    return go(left[0], right[0]) + (go(left[1], right[0]) + go(left[0], right[1]))


def basis_rows(table, start, blocks):
    places = (table.shape[0] - 2 * LANES - 8) // 2
    parts = []
    for block in range(blocks):
        a = table[pl.ds(2 * LANES + start + block, 1), :]
        b = table[pl.ds(2 * LANES + places + start + block, 1), :]
        parts.append(a * table[:LANES, :] + b * table[LANES : 2 * LANES, :])
    return parts[0] if blocks == 1 else jnp.concatenate(parts, axis=0)


def edges(table):
    last = table.shape[0] - 8
    half = table.shape[1] // 2
    return table[last : last + 1, :LANES], table[LANES : 2 * LANES, half - 1 : half]


def put(array, row, column, value):
    rows = lax.broadcasted_iota(jnp.int32, array.shape, 0)
    columns = lax.broadcasted_iota(jnp.int32, array.shape, 1)
    return jnp.where((rows == row) & (columns == column), value, array)


def store_pieces(out, array):
    band = array.shape[1]
    pieces = [array[:, place : place + LANES] for place in range(0, band, LANES)]
    flat = pieces[0] if len(pieces) == 1 else jnp.concatenate(pieces, axis=0)
    out[...] = flat.reshape(out.shape)


def load_pieces(ref, band):
    flat = ref[...].reshape(band * band // LANES, LANES)
    pieces = [flat[place : place + band] for place in range(0, flat.shape[0], band)]
    return pieces[0] if len(pieces) == 1 else jnp.concatenate(pieces, axis=1)


def mask_kernel(mask_hbm, table_hbm, out, mask, table, even, odd, sems):
    count, rows_here, chunk = mask.shape
    band = even.shape[1] // 2 * 2
    half = band // 2
    blocks = chunk // LANES
    pairs = count // 2
    order = [place + side * pairs for place in range(pairs) for side in range(2)]

    def copy(place):
        columns = pl.ds(place * chunk, chunk)
        return pltpu.make_async_copy(mask_hbm.at[:, columns], mask.at[place], sems.at[place])

    copy_table = pltpu.make_async_copy(table_hbm, table, sems.at[count])
    copy(order[0]).start()
    copy(order[1]).start()
    copy_table.start()
    for place in order[2:]:
        copy(place).start()
    copy_table.wait()
    line = jnp.zeros((1, LANES), f32)
    for place in range(pairs):
        copy(place).wait()
        copy(place + pairs).wait()
        near = jnp.tanh(mask[place])
        far = jnp.tanh(mask[place + pairs])
        hi, lo = split(basis_rows(table, place * blocks, blocks))
        for total, value, columns in (
            (even, near + far, slice(0, half)),
            (odd, near - far, slice(half, band)),
        ):
            weights = jnp.concatenate([hi[:, columns], lo[:, columns]], axis=1)
            product = dot(jnp.concatenate(split(value), axis=0), weights)
            if place == 0:
                total[...] = product
            else:
                total[...] += product
        both_sum = jnp.sum(near + far, axis=0, keepdims=True)
        for start in range(0, chunk, LANES):
            line += both_sum[:, start : start + LANES]
    parts = []
    for total in (even, odd):
        part = total[:rows_here, :] + total[rows_here:, :]
        parts.append(part[:, :half] + part[:, half:])
    row_part = jnp.concatenate(parts, axis=1)
    rows = split(basis_rows(table, lax.axis_index("px"), 1))
    packed = dot_split(rows, split(row_part), 0, 0)
    edge_row, edge_col = edges(table)
    edge_u = jnp.sum(edge_col * row_part[:, 0:1])
    edge_v = jnp.sum(edge_row * line)
    packed = put(put(packed, half - 1, 1, edge_u), 1, half - 1, edge_v)
    store_pieces(out, packed)


def prepare_kernel(
    corner,
    extent,
    y_big,
    y_fine,
    after,
    mask_hbm,
    target,
    y_rows,
    y_cols,
    slope,
    sem,
):
    band = y_fine.shape[2]
    rows_here, image = target.shape
    cols_here = slope.shape[1]
    place_px = lax.axis_index("px")
    place_cond = lax.axis_index("cond")
    mine = pl.ds(pl.multiple_of(place_cond * cols_here, cols_here), cols_here)
    copy_mask = pltpu.make_async_copy(mask_hbm.at[:, mine], slope, sem)
    copy_mask.start()

    rects = corner.shape[1]
    top = corner[0:1, :]
    bottom = top + extent[0:1, :]
    left = corner[1:2, :]
    right = left + extent[1:2, :]
    places = place_px * rows_here + lax.broadcasted_iota(jnp.int32, (rows_here, rects), 0)
    rows_in = jnp.where((places >= top) & (places < bottom), 1.0, 0.0).astype(bf16)
    for start, count, first, stride in column_runs(band, image):
        places = first + stride * lax.broadcasted_iota(jnp.int32, (count, rects), 0)
        cols_in = jnp.where((places >= left) & (places < right), 1.0, 0.0).astype(bf16)
        target[:, start : start + count] = jnp.minimum(dot(rows_in, cols_in, 1, 1), 1.0)

    big_cos = y_big[0, pl.ds(place_px, 1), :]
    big_sin = y_big[1, pl.ds(place_px, 1), :]
    cos_y = (big_cos * y_fine[0] - big_sin * y_fine[1]) * (1.0 / band)
    sin_y = (big_sin * y_fine[0] + big_cos * y_fine[1]) * (1.0 / band)
    waves = jnp.concatenate(
        [
            jnp.concatenate([cos_y, 0.0 - sin_y], axis=1),
            jnp.concatenate([sin_y, cos_y], axis=1),
        ],
        axis=0,
    )
    waves_hi, waves_lo = split(waves)
    y_rows[...] = jnp.concatenate([waves_hi, waves_lo], axis=0)
    waves_hi, waves_lo = waves_hi.astype(f32), waves_lo.astype(f32)
    stacked = jnp.concatenate([waves_hi, waves_hi, waves_lo], axis=0)
    y_cols[...] = jnp.transpose(stacked).astype(bf16)

    copy_mask.wait()
    for start in range(0, cols_here, LANES):
        here = pl.ds(start, LANES)
        transmit = jnp.tanh(slope[:, here])
        slope[:, here] = 1.0 - transmit * transmit


def field_kernel(
    cutoff_hbm,
    weight_hbm,
    dose_hbm,
    packed_hbm,
    both_hbm,
    y_rows_hbm,
    kernels,
    x_hbm,
    up_hbm,
    target_hbm,
    y_cols_hbm,
    both_t_hbm,
    out,
    cutoff,
    weight,
    dose,
    packed,
    both,
    y_rows,
    kern,
    x_wave,
    up,
    target,
    y_cols,
    both_t,
    spec,
    radius,
    prod_hi,
    prod_lo,
    wide_hi,
    wide_lo,
    deep_hi,
    deep_lo,
    cs,
    back,
    gs,
    sems,
    kern_sems,
    *,
    width,
):
    count, _, band, _ = kern.shape
    rows_here, image = target.shape
    half = band // 2
    total_rows = count * rows_here
    part = 64
    pairs = (
        (packed_hbm, packed),
        (cutoff_hbm, cutoff),
        (weight_hbm, weight),
        (dose_hbm, dose),
        (both_hbm, both),
        (y_rows_hbm, y_rows),
        (x_hbm, x_wave),
        (up_hbm, up),
        (target_hbm, target),
        (y_cols_hbm, y_cols),
        (both_t_hbm, both_t),
    )
    copies = [pltpu.make_async_copy(*pair, sems.at[place]) for place, pair in enumerate(pairs)]
    copy_x, copy_up, copy_target, copy_y_cols, copy_both_t = copies[6:]

    def copy(place):
        return pltpu.make_async_copy(kernels.at[0, place], kern.at[place], kern_sems.at[place])

    for early in copies[:6]:
        early.start()
    later = [copy(place) for place in range(count)] + copies[6:]
    for item in later[:AHEAD]:
        item.start()
    fu = lax.broadcasted_iota(jnp.int32, (band, band), 0) - half
    fv = lax.broadcasted_iota(jnp.int32, (band, band), 1) - half
    radius[...] = fu * fu + fv * fv
    for early in copies[:6]:
        early.wait()

    box = load_pieces(packed, band)
    edge_u = box[half - 1 : half, 1:2] * (1.0 / width)
    edge_v = box[1:2, half - 1 : half] * (1.0 / width)
    box_hi, box_lo = split(box * (1.0 / width))
    opened = dot(both[...], box_hi) + dot(both[...], box_lo)
    box_hi, box_lo = split(opened)
    opened = dot(box_hi, both[...], 1, 1) + dot(box_lo, both[...], 1, 1)
    spec_im = opened[band:, :band] + opened[:band, band:]
    spec[0] = opened[:band, :band] - opened[band:, band:]
    at_u = (fu == -half) & (fv == 0)
    at_v = (fu == 0) & (fv == -half)
    spec[1] = spec_im + jnp.where(at_u, edge_u, 0.0) + jnp.where(at_v, edge_v, 0.0)

    for place in range(count):
        copy(place).wait()
        if place + AHEAD < len(later):
            later[place + AHEAD].start()
        limit = cutoff[0, place] * cutoff[0, place]
        slot = place % prod_hi.shape[0]
        for start in range(0, band, part):
            here = pl.ds(start, part)
            there = pl.ds(band + start, part)
            inside = radius[here, :] <= limit
            k_re = jnp.where(inside, kern[place, 0, here, :], 0.0)
            k_im = jnp.where(inside, kern[place, 1, here, :], 0.0)
            kern[place, 0, here, :] = k_re
            kern[place, 1, here, :] = k_im
            s_re = spec[0, here, :]
            s_im = spec[1, here, :]
            re_hi, re_lo = split(k_re * s_re - k_im * s_im)
            im_hi, im_lo = split(k_re * s_im + k_im * s_re)
            prod_hi[slot, here, :] = re_hi
            prod_lo[slot, here, :] = re_lo
            prod_hi[slot, there, :] = im_hi
            prod_lo[slot, there, :] = im_lo
        main = dot(y_rows[...], prod_hi[slot])
        rest = dot(y_rows[: 2 * rows_here, :], prod_lo[slot])
        hi, lo = split(main[: 2 * rows_here] + (main[2 * rows_here :] + rest))
        here = pl.ds(place * rows_here, rows_here)
        there = pl.ds(total_rows + place * rows_here, rows_here)
        wide_hi[here, :] = hi[:rows_here]
        wide_lo[here, :] = lo[:rows_here]
        wide_hi[there, :] = hi[rows_here:]
        wide_lo[there, :] = lo[rows_here:]

    for item in later[count + AHEAD :]:
        item.start()
    copy_x.wait()
    cs[...] = dot_split((wide_hi[...], wide_lo[...]), (x_wave[0], x_wave[1]))

    def fields(place):
        here = pl.ds(place * rows_here, rows_here)
        there = pl.ds(total_rows + place * rows_here, rows_here)
        c_re = cs[here, :band]
        s_re = cs[here, band:]
        c_im = cs[there, :band]
        s_im = cs[there, band:]
        return (c_re - s_im, c_im + s_re, c_re + s_im, c_im - s_re), here, there

    plus = jnp.zeros((rows_here, band), f32)
    minus = jnp.zeros((rows_here, band), f32)
    for place in range(count):
        (p_re, p_im, m_re, m_im), _, _ = fields(place)
        scale = weight[0, place]
        plus += scale * (p_re * p_re + p_im * p_im)
        minus += scale * (m_re * m_re + m_im * m_im)
    dose_here = dose[0]
    scale = 2.0 * (width / band) * steepness * dose_here

    def slope_of(intensity, start):
        level = steepness * (dose_here * intensity - threshold)
        resist = 1.0 / (1.0 + jnp.exp(0.0 - level))
        aim = target[:, start : start + intensity.shape[1]]
        return scale * (resist - aim) * resist * (1.0 - resist)

    def resample(value, rows, transposed):
        hi, lo = split(value)
        dim = 1 if transposed else 0
        main = dot(jnp.concatenate([hi, lo], axis=0), up[0, rows, :], 1, dim)
        rest = dot(hi, up[1, rows, :], 1, dim)
        return main[:rows_here] + (main[rows_here:] + rest)

    sums, gaps, whole_rows = slice(0, band), slice(band, 2 * band), slice(2 * band, 4 * band)
    copy_up.wait()
    copy_target.wait()
    sum_part = resample(plus + minus, sums, False)
    gap_part = resample(plus - minus, gaps, False)
    fourth = resample(jnp.concatenate([plus, minus], axis=1), whole_rows, False)
    slope_plus = slope_of(plus, 0)
    slope_minus = slope_of(minus, band)
    right = slope_of(sum_part + gap_part, 2 * band)
    left = slope_of(sum_part - gap_part, 4 * band)
    fourth = resample(slope_of(fourth, 6 * band), whole_rows, True)
    sum_part = resample(right + left, sums, True)
    gap_part = resample(right - left, gaps, True)
    slope_plus = 2.0 * (slope_plus + (sum_part + gap_part) + fourth[:, :band])
    slope_minus = 2.0 * (slope_minus + (sum_part - gap_part) + fourth[:, band:])

    for place in range(count):
        (p_re, p_im, m_re, m_im), here, there = fields(place)
        scale = weight[0, place]
        plus = scale * slope_plus
        minus = scale * slope_minus
        p_re, p_im, m_re, m_im = plus * p_re, plus * p_im, minus * m_re, minus * m_im
        for rows, columns, value in (
            (here, slice(0, band), p_re + m_re),
            (here, slice(band, 2 * band), p_im - m_im),
            (there, slice(0, band), p_im + m_im),
            (there, slice(band, 2 * band), m_re - p_re),
        ):
            hi, lo = split(value)
            deep_hi[rows, columns] = hi
            deep_lo[rows, columns] = lo
    back[...] = dot_split((deep_hi[...], deep_lo[...]), (x_wave[0], x_wave[1]), 1, 1)

    copy_y_cols.wait()
    copy_both_t.wait()
    for place in range(count):
        here = pl.ds(place * rows_here, rows_here)
        there = pl.ds(total_rows + place * rows_here, rows_here)
        hi, lo = split(jnp.concatenate([back[here, :], back[there, :]], axis=0))
        grad = dot(y_cols[...], jnp.concatenate([hi, lo, hi], axis=0))
        for start in range(0, band, part):
            here = pl.ds(start, part)
            k_re = kern[place, 0, here, :]
            k_im = kern[place, 1, here, :]
            g_re = grad[start : start + part]
            g_im = grad[band + start : band + start + part]
            if place == 0:
                gs[0, here, :] = k_re * g_re + k_im * g_im
                gs[1, here, :] = k_re * g_im - k_im * g_re
            else:
                gs[0, here, :] += k_re * g_re + k_im * g_im
                gs[1, here, :] += k_re * g_im - k_im * g_re
    g_re = gs[0]
    g_im = gs[1]
    edge_u = g_im[0:1, half : half + 1]
    edge_v = g_im[half : half + 1, 0:1]
    re_hi, re_lo = split(g_re)
    im_hi, im_lo = split(g_im)
    even, odd = both_t[:, :band], both_t[:, band:]
    left = dot(even, re_hi) + dot(even, re_lo) + dot(odd, im_hi) + dot(odd, im_lo)
    right = dot(even, im_hi) + dot(even, im_lo) - dot(odd, re_hi) - dot(odd, re_lo)
    l_hi, l_lo = split(left)
    r_hi, r_lo = split(right)
    even, odd = both[:band, :], both[band:, :]
    folded = dot(l_hi, even) + dot(l_lo, even) + dot(r_hi, odd) + dot(r_lo, odd)
    store_pieces(out, put(put(folded, half - 1, 1, edge_u), 1, half - 1, edge_v))


def spread_kernel(packed, table, slope_hbm, out_hbm, slope, out, cols, in_sems, out_sems):
    steps, count, step = out.shape
    band = table.shape[1]
    half = band // 2
    blocks = step // LANES
    width = (table.shape[0] - 2 * LANES - 8) // 2 * LANES
    first_block = lax.axis_index("cond") * (steps * blocks)

    def copy_in(place):
        here = pl.ds(place * step, step)
        return pltpu.make_async_copy(slope_hbm.at[:, here], slope.at[place], in_sems.at[place])

    def copy_out(place):
        here = pl.ds(place * step, step)
        return pltpu.make_async_copy(out.at[place], out_hbm.at[:, here], out_sems.at[place])

    for place in range(steps):
        copy_in(place).start()
    row_hi, row_lo = split(basis_rows(table, lax.axis_index("px"), 1))
    for place in range(steps):
        hi, lo = split(basis_rows(table, first_block + place * blocks, blocks))
        cols[place, 0] = hi
        cols[place, 1] = lo
    box = load_pieces(packed, band) * (1.0 / width)
    edge_u = box[half - 1 : half, 1:2]
    edge_v = box[1:2, half - 1 : half]
    box = put(put(box, half - 1, 1, 0.0), 1, half - 1, 0.0)
    mixed_hi, mixed_lo = split(dot_split((row_hi, row_lo), split(box)))
    mixed = jnp.concatenate([mixed_hi, mixed_lo], axis=0)
    edge_row, edge_col = edges(table)
    side = edge_u * edge_col + edge_v * edge_row
    for place in range(steps):
        copy_in(place).wait()
        main = dot(mixed, cols[place, 0], 1, 1)
        rest = dot(mixed_hi, cols[place, 1], 1, 1)
        grad = main[:count] + (main[count:] + rest)
        for inner in range(0, step, LANES):
            there = pl.ds(inner, LANES)
            out[place, :, there] = (grad[:, inner : inner + LANES] + side) * slope[place, :, there]
        copy_out(place).start()
    for place in range(steps):
        copy_out(place).wait()


def params(mebibytes):
    return pltpu.CompilerParams(vmem_limit_bytes=mebibytes * 1024 * 1024)


vmem = pl.BlockSpec(memory_space=pltpu.VMEM)
anywhere = pl.BlockSpec(memory_space=pl.ANY)


def call_mask(mask_level, table, pieces):
    rows_here, width = mask_level.shape
    band = table.shape[1]
    chunk = min(512, width // 4)
    steps = width // chunk
    return pl.pallas_call(
        mask_kernel,
        out_shape=jax.ShapeDtypeStruct(pieces, f32),
        in_specs=[anywhere, anywhere],
        out_specs=vmem,
        scratch_shapes=[
            pltpu.VMEM((steps, rows_here, chunk), f32),
            pltpu.VMEM(table.shape, f32),
            pltpu.VMEM((2 * rows_here, band), f32),
            pltpu.VMEM((2 * rows_here, band), f32),
            pltpu.SemaphoreType.DMA((steps + 1,)),
        ],
        compiler_params=params(ROOM),
        name="mask_rows",
    )(mask_level, table)


def call_prepare(shape_corner, shape_extent, after, mask_level, band, pencils, conds):
    rows_here, width = mask_level.shape
    image_rows = IMAGE // pencils
    cols_here = width // conds
    y_big = np.stack(wave(image_rows * np.arange(pencils), band, IMAGE)).astype(np.float32)
    y_fine = np.stack(wave(np.arange(image_rows), band, IMAGE)).astype(np.float32)
    shapes = [
        ((image_rows, IMAGE), f32),
        ((4 * image_rows, 2 * band), bf16),
        ((2 * band, 6 * image_rows), bf16),
        ((rows_here, cols_here), f32),
    ]
    return pl.pallas_call(
        prepare_kernel,
        out_shape=[jax.ShapeDtypeStruct(*shape) for shape in shapes],
        in_specs=[vmem] * 4 + [anywhere] * 2,
        out_specs=[vmem] * len(shapes),
        scratch_shapes=[pltpu.SemaphoreType.DMA],
        compiler_params=params(ROOM),
        cost_estimate=pl.CostEstimate(flops=10**9, bytes_accessed=2 * 10**7, transcendentals=10**6),
        name="prepare",
    )(shape_corner.T, shape_extent.T, y_big, y_fine, after, mask_level)


def call_field(
    band_cutoff, kernel_weight, dose_scale, packed, socs_kernels, target, y_rows, y_cols, width
):
    _, count, _, band, _ = socs_kernels.shape
    image_rows = target.shape[0]
    both = fold_table(band)
    x_cos, x_sin = wave(2 * np.arange(band) + 1, band, 4 * band)
    x_wave = np.stack(halves(np.concatenate([x_cos.T, x_sin.T], axis=1)))
    up = np.stack(halves(resample_table(band, IMAGE)))
    deep = 2 * count * image_rows
    return pl.pallas_call(
        functools.partial(field_kernel, width=width),
        out_shape=jax.ShapeDtypeStruct(packed.shape, f32),
        in_specs=[anywhere] * 12,
        out_specs=vmem,
        scratch_shapes=[
            pltpu.SMEM(band_cutoff.shape, jnp.int32),
            pltpu.SMEM(kernel_weight.shape, f32),
            pltpu.SMEM(dose_scale.shape, f32),
            pltpu.VMEM(packed.shape, f32),
            pltpu.VMEM(both.shape, bf16),
            pltpu.VMEM(y_rows.shape, bf16),
            pltpu.VMEM((count, 2, band, band), f32),
            pltpu.VMEM(x_wave.shape, bf16),
            pltpu.VMEM(up.shape, bf16),
            pltpu.VMEM(target.shape, f32),
            pltpu.VMEM(y_cols.shape, bf16),
            pltpu.VMEM(both.T.shape, bf16),
            pltpu.VMEM((2, band, band), f32),
            pltpu.VMEM((band, band), jnp.int32),
            pltpu.VMEM((SLOTS, 2 * band, band), bf16),
            pltpu.VMEM((SLOTS, 2 * band, band), bf16),
            pltpu.VMEM((deep, band), bf16),
            pltpu.VMEM((deep, band), bf16),
            pltpu.VMEM((deep, 2 * band), bf16),
            pltpu.VMEM((deep, 2 * band), bf16),
            pltpu.VMEM((deep, 2 * band), f32),
            pltpu.VMEM((deep, band), f32),
            pltpu.VMEM((2, band, band), f32),
            pltpu.SemaphoreType.DMA((11,)),
            pltpu.SemaphoreType.DMA((count,)),
        ],
        compiler_params=params(ROOM),
        name="image_rows",
    )(
        band_cutoff,
        kernel_weight,
        dose_scale,
        packed,
        both.astype(bf16),
        y_rows,
        socs_kernels,
        x_wave,
        up,
        target,
        y_cols,
        both.T.astype(bf16),
    )


def call_spread(folded, slope, table):
    count, cols_here = slope.shape
    band = table.shape[1]
    step = min(512, cols_here)
    steps = cols_here // step
    return pl.pallas_call(
        spread_kernel,
        out_shape=jax.ShapeDtypeStruct(slope.shape, f32),
        in_specs=[vmem, vmem, anywhere],
        out_specs=anywhere,
        scratch_shapes=[
            pltpu.VMEM((steps, count, step), f32),
            pltpu.VMEM((steps, count, step), f32),
            pltpu.VMEM((steps, 2, step, band), bf16),
            pltpu.SemaphoreType.DMA((steps,)),
            pltpu.SemaphoreType.DMA((steps,)),
        ],
        compiler_params=params(40),
        name="mask_gradient",
    )(folded, table, slope)


def local(
    mask_level, socs_kernels, band_cutoff, kernel_weight, dose_scale, shape_corner, shape_extent
):
    width = mask_level.shape[1]
    band = socs_kernels.shape[3]
    pencils = lax.axis_size("px")
    conds = lax.axis_size("cond")
    pieces = (pencils, band * band // LANES // pencils, LANES)
    table = basis_tables(band, width)

    packed = call_mask(mask_level, table, pieces)
    piece = collect(packed)
    target, y_rows, y_cols, slope = call_prepare(
        shape_corner, shape_extent, piece, mask_level, band, pencils, conds
    )
    packed = hand_out(piece, pieces)
    folded = call_field(
        band_cutoff, kernel_weight, dose_scale, packed, socs_kernels, target, y_rows, y_cols, width
    )
    piece = collect(folded)
    copies = jnp.broadcast_to(piece[None], (conds, *piece.shape))
    copies = lax.all_to_all(copies, "cond", split_axis=0, concat_axis=0, tiled=True)
    piece = jnp.sum(copies, axis=0)
    folded = hand_out(piece, pieces)
    return call_spread(folded, slope, table)


def collect(packed):
    arrived = lax.all_to_all(packed, "px", split_axis=0, concat_axis=0, tiled=True)
    return jnp.sum(arrived, axis=0)


def hand_out(piece, pieces):
    outgoing = jnp.broadcast_to(piece[None], pieces)
    return lax.all_to_all(outgoing, "px", split_axis=0, concat_axis=0, tiled=True)


def solution(mesh):
    in_specs = (
        P("px", None),
        P("cond", None, None, None, None),
        P("cond", None),
        P("cond", None),
        P("cond"),
        P(),
        P(),
    )
    out_specs = P("px", "cond")
    return jax.shard_map(local, mesh=mesh, in_specs=in_specs, out_specs=out_specs, check_vma=False)
```

```python
import functools
import math

import jax
import jax.numpy as jnp
import numpy as np
from jax import lax
from jax.experimental import pallas as pl
from jax.experimental.pallas import tpu as pltpu
from jax.sharding import PartitionSpec as P

IMAGE = 2048
LANES = 128
SLOTS = 2
ROOM = 60
AHEAD = 4
steepness = 6.0
threshold = 0.3
f32 = jnp.float32
bf16 = jnp.bfloat16


def basis_slots(band):
    half = band // 2
    even = np.arange(0, half, 2)
    odd = np.arange(1, half, 2)
    freq = np.concatenate([even, even[1:], [half], odd, odd])
    is_sin = np.concatenate([0 * even, 1 + 0 * even[1:], [0], 0 * odd, 1 + 0 * odd]) > 0
    return freq, is_sin


def basis_tables(band, width):
    freq, is_sin = basis_slots(band)
    fine = 2.0 * np.pi * ((np.arange(LANES)[:, None] * freq[None]) % width) / width
    big = 2.0 * np.pi * ((LANES * np.arange(width // LANES)[:, None] * freq[None]) % width) / width
    first = np.where(is_sin, np.sin(big), np.cos(big))
    second = np.where(is_sin, np.cos(big), -np.sin(big))
    edge = np.sin(2.0 * np.pi * ((np.arange(LANES) * (band // 2)) % width) / width)
    edge = np.tile(edge, (8, band // LANES))
    table = np.concatenate([np.cos(fine), np.sin(fine), first, second, edge], axis=0)
    return table.astype(np.float32)


def fold_table(band):
    half = band // 2
    freq, is_sin = basis_slots(band)
    both = np.zeros((2 * band, band), np.float32)
    for slot in range(band):
        places = [half - freq[slot]] if freq[slot] == half else [half - freq[slot], half + freq[slot]]
        for place in places:
            if is_sin[slot]:
                both[band + place, slot] = -1.0 if place > half else 1.0
            else:
                both[place, slot] = 1.0
    return both


def wave(places, band, period):
    offsets = np.arange(band) - band // 2
    angle = 2.0 * np.pi * ((places[:, None] * offsets[None, :]) % period) / period
    return np.cos(angle), np.sin(angle)


def resample_table(band, image):
    assert image == 8 * band
    base = np.arange(image)
    row = np.ones(image)
    for freq in range(1, band):
        row += 2.0 * np.cos(2.0 * np.pi * ((base * freq) % image) / image)
    row /= 2 * band
    place = 4 * np.arange(band)[:, None] + 2
    odd = 2 * np.arange(2 * band)[None, :] + 1
    near, far = row[(odd - place) % image], row[(odd + place) % image]
    fourth = 4 * np.arange(2 * band)[None, :]
    direct = [row[(fourth - place) % image], row[(fourth + place) % image]]
    return np.concatenate([(near + far) / 2, (near - far) / 2, *direct], axis=0)


def column_runs(band, image):
    return (
        (0, band, 2, 4),
        (band, band, image - 2, -4),
        (2 * band, 2 * band, 1, 2),
        (4 * band, 2 * band, image - 1, -2),
        (6 * band, 2 * band, 0, 4),
    )


def halves(table):
    table = np.asarray(table, np.float32)
    top = table.astype(bf16)
    rest = (table - top.astype(np.float32)).astype(bf16)
    return top, rest


def split(value):
    top = value.astype(bf16)
    return top, (value - top.astype(f32)).astype(bf16)


def dot(left, right, left_dim=1, right_dim=0):
    return lax.dot_general(
        left, right, (((left_dim,), (right_dim,)), ((), ())), preferred_element_type=f32
    )


def dot_split(left, right, left_dim=1, right_dim=0):
    go = functools.partial(dot, left_dim=left_dim, right_dim=right_dim)
    return go(left[0], right[0]) + (go(left[1], right[0]) + go(left[0], right[1]))


def basis_rows(table, start, blocks):
    places = (table.shape[0] - 2 * LANES - 8) // 2
    parts = []
    for block in range(blocks):
        a = table[pl.ds(2 * LANES + start + block, 1), :]
        b = table[pl.ds(2 * LANES + places + start + block, 1), :]
        parts.append(a * table[:LANES, :] + b * table[LANES : 2 * LANES, :])
    return parts[0] if blocks == 1 else jnp.concatenate(parts, axis=0)


def edges(table):
    last = table.shape[0] - 8
    half = table.shape[1] // 2
    return table[last : last + 1, :LANES], table[LANES : 2 * LANES, half - 1 : half]


def put(array, row, column, value):
    rows = lax.broadcasted_iota(jnp.int32, array.shape, 0)
    columns = lax.broadcasted_iota(jnp.int32, array.shape, 1)
    return jnp.where((rows == row) & (columns == column), value, array)


def store_pieces(out, array):
    band = array.shape[1]
    pieces = [array[:, place : place + LANES] for place in range(0, band, LANES)]
    flat = pieces[0] if len(pieces) == 1 else jnp.concatenate(pieces, axis=0)
    out[...] = flat.reshape(out.shape)


def load_pieces(ref, band):
    flat = ref[...].reshape(band * band // LANES, LANES)
    pieces = [flat[place : place + band] for place in range(0, flat.shape[0], band)]
    return pieces[0] if len(pieces) == 1 else jnp.concatenate(pieces, axis=1)


def mask_kernel(mask_hbm, table_hbm, out, mask, table, even, odd, sems):
    count, rows_here, chunk = mask.shape
    band = even.shape[1] // 2 * 2
    half = band // 2
    blocks = chunk // LANES
    pairs = count // 2
    order = [place + side * pairs for place in range(pairs) for side in range(2)]

    def copy(place):
        columns = pl.ds(place * chunk, chunk)
        return pltpu.make_async_copy(mask_hbm.at[:, columns], mask.at[place], sems.at[place])

    copy_table = pltpu.make_async_copy(table_hbm, table, sems.at[count])
    copy(order[0]).start()
    copy(order[1]).start()
    copy_table.start()
    for place in order[2:]:
        copy(place).start()
    copy_table.wait()
    line = jnp.zeros((1, LANES), f32)
    for place in range(pairs):
        copy(place).wait()
        copy(place + pairs).wait()
        near = jnp.tanh(mask[place])
        far = jnp.tanh(mask[place + pairs])
        hi, lo = split(basis_rows(table, place * blocks, blocks))
        for total, value, columns in (
            (even, near + far, slice(0, half)),
            (odd, near - far, slice(half, band)),
        ):
            weights = jnp.concatenate([hi[:, columns], lo[:, columns]], axis=1)
            product = dot(jnp.concatenate(split(value), axis=0), weights)
            if place == 0:
                total[...] = product
            else:
                total[...] += product
        both_sum = jnp.sum(near + far, axis=0, keepdims=True)
        for start in range(0, chunk, LANES):
            line += both_sum[:, start : start + LANES]
    parts = []
    for total in (even, odd):
        part = total[:rows_here, :] + total[rows_here:, :]
        parts.append(part[:, :half] + part[:, half:])
    row_part = jnp.concatenate(parts, axis=1)
    rows = split(basis_rows(table, lax.axis_index("px"), 1))
    packed = dot_split(rows, split(row_part), 0, 0)
    edge_row, edge_col = edges(table)
    edge_u = jnp.sum(edge_col * row_part[:, 0:1])
    edge_v = jnp.sum(edge_row * line)
    packed = put(put(packed, half - 1, 1, edge_u), 1, half - 1, edge_v)
    store_pieces(out, packed)


def prepare_kernel(
    corner,
    extent,
    y_big,
    y_fine,
    after,
    mask_hbm,
    target,
    y_rows,
    y_cols,
    slope,
    sem,
):
    band = y_fine.shape[2]
    rows_here, image = target.shape
    cols_here = slope.shape[1]
    place_px = lax.axis_index("px")
    place_cond = lax.axis_index("cond")
    mine = pl.ds(pl.multiple_of(place_cond * cols_here, cols_here), cols_here)
    copy_mask = pltpu.make_async_copy(mask_hbm.at[:, mine], slope, sem)
    copy_mask.start()

    rects = corner.shape[1]
    top = corner[0:1, :]
    bottom = top + extent[0:1, :]
    left = corner[1:2, :]
    right = left + extent[1:2, :]
    places = place_px * rows_here + lax.broadcasted_iota(jnp.int32, (rows_here, rects), 0)
    rows_in = jnp.where((places >= top) & (places < bottom), 1.0, 0.0).astype(bf16)
    for start, count, first, stride in column_runs(band, image):
        places = first + stride * lax.broadcasted_iota(jnp.int32, (count, rects), 0)
        cols_in = jnp.where((places >= left) & (places < right), 1.0, 0.0).astype(bf16)
        target[:, start : start + count] = jnp.minimum(dot(rows_in, cols_in, 1, 1), 1.0)

    big_cos = y_big[0, pl.ds(place_px, 1), :]
    big_sin = y_big[1, pl.ds(place_px, 1), :]
    cos_y = (big_cos * y_fine[0] - big_sin * y_fine[1]) * (1.0 / band)
    sin_y = (big_sin * y_fine[0] + big_cos * y_fine[1]) * (1.0 / band)
    waves = jnp.concatenate(
        [
            jnp.concatenate([cos_y, 0.0 - sin_y], axis=1),
            jnp.concatenate([sin_y, cos_y], axis=1),
        ],
        axis=0,
    )
    waves_hi, waves_lo = split(waves)
    y_rows[...] = jnp.concatenate([waves_hi, waves_lo], axis=0)
    waves_hi, waves_lo = waves_hi.astype(f32), waves_lo.astype(f32)
    stacked = jnp.concatenate([waves_hi, waves_hi, waves_lo], axis=0)
    y_cols[...] = jnp.transpose(stacked).astype(bf16)

    copy_mask.wait()
    for start in range(0, cols_here, LANES):
        here = pl.ds(start, LANES)
        transmit = jnp.tanh(slope[:, here])
        slope[:, here] = 1.0 - transmit * transmit


def field_kernel(
    cutoff_hbm,
    weight_hbm,
    dose_hbm,
    packed_hbm,
    both_hbm,
    y_rows_hbm,
    kernels,
    x_hbm,
    up_hbm,
    target_hbm,
    y_cols_hbm,
    both_t_hbm,
    out,
    cutoff,
    weight,
    dose,
    packed,
    both,
    y_rows,
    kern,
    x_wave,
    up,
    target,
    y_cols,
    both_t,
    spec,
    radius,
    prod_hi,
    prod_lo,
    wide_hi,
    wide_lo,
    deep_hi,
    deep_lo,
    cs,
    back,
    gs,
    sems,
    kern_sems,
    *,
    width,
):
    count, _, band, _ = kern.shape
    rows_here, image = target.shape
    half = band // 2
    total_rows = count * rows_here
    part = 64
    pairs = (
        (packed_hbm, packed),
        (cutoff_hbm, cutoff),
        (weight_hbm, weight),
        (dose_hbm, dose),
        (both_hbm, both),
        (y_rows_hbm, y_rows),
        (x_hbm, x_wave),
        (up_hbm, up),
        (target_hbm, target),
        (y_cols_hbm, y_cols),
        (both_t_hbm, both_t),
    )
    copies = [pltpu.make_async_copy(*pair, sems.at[place]) for place, pair in enumerate(pairs)]
    copy_x, copy_up, copy_target, copy_y_cols, copy_both_t = copies[6:]

    def copy(place):
        return pltpu.make_async_copy(kernels.at[0, place], kern.at[place], kern_sems.at[place])

    for early in copies[:6]:
        early.start()
    later = [copy(place) for place in range(count)] + copies[6:]
    for item in later[:AHEAD]:
        item.start()
    fu = lax.broadcasted_iota(jnp.int32, (band, band), 0) - half
    fv = lax.broadcasted_iota(jnp.int32, (band, band), 1) - half
    radius[...] = fu * fu + fv * fv
    for early in copies[:6]:
        early.wait()

    box = load_pieces(packed, band)
    edge_u = box[half - 1 : half, 1:2] * (1.0 / width)
    edge_v = box[1:2, half - 1 : half] * (1.0 / width)
    box_hi, box_lo = split(box * (1.0 / width))
    opened = dot(both[...], box_hi) + dot(both[...], box_lo)
    box_hi, box_lo = split(opened)
    opened = dot(box_hi, both[...], 1, 1) + dot(box_lo, both[...], 1, 1)
    spec_im = opened[band:, :band] + opened[:band, band:]
    spec[0] = opened[:band, :band] - opened[band:, band:]
    at_u = (fu == -half) & (fv == 0)
    at_v = (fu == 0) & (fv == -half)
    spec[1] = spec_im + jnp.where(at_u, edge_u, 0.0) + jnp.where(at_v, edge_v, 0.0)

    for place in range(count):
        copy(place).wait()
        if place + AHEAD < len(later):
            later[place + AHEAD].start()
        limit = cutoff[0, place] * cutoff[0, place]
        slot = place % prod_hi.shape[0]
        for start in range(0, band, part):
            here = pl.ds(start, part)
            there = pl.ds(band + start, part)
            inside = radius[here, :] <= limit
            k_re = jnp.where(inside, kern[place, 0, here, :], 0.0)
            k_im = jnp.where(inside, kern[place, 1, here, :], 0.0)
            kern[place, 0, here, :] = k_re
            kern[place, 1, here, :] = k_im
            s_re = spec[0, here, :]
            s_im = spec[1, here, :]
            re_hi, re_lo = split(k_re * s_re - k_im * s_im)
            im_hi, im_lo = split(k_re * s_im + k_im * s_re)
            prod_hi[slot, here, :] = re_hi
            prod_lo[slot, here, :] = re_lo
            prod_hi[slot, there, :] = im_hi
            prod_lo[slot, there, :] = im_lo
        main = dot(y_rows[...], prod_hi[slot])
        rest = dot(y_rows[: 2 * rows_here, :], prod_lo[slot])
        hi, lo = split(main[: 2 * rows_here] + (main[2 * rows_here :] + rest))
        here = pl.ds(place * rows_here, rows_here)
        there = pl.ds(total_rows + place * rows_here, rows_here)
        wide_hi[here, :] = hi[:rows_here]
        wide_lo[here, :] = lo[:rows_here]
        wide_hi[there, :] = hi[rows_here:]
        wide_lo[there, :] = lo[rows_here:]

    for item in later[count + AHEAD :]:
        item.start()
    copy_x.wait()
    cs[...] = dot_split((wide_hi[...], wide_lo[...]), (x_wave[0], x_wave[1]))

    def fields(place):
        here = pl.ds(place * rows_here, rows_here)
        there = pl.ds(total_rows + place * rows_here, rows_here)
        c_re = cs[here, :band]
        s_re = cs[here, band:]
        c_im = cs[there, :band]
        s_im = cs[there, band:]
        return (c_re - s_im, c_im + s_re, c_re + s_im, c_im - s_re), here, there

    plus = jnp.zeros((rows_here, band), f32)
    minus = jnp.zeros((rows_here, band), f32)
    for place in range(count):
        (p_re, p_im, m_re, m_im), _, _ = fields(place)
        scale = weight[0, place]
        plus += scale * (p_re * p_re + p_im * p_im)
        minus += scale * (m_re * m_re + m_im * m_im)
    dose_here = dose[0]
    scale = 2.0 * (width / band) * steepness * dose_here

    def slope_of(intensity, start):
        level = steepness * (dose_here * intensity - threshold)
        resist = 1.0 / (1.0 + jnp.exp(0.0 - level))
        aim = target[:, start : start + intensity.shape[1]]
        return scale * (resist - aim) * resist * (1.0 - resist)

    def resample(value, rows, transposed):
        hi, lo = split(value)
        dim = 1 if transposed else 0
        main = dot(jnp.concatenate([hi, lo], axis=0), up[0, rows, :], 1, dim)
        rest = dot(hi, up[1, rows, :], 1, dim)
        return main[:rows_here] + (main[rows_here:] + rest)

    sums, gaps, whole_rows = slice(0, band), slice(band, 2 * band), slice(2 * band, 4 * band)
    copy_up.wait()
    copy_target.wait()
    sum_part = resample(plus + minus, sums, False)
    gap_part = resample(plus - minus, gaps, False)
    fourth = resample(jnp.concatenate([plus, minus], axis=1), whole_rows, False)
    slope_plus = slope_of(plus, 0)
    slope_minus = slope_of(minus, band)
    right = slope_of(sum_part + gap_part, 2 * band)
    left = slope_of(sum_part - gap_part, 4 * band)
    fourth = resample(slope_of(fourth, 6 * band), whole_rows, True)
    sum_part = resample(right + left, sums, True)
    gap_part = resample(right - left, gaps, True)
    slope_plus = 2.0 * (slope_plus + (sum_part + gap_part) + fourth[:, :band])
    slope_minus = 2.0 * (slope_minus + (sum_part - gap_part) + fourth[:, band:])

    for place in range(count):
        (p_re, p_im, m_re, m_im), here, there = fields(place)
        scale = weight[0, place]
        plus = scale * slope_plus
        minus = scale * slope_minus
        p_re, p_im, m_re, m_im = plus * p_re, plus * p_im, minus * m_re, minus * m_im
        for rows, columns, value in (
            (here, slice(0, band), p_re + m_re),
            (here, slice(band, 2 * band), p_im - m_im),
            (there, slice(0, band), p_im + m_im),
            (there, slice(band, 2 * band), m_re - p_re),
        ):
            hi, lo = split(value)
            deep_hi[rows, columns] = hi
            deep_lo[rows, columns] = lo
    back[...] = dot_split((deep_hi[...], deep_lo[...]), (x_wave[0], x_wave[1]), 1, 1)

    copy_y_cols.wait()
    copy_both_t.wait()
    for place in range(count):
        here = pl.ds(place * rows_here, rows_here)
        there = pl.ds(total_rows + place * rows_here, rows_here)
        hi, lo = split(jnp.concatenate([back[here, :], back[there, :]], axis=0))
        grad = dot(y_cols[...], jnp.concatenate([hi, lo, hi], axis=0))
        for start in range(0, band, part):
            here = pl.ds(start, part)
            k_re = kern[place, 0, here, :]
            k_im = kern[place, 1, here, :]
            g_re = grad[start : start + part]
            g_im = grad[band + start : band + start + part]
            if place == 0:
                gs[0, here, :] = k_re * g_re + k_im * g_im
                gs[1, here, :] = k_re * g_im - k_im * g_re
            else:
                gs[0, here, :] += k_re * g_re + k_im * g_im
                gs[1, here, :] += k_re * g_im - k_im * g_re
    g_re = gs[0]
    g_im = gs[1]
    edge_u = g_im[0:1, half : half + 1]
    edge_v = g_im[half : half + 1, 0:1]
    re_hi, re_lo = split(g_re)
    im_hi, im_lo = split(g_im)
    even, odd = both_t[:, :band], both_t[:, band:]
    left = dot(even, re_hi) + dot(even, re_lo) + dot(odd, im_hi) + dot(odd, im_lo)
    right = dot(even, im_hi) + dot(even, im_lo) - dot(odd, re_hi) - dot(odd, re_lo)
    l_hi, l_lo = split(left)
    r_hi, r_lo = split(right)
    even, odd = both[:band, :], both[band:, :]
    folded = dot(l_hi, even) + dot(l_lo, even) + dot(r_hi, odd) + dot(r_lo, odd)
    store_pieces(out, put(put(folded, half - 1, 1, edge_u), 1, half - 1, edge_v))


def spread_kernel(packed, table, slope_hbm, out_hbm, slope, out, cols, in_sems, out_sems):
    steps, count, step = out.shape
    band = table.shape[1]
    half = band // 2
    blocks = step // LANES
    width = (table.shape[0] - 2 * LANES - 8) // 2 * LANES
    first_block = lax.axis_index("cond") * (steps * blocks)

    def copy_in(place):
        here = pl.ds(place * step, step)
        return pltpu.make_async_copy(slope_hbm.at[:, here], slope.at[place], in_sems.at[place])

    def copy_out(place):
        here = pl.ds(place * step, step)
        return pltpu.make_async_copy(out.at[place], out_hbm.at[:, here], out_sems.at[place])

    for place in range(steps):
        copy_in(place).start()
    row_hi, row_lo = split(basis_rows(table, lax.axis_index("px"), 1))
    for place in range(steps):
        hi, lo = split(basis_rows(table, first_block + place * blocks, blocks))
        cols[place, 0] = hi
        cols[place, 1] = lo
    box = load_pieces(packed, band) * (1.0 / width)
    edge_u = box[half - 1 : half, 1:2]
    edge_v = box[1:2, half - 1 : half]
    box = put(put(box, half - 1, 1, 0.0), 1, half - 1, 0.0)
    mixed_hi, mixed_lo = split(dot_split((row_hi, row_lo), split(box)))
    mixed = jnp.concatenate([mixed_hi, mixed_lo], axis=0)
    edge_row, edge_col = edges(table)
    side = edge_u * edge_col + edge_v * edge_row
    for place in range(steps):
        copy_in(place).wait()
        main = dot(mixed, cols[place, 0], 1, 1)
        rest = dot(mixed_hi, cols[place, 1], 1, 1)
        grad = main[:count] + (main[count:] + rest)
        for inner in range(0, step, LANES):
            there = pl.ds(inner, LANES)
            out[place, :, there] = (grad[:, inner : inner + LANES] + side) * slope[place, :, there]
        copy_out(place).start()
    for place in range(steps):
        copy_out(place).wait()


def params(mebibytes):
    return pltpu.CompilerParams(vmem_limit_bytes=mebibytes * 1024 * 1024)


vmem = pl.BlockSpec(memory_space=pltpu.VMEM)
anywhere = pl.BlockSpec(memory_space=pl.ANY)


def call_mask(mask_level, table, pieces):
    rows_here, width = mask_level.shape
    band = table.shape[1]
    chunk = min(512, width // 4)
    steps = width // chunk
    return pl.pallas_call(
        mask_kernel,
        out_shape=jax.ShapeDtypeStruct(pieces, f32),
        in_specs=[anywhere, anywhere],
        out_specs=vmem,
        scratch_shapes=[
            pltpu.VMEM((steps, rows_here, chunk), f32),
            pltpu.VMEM(table.shape, f32),
            pltpu.VMEM((2 * rows_here, band), f32),
            pltpu.VMEM((2 * rows_here, band), f32),
            pltpu.SemaphoreType.DMA((steps + 1,)),
        ],
        compiler_params=params(ROOM),
        name="mask_rows",
    )(mask_level, table)


def call_prepare(shape_corner, shape_extent, after, mask_level, band, pencils, conds):
    rows_here, width = mask_level.shape
    image_rows = IMAGE // pencils
    cols_here = width // conds
    y_big = np.stack(wave(image_rows * np.arange(pencils), band, IMAGE)).astype(np.float32)
    y_fine = np.stack(wave(np.arange(image_rows), band, IMAGE)).astype(np.float32)
    shapes = [
        ((image_rows, IMAGE), f32),
        ((4 * image_rows, 2 * band), bf16),
        ((2 * band, 6 * image_rows), bf16),
        ((rows_here, cols_here), f32),
    ]
    return pl.pallas_call(
        prepare_kernel,
        out_shape=[jax.ShapeDtypeStruct(*shape) for shape in shapes],
        in_specs=[vmem] * 4 + [anywhere] * 2,
        out_specs=[vmem] * len(shapes),
        scratch_shapes=[pltpu.SemaphoreType.DMA],
        compiler_params=params(ROOM),
        cost_estimate=pl.CostEstimate(flops=10**9, bytes_accessed=2 * 10**7, transcendentals=10**6),
        name="prepare",
    )(shape_corner.T, shape_extent.T, y_big, y_fine, after, mask_level)


def call_field(
    band_cutoff, kernel_weight, dose_scale, packed, socs_kernels, target, y_rows, y_cols, width
):
    _, count, _, band, _ = socs_kernels.shape
    image_rows = target.shape[0]
    both = fold_table(band)
    x_cos, x_sin = wave(2 * np.arange(band) + 1, band, 4 * band)
    x_wave = np.stack(halves(np.concatenate([x_cos.T, x_sin.T], axis=1)))
    up = np.stack(halves(resample_table(band, IMAGE)))
    deep = 2 * count * image_rows
    return pl.pallas_call(
        functools.partial(field_kernel, width=width),
        out_shape=jax.ShapeDtypeStruct(packed.shape, f32),
        in_specs=[anywhere] * 12,
        out_specs=vmem,
        scratch_shapes=[
            pltpu.SMEM(band_cutoff.shape, jnp.int32),
            pltpu.SMEM(kernel_weight.shape, f32),
            pltpu.SMEM(dose_scale.shape, f32),
            pltpu.VMEM(packed.shape, f32),
            pltpu.VMEM(both.shape, bf16),
            pltpu.VMEM(y_rows.shape, bf16),
            pltpu.VMEM((count, 2, band, band), f32),
            pltpu.VMEM(x_wave.shape, bf16),
            pltpu.VMEM(up.shape, bf16),
            pltpu.VMEM(target.shape, f32),
            pltpu.VMEM(y_cols.shape, bf16),
            pltpu.VMEM(both.T.shape, bf16),
            pltpu.VMEM((2, band, band), f32),
            pltpu.VMEM((band, band), jnp.int32),
            pltpu.VMEM((SLOTS, 2 * band, band), bf16),
            pltpu.VMEM((SLOTS, 2 * band, band), bf16),
            pltpu.VMEM((deep, band), bf16),
            pltpu.VMEM((deep, band), bf16),
            pltpu.VMEM((deep, 2 * band), bf16),
            pltpu.VMEM((deep, 2 * band), bf16),
            pltpu.VMEM((deep, 2 * band), f32),
            pltpu.VMEM((deep, band), f32),
            pltpu.VMEM((2, band, band), f32),
            pltpu.SemaphoreType.DMA((11,)),
            pltpu.SemaphoreType.DMA((count,)),
        ],
        compiler_params=params(ROOM),
        name="image_rows",
    )(
        band_cutoff,
        kernel_weight,
        dose_scale,
        packed,
        both.astype(bf16),
        y_rows,
        socs_kernels,
        x_wave,
        up,
        target,
        y_cols,
        both.T.astype(bf16),
    )


def call_spread(folded, slope, table):
    count, cols_here = slope.shape
    band = table.shape[1]
    step = min(512, cols_here)
    steps = cols_here // step
    return pl.pallas_call(
        spread_kernel,
        out_shape=jax.ShapeDtypeStruct(slope.shape, f32),
        in_specs=[vmem, vmem, anywhere],
        out_specs=anywhere,
        scratch_shapes=[
            pltpu.VMEM((steps, count, step), f32),
            pltpu.VMEM((steps, count, step), f32),
            pltpu.VMEM((steps, 2, step, band), bf16),
            pltpu.SemaphoreType.DMA((steps,)),
            pltpu.SemaphoreType.DMA((steps,)),
        ],
        compiler_params=params(40),
        name="mask_gradient",
    )(folded, table, slope)


def local(
    mask_level, socs_kernels, band_cutoff, kernel_weight, dose_scale, shape_corner, shape_extent
):
    width = mask_level.shape[1]
    band = socs_kernels.shape[3]
    pencils = lax.axis_size("px")
    conds = lax.axis_size("cond")
    pieces = (pencils, band * band // LANES // pencils, LANES)
    table = basis_tables(band, width)

    packed = call_mask(mask_level, table, pieces)
    piece = collect(packed)
    target, y_rows, y_cols, slope = call_prepare(
        shape_corner, shape_extent, piece, mask_level, band, pencils, conds
    )
    packed = hand_out(piece, pieces)
    folded = call_field(
        band_cutoff, kernel_weight, dose_scale, packed, socs_kernels, target, y_rows, y_cols, width
    )
    piece = collect(folded)
    others = [
        lax.ppermute(piece, "cond", [(i, (i + d) % conds) for i in range(conds)])
        for d in range(1, conds)
    ]
    piece = functools.reduce(jnp.add, others, piece)
    folded = hand_out(piece, pieces)
    return call_spread(folded, slope, table)


def collect(packed):
    arrived = lax.all_to_all(packed, "px", split_axis=0, concat_axis=0, tiled=True)
    return jnp.sum(arrived, axis=0)


def hand_out(piece, pieces):
    outgoing = jnp.broadcast_to(piece[None], pieces)
    return lax.all_to_all(outgoing, "px", split_axis=0, concat_axis=0, tiled=True)


def solution(mesh):
    in_specs = (
        P("px", None),
        P("cond", None, None, None, None),
        P("cond", None),
        P("cond", None),
        P("cond"),
        P(),
        P(),
    )
    out_specs = P("px", "cond")
    return jax.shard_map(local, mesh=mesh, in_specs=in_specs, out_specs=out_specs, check_vma=False)
```

```python
import functools
import math

import jax
import jax.numpy as jnp
import numpy as np
from jax import lax
from jax.experimental import pallas as pl
from jax.experimental.pallas import tpu as pltpu
from jax.sharding import PartitionSpec as P

IMAGE = 2048
LANES = 128
SLOTS = 2
ROOM = 60
AHEAD = 4
steepness = 6.0
threshold = 0.3
f32 = jnp.float32
bf16 = jnp.bfloat16


def basis_slots(band):
    half = band // 2
    even = np.arange(0, half, 2)
    odd = np.arange(1, half, 2)
    freq = np.concatenate([even, even[1:], [half], odd, odd])
    is_sin = np.concatenate([0 * even, 1 + 0 * even[1:], [0], 0 * odd, 1 + 0 * odd]) > 0
    return freq, is_sin


def basis_tables(band, width):
    freq, is_sin = basis_slots(band)
    fine = 2.0 * np.pi * ((np.arange(LANES)[:, None] * freq[None]) % width) / width
    big = 2.0 * np.pi * ((LANES * np.arange(width // LANES)[:, None] * freq[None]) % width) / width
    first = np.where(is_sin, np.sin(big), np.cos(big))
    second = np.where(is_sin, np.cos(big), -np.sin(big))
    edge = np.sin(2.0 * np.pi * ((np.arange(LANES) * (band // 2)) % width) / width)
    edge = np.tile(edge, (8, band // LANES))
    table = np.concatenate([np.cos(fine), np.sin(fine), first, second, edge], axis=0)
    return table.astype(np.float32)


def fold_table(band):
    half = band // 2
    freq, is_sin = basis_slots(band)
    both = np.zeros((2 * band, band), np.float32)
    for slot in range(band):
        places = [half - freq[slot]] if freq[slot] == half else [half - freq[slot], half + freq[slot]]
        for place in places:
            if is_sin[slot]:
                both[band + place, slot] = -1.0 if place > half else 1.0
            else:
                both[place, slot] = 1.0
    return both


def wave(places, band, period):
    offsets = np.arange(band) - band // 2
    angle = 2.0 * np.pi * ((places[:, None] * offsets[None, :]) % period) / period
    return np.cos(angle), np.sin(angle)


def resample_table(band, image):
    assert image == 8 * band
    base = np.arange(image)
    row = np.ones(image)
    for freq in range(1, band):
        row += 2.0 * np.cos(2.0 * np.pi * ((base * freq) % image) / image)
    row /= 2 * band
    place = 4 * np.arange(band)[:, None] + 2
    odd = 2 * np.arange(2 * band)[None, :] + 1
    near, far = row[(odd - place) % image], row[(odd + place) % image]
    fourth = 4 * np.arange(2 * band)[None, :]
    direct = [row[(fourth - place) % image], row[(fourth + place) % image]]
    return np.concatenate([(near + far) / 2, (near - far) / 2, *direct], axis=0)


def column_runs(band, image):
    return (
        (0, band, 2, 4),
        (band, band, image - 2, -4),
        (2 * band, 2 * band, 1, 2),
        (4 * band, 2 * band, image - 1, -2),
        (6 * band, 2 * band, 0, 4),
    )


def halves(table):
    table = np.asarray(table, np.float32)
    top = table.astype(bf16)
    rest = (table - top.astype(np.float32)).astype(bf16)
    return top, rest


def split(value):
    top = value.astype(bf16)
    return top, (value - top.astype(f32)).astype(bf16)


def dot(left, right, left_dim=1, right_dim=0):
    return lax.dot_general(
        left, right, (((left_dim,), (right_dim,)), ((), ())), preferred_element_type=f32
    )


def dot_split(left, right, left_dim=1, right_dim=0):
    go = functools.partial(dot, left_dim=left_dim, right_dim=right_dim)
    return go(left[0], right[0]) + (go(left[1], right[0]) + go(left[0], right[1]))


def basis_rows(table, start, blocks):
    places = (table.shape[0] - 2 * LANES - 8) // 2
    parts = []
    for block in range(blocks):
        a = table[pl.ds(2 * LANES + start + block, 1), :]
        b = table[pl.ds(2 * LANES + places + start + block, 1), :]
        parts.append(a * table[:LANES, :] + b * table[LANES : 2 * LANES, :])
    return parts[0] if blocks == 1 else jnp.concatenate(parts, axis=0)


def edges(table):
    last = table.shape[0] - 8
    half = table.shape[1] // 2
    return table[last : last + 1, :LANES], table[LANES : 2 * LANES, half - 1 : half]


def put(array, row, column, value):
    rows = lax.broadcasted_iota(jnp.int32, array.shape, 0)
    columns = lax.broadcasted_iota(jnp.int32, array.shape, 1)
    return jnp.where((rows == row) & (columns == column), value, array)


def store_pieces(out, array):
    band = array.shape[1]
    pieces = [array[:, place : place + LANES] for place in range(0, band, LANES)]
    flat = pieces[0] if len(pieces) == 1 else jnp.concatenate(pieces, axis=0)
    out[...] = flat.reshape(out.shape)


def load_pieces(ref, band):
    flat = ref[...].reshape(band * band // LANES, LANES)
    pieces = [flat[place : place + band] for place in range(0, flat.shape[0], band)]
    return pieces[0] if len(pieces) == 1 else jnp.concatenate(pieces, axis=1)


def mask_kernel(mask_hbm, table_hbm, out, mask, table, even, odd, sems):
    count, rows_here, chunk = mask.shape
    band = even.shape[1] // 2 * 2
    half = band // 2
    blocks = chunk // LANES
    pairs = count // 2
    order = [place + side * pairs for place in range(pairs) for side in range(2)]

    def copy(place):
        columns = pl.ds(place * chunk, chunk)
        return pltpu.make_async_copy(mask_hbm.at[:, columns], mask.at[place], sems.at[place])

    copy_table = pltpu.make_async_copy(table_hbm, table, sems.at[count])
    copy(order[0]).start()
    copy(order[1]).start()
    copy_table.start()
    for place in order[2:]:
        copy(place).start()
    copy_table.wait()
    line = jnp.zeros((1, LANES), f32)
    for place in range(pairs):
        copy(place).wait()
        copy(place + pairs).wait()
        near = jnp.tanh(mask[place])
        far = jnp.tanh(mask[place + pairs])
        hi, lo = split(basis_rows(table, place * blocks, blocks))
        for total, value, columns in (
            (even, near + far, slice(0, half)),
            (odd, near - far, slice(half, band)),
        ):
            weights = jnp.concatenate([hi[:, columns], lo[:, columns]], axis=1)
            product = dot(jnp.concatenate(split(value), axis=0), weights)
            if place == 0:
                total[...] = product
            else:
                total[...] += product
        both_sum = jnp.sum(near + far, axis=0, keepdims=True)
        for start in range(0, chunk, LANES):
            line += both_sum[:, start : start + LANES]
    parts = []
    for total in (even, odd):
        part = total[:rows_here, :] + total[rows_here:, :]
        parts.append(part[:, :half] + part[:, half:])
    row_part = jnp.concatenate(parts, axis=1)
    rows = split(basis_rows(table, lax.axis_index("px"), 1))
    packed = dot_split(rows, split(row_part), 0, 0)
    edge_row, edge_col = edges(table)
    edge_u = jnp.sum(edge_col * row_part[:, 0:1])
    edge_v = jnp.sum(edge_row * line)
    packed = put(put(packed, half - 1, 1, edge_u), 1, half - 1, edge_v)
    store_pieces(out, packed)


def prepare_kernel(
    corner,
    extent,
    y_big,
    y_fine,
    table,
    after,
    mask_hbm,
    target,
    y_rows,
    y_cols,
    tables,
    slope,
    sem,
):
    band = y_fine.shape[2]
    rows_here, image = target.shape
    count, cols_here = slope.shape
    count -= 8
    blocks = cols_here // LANES
    width = (table.shape[0] - 2 * LANES - 8) // 2 * LANES
    place_px = lax.axis_index("px")
    place_cond = lax.axis_index("cond")
    mine = pl.ds(pl.multiple_of(place_cond * cols_here, cols_here), cols_here)
    copy_mask = pltpu.make_async_copy(mask_hbm.at[:, mine], slope.at[:count, :], sem)
    copy_mask.start()

    rects = corner.shape[1]
    top = corner[0:1, :]
    bottom = top + extent[0:1, :]
    left = corner[1:2, :]
    right = left + extent[1:2, :]
    places = place_px * rows_here + lax.broadcasted_iota(jnp.int32, (rows_here, rects), 0)
    rows_in = jnp.where((places >= top) & (places < bottom), 1.0, 0.0).astype(bf16)
    for start, run, first, stride in column_runs(band, image):
        places = first + stride * lax.broadcasted_iota(jnp.int32, (run, rects), 0)
        cols_in = jnp.where((places >= left) & (places < right), 1.0, 0.0).astype(bf16)
        target[:, start : start + run] = jnp.minimum(dot(rows_in, cols_in, 1, 1), 1.0)

    big_cos = y_big[0, pl.ds(place_px, 1), :]
    big_sin = y_big[1, pl.ds(place_px, 1), :]
    cos_y = (big_cos * y_fine[0] - big_sin * y_fine[1]) * (1.0 / band)
    sin_y = (big_sin * y_fine[0] + big_cos * y_fine[1]) * (1.0 / band)
    waves = jnp.concatenate(
        [
            jnp.concatenate([cos_y, 0.0 - sin_y], axis=1),
            jnp.concatenate([sin_y, cos_y], axis=1),
        ],
        axis=0,
    )
    waves_hi, waves_lo = split(waves)
    y_rows[...] = jnp.concatenate([waves_hi, waves_lo], axis=0)
    waves_hi, waves_lo = waves_hi.astype(f32), waves_lo.astype(f32)
    stacked = jnp.concatenate([waves_hi, waves_hi, waves_lo], axis=0)
    y_cols[...] = jnp.transpose(stacked).astype(bf16)

    for block in range(blocks + 1):
        here = pl.ds(block * LANES, LANES)
        place = place_cond * blocks + block if block < blocks else place_px
        hi, lo = split(basis_rows(table, place, 1))
        tables[0, here, :] = hi
        tables[1, here, :] = lo
    copy_mask.wait()
    edge_row, _ = edges(table)
    for start in range(0, cols_here, LANES):
        here = pl.ds(start, LANES)
        transmit = jnp.tanh(slope[:count, here])
        slope[:count, here] = (1.0 - transmit * transmit) * (1.0 / width)
        slope[count:, here] = jnp.broadcast_to(edge_row, (8, LANES))


def field_kernel(
    cutoff_hbm,
    weight_hbm,
    dose_hbm,
    packed_hbm,
    both_hbm,
    y_rows_hbm,
    kernels,
    x_hbm,
    up_hbm,
    target_hbm,
    y_cols_hbm,
    both_t_hbm,
    out,
    cutoff,
    weight,
    dose,
    packed,
    both,
    y_rows,
    kern,
    x_wave,
    up,
    target,
    y_cols,
    both_t,
    spec,
    radius,
    prod_hi,
    prod_lo,
    wide_hi,
    wide_lo,
    deep_hi,
    deep_lo,
    cs,
    back,
    gs,
    sems,
    kern_sems,
    *,
    width,
):
    count, _, band, _ = kern.shape
    rows_here, image = target.shape
    half = band // 2
    total_rows = count * rows_here
    part = 64
    pairs = (
        (packed_hbm, packed),
        (cutoff_hbm, cutoff),
        (weight_hbm, weight),
        (dose_hbm, dose),
        (both_hbm, both),
        (y_rows_hbm, y_rows),
        (x_hbm, x_wave),
        (up_hbm, up),
        (target_hbm, target),
        (y_cols_hbm, y_cols),
        (both_t_hbm, both_t),
    )
    copies = [pltpu.make_async_copy(*pair, sems.at[place]) for place, pair in enumerate(pairs)]
    copy_x, copy_up, copy_target, copy_y_cols, copy_both_t = copies[6:]

    def copy(place):
        return pltpu.make_async_copy(kernels.at[0, place], kern.at[place], kern_sems.at[place])

    for early in copies[:6]:
        early.start()
    later = [copy(place) for place in range(count)] + copies[6:]
    for item in later[:AHEAD]:
        item.start()
    fu = lax.broadcasted_iota(jnp.int32, (band, band), 0) - half
    fv = lax.broadcasted_iota(jnp.int32, (band, band), 1) - half
    radius[...] = fu * fu + fv * fv
    for early in copies[:6]:
        early.wait()

    box = load_pieces(packed, band)
    edge_u = box[half - 1 : half, 1:2] * (1.0 / width)
    edge_v = box[1:2, half - 1 : half] * (1.0 / width)
    box_hi, box_lo = split(box * (1.0 / width))
    opened = dot(both[...], box_hi) + dot(both[...], box_lo)
    box_hi, box_lo = split(opened)
    opened = dot(box_hi, both[...], 1, 1) + dot(box_lo, both[...], 1, 1)
    spec_im = opened[band:, :band] + opened[:band, band:]
    spec[0] = opened[:band, :band] - opened[band:, band:]
    at_u = (fu == -half) & (fv == 0)
    at_v = (fu == 0) & (fv == -half)
    spec[1] = spec_im + jnp.where(at_u, edge_u, 0.0) + jnp.where(at_v, edge_v, 0.0)

    for place in range(count):
        copy(place).wait()
        if place + AHEAD < len(later):
            later[place + AHEAD].start()
        limit = cutoff[0, place] * cutoff[0, place]
        slot = place % prod_hi.shape[0]
        for start in range(0, band, part):
            here = pl.ds(start, part)
            there = pl.ds(band + start, part)
            inside = radius[here, :] <= limit
            k_re = jnp.where(inside, kern[place, 0, here, :], 0.0)
            k_im = jnp.where(inside, kern[place, 1, here, :], 0.0)
            kern[place, 0, here, :] = k_re
            kern[place, 1, here, :] = k_im
            s_re = spec[0, here, :]
            s_im = spec[1, here, :]
            re_hi, re_lo = split(k_re * s_re - k_im * s_im)
            im_hi, im_lo = split(k_re * s_im + k_im * s_re)
            prod_hi[slot, here, :] = re_hi
            prod_lo[slot, here, :] = re_lo
            prod_hi[slot, there, :] = im_hi
            prod_lo[slot, there, :] = im_lo
        main = dot(y_rows[...], prod_hi[slot])
        rest = dot(y_rows[: 2 * rows_here, :], prod_lo[slot])
        hi, lo = split(main[: 2 * rows_here] + (main[2 * rows_here :] + rest))
        here = pl.ds(place * rows_here, rows_here)
        there = pl.ds(total_rows + place * rows_here, rows_here)
        wide_hi[here, :] = hi[:rows_here]
        wide_lo[here, :] = lo[:rows_here]
        wide_hi[there, :] = hi[rows_here:]
        wide_lo[there, :] = lo[rows_here:]

    for item in later[count + AHEAD :]:
        item.start()
    copy_x.wait()
    cs[...] = dot_split((wide_hi[...], wide_lo[...]), (x_wave[0], x_wave[1]))

    def fields(place):
        here = pl.ds(place * rows_here, rows_here)
        there = pl.ds(total_rows + place * rows_here, rows_here)
        c_re = cs[here, :band]
        s_re = cs[here, band:]
        c_im = cs[there, :band]
        s_im = cs[there, band:]
        return (c_re - s_im, c_im + s_re, c_re + s_im, c_im - s_re), here, there

    plus = jnp.zeros((rows_here, band), f32)
    minus = jnp.zeros((rows_here, band), f32)
    for place in range(count):
        (p_re, p_im, m_re, m_im), _, _ = fields(place)
        scale = weight[0, place]
        plus += scale * (p_re * p_re + p_im * p_im)
        minus += scale * (m_re * m_re + m_im * m_im)
    dose_here = dose[0]
    scale = 2.0 * (width / band) * steepness * dose_here

    def slope_of(intensity, start):
        level = steepness * (dose_here * intensity - threshold)
        resist = 1.0 / (1.0 + jnp.exp(0.0 - level))
        aim = target[:, start : start + intensity.shape[1]]
        return scale * (resist - aim) * resist * (1.0 - resist)

    def resample(value, rows, transposed):
        hi, lo = split(value)
        dim = 1 if transposed else 0
        main = dot(jnp.concatenate([hi, lo], axis=0), up[0, rows, :], 1, dim)
        rest = dot(hi, up[1, rows, :], 1, dim)
        return main[:rows_here] + (main[rows_here:] + rest)

    sums, gaps, whole_rows = slice(0, band), slice(band, 2 * band), slice(2 * band, 4 * band)
    copy_up.wait()
    copy_target.wait()
    sum_part = resample(plus + minus, sums, False)
    gap_part = resample(plus - minus, gaps, False)
    fourth = resample(jnp.concatenate([plus, minus], axis=1), whole_rows, False)
    slope_plus = slope_of(plus, 0)
    slope_minus = slope_of(minus, band)
    right = slope_of(sum_part + gap_part, 2 * band)
    left = slope_of(sum_part - gap_part, 4 * band)
    fourth = resample(slope_of(fourth, 6 * band), whole_rows, True)
    sum_part = resample(right + left, sums, True)
    gap_part = resample(right - left, gaps, True)
    slope_plus = 2.0 * (slope_plus + (sum_part + gap_part) + fourth[:, :band])
    slope_minus = 2.0 * (slope_minus + (sum_part - gap_part) + fourth[:, band:])

    for place in range(count):
        (p_re, p_im, m_re, m_im), here, there = fields(place)
        scale = weight[0, place]
        plus = scale * slope_plus
        minus = scale * slope_minus
        p_re, p_im, m_re, m_im = plus * p_re, plus * p_im, minus * m_re, minus * m_im
        for rows, columns, value in (
            (here, slice(0, band), p_re + m_re),
            (here, slice(band, 2 * band), p_im - m_im),
            (there, slice(0, band), p_im + m_im),
            (there, slice(band, 2 * band), m_re - p_re),
        ):
            hi, lo = split(value)
            deep_hi[rows, columns] = hi
            deep_lo[rows, columns] = lo
    back[...] = dot_split((deep_hi[...], deep_lo[...]), (x_wave[0], x_wave[1]), 1, 1)

    copy_y_cols.wait()
    copy_both_t.wait()
    for place in range(count):
        here = pl.ds(place * rows_here, rows_here)
        there = pl.ds(total_rows + place * rows_here, rows_here)
        hi, lo = split(jnp.concatenate([back[here, :], back[there, :]], axis=0))
        grad = dot(y_cols[...], jnp.concatenate([hi, lo, hi], axis=0))
        for start in range(0, band, part):
            here = pl.ds(start, part)
            k_re = kern[place, 0, here, :]
            k_im = kern[place, 1, here, :]
            g_re = grad[start : start + part]
            g_im = grad[band + start : band + start + part]
            if place == 0:
                gs[0, here, :] = k_re * g_re + k_im * g_im
                gs[1, here, :] = k_re * g_im - k_im * g_re
            else:
                gs[0, here, :] += k_re * g_re + k_im * g_im
                gs[1, here, :] += k_re * g_im - k_im * g_re
    g_re = gs[0]
    g_im = gs[1]
    edge_u = g_im[0:1, half : half + 1]
    edge_v = g_im[half : half + 1, 0:1]
    re_hi, re_lo = split(g_re)
    im_hi, im_lo = split(g_im)
    stacked = jnp.concatenate([re_hi, re_lo, im_hi, im_lo], axis=0)
    with_even = dot(stacked, both[:band, :])
    with_odd = dot(stacked, both[band:, :])
    re_even = with_even[:band] + with_even[band : 2 * band]
    im_even = with_even[2 * band : 3 * band] + with_even[3 * band :]
    re_odd = with_odd[:band] + with_odd[band : 2 * band]
    im_odd = with_odd[2 * band : 3 * band] + with_odd[3 * band :]
    hi, lo = split(jnp.concatenate([re_even + im_odd, im_even - re_odd], axis=0))
    folded = dot(both_t[...], hi) + dot(both_t[...], lo)
    store_pieces(out, put(put(folded, half - 1, 1, edge_u), 1, half - 1, edge_v))


def spread_kernel(packed, tables, slope, out):
    count, cols_here = out.shape
    band = tables.shape[2]
    half = band // 2
    rows = pl.ds(cols_here, count)
    box = load_pieces(packed, band)
    edge_u = box[half - 1 : half, 1:2]
    edge_v = box[1:2, half - 1 : half]
    box = put(put(box, half - 1, 1, 0.0), 1, half - 1, 0.0)
    mixed_hi, mixed_lo = split(dot_split((tables[0, rows, :], tables[1, rows, :]), split(box)))
    mixed = jnp.concatenate([mixed_hi, mixed_lo], axis=0)
    edge = jnp.broadcast_to(slope[count : count + 1, :LANES], (LANES, LANES))
    side = edge_u * jnp.transpose(edge) + edge_v * edge
    step = min(512, cols_here)
    for start in range(0, cols_here, step):
        here = pl.ds(start, step)
        main = dot(mixed, tables[0, here, :], 1, 1)
        rest = dot(mixed_hi, tables[1, here, :], 1, 1)
        grad = main[:count] + (main[count:] + rest)
        for inner in range(0, step, LANES):
            there = pl.ds(start + inner, LANES)
            out[:, there] = (grad[:, inner : inner + LANES] + side) * slope[:count, there]


def params(mebibytes):
    return pltpu.CompilerParams(vmem_limit_bytes=mebibytes * 1024 * 1024)


vmem = pl.BlockSpec(memory_space=pltpu.VMEM)
anywhere = pl.BlockSpec(memory_space=pl.ANY)


def call_mask(mask_level, table, pieces):
    rows_here, width = mask_level.shape
    band = table.shape[1]
    chunk = min(512, width // 4)
    steps = width // chunk
    return pl.pallas_call(
        mask_kernel,
        out_shape=jax.ShapeDtypeStruct(pieces, f32),
        in_specs=[anywhere, anywhere],
        out_specs=vmem,
        scratch_shapes=[
            pltpu.VMEM((steps, rows_here, chunk), f32),
            pltpu.VMEM(table.shape, f32),
            pltpu.VMEM((2 * rows_here, band), f32),
            pltpu.VMEM((2 * rows_here, band), f32),
            pltpu.SemaphoreType.DMA((steps + 1,)),
        ],
        compiler_params=params(ROOM),
        name="mask_rows",
    )(mask_level, table)


def call_prepare(shape_corner, shape_extent, after, mask_level, table, pencils, conds):
    rows_here, width = mask_level.shape
    band = table.shape[1]
    image_rows = IMAGE // pencils
    cols_here = width // conds
    y_big = np.stack(wave(image_rows * np.arange(pencils), band, IMAGE)).astype(np.float32)
    y_fine = np.stack(wave(np.arange(image_rows), band, IMAGE)).astype(np.float32)
    shapes = [
        ((image_rows, IMAGE), f32),
        ((4 * image_rows, 2 * band), bf16),
        ((2 * band, 6 * image_rows), bf16),
        ((2, cols_here + rows_here, band), bf16),
        ((rows_here + 8, cols_here), f32),
    ]
    return pl.pallas_call(
        prepare_kernel,
        out_shape=[jax.ShapeDtypeStruct(*shape) for shape in shapes],
        in_specs=[vmem] * 5 + [anywhere] * 2,
        out_specs=[vmem] * len(shapes),
        scratch_shapes=[pltpu.SemaphoreType.DMA],
        compiler_params=params(ROOM),
        cost_estimate=pl.CostEstimate(flops=10**9, bytes_accessed=2 * 10**7, transcendentals=10**6),
        name="prepare",
    )(shape_corner.T, shape_extent.T, y_big, y_fine, table, after, mask_level)


def call_field(
    band_cutoff, kernel_weight, dose_scale, packed, socs_kernels, target, y_rows, y_cols, width
):
    _, count, _, band, _ = socs_kernels.shape
    image_rows = target.shape[0]
    both = fold_table(band)
    x_cos, x_sin = wave(2 * np.arange(band) + 1, band, 4 * band)
    x_wave = np.stack(halves(np.concatenate([x_cos.T, x_sin.T], axis=1)))
    up = np.stack(halves(resample_table(band, IMAGE)))
    deep = 2 * count * image_rows
    return pl.pallas_call(
        functools.partial(field_kernel, width=width),
        out_shape=jax.ShapeDtypeStruct(packed.shape, f32),
        in_specs=[anywhere] * 12,
        out_specs=vmem,
        scratch_shapes=[
            pltpu.SMEM(band_cutoff.shape, jnp.int32),
            pltpu.SMEM(kernel_weight.shape, f32),
            pltpu.SMEM(dose_scale.shape, f32),
            pltpu.VMEM(packed.shape, f32),
            pltpu.VMEM(both.shape, bf16),
            pltpu.VMEM(y_rows.shape, bf16),
            pltpu.VMEM((count, 2, band, band), f32),
            pltpu.VMEM(x_wave.shape, bf16),
            pltpu.VMEM(up.shape, bf16),
            pltpu.VMEM(target.shape, f32),
            pltpu.VMEM(y_cols.shape, bf16),
            pltpu.VMEM(both.T.shape, bf16),
            pltpu.VMEM((2, band, band), f32),
            pltpu.VMEM((band, band), jnp.int32),
            pltpu.VMEM((SLOTS, 2 * band, band), bf16),
            pltpu.VMEM((SLOTS, 2 * band, band), bf16),
            pltpu.VMEM((deep, band), bf16),
            pltpu.VMEM((deep, band), bf16),
            pltpu.VMEM((deep, 2 * band), bf16),
            pltpu.VMEM((deep, 2 * band), bf16),
            pltpu.VMEM((deep, 2 * band), f32),
            pltpu.VMEM((deep, band), f32),
            pltpu.VMEM((2, band, band), f32),
            pltpu.SemaphoreType.DMA((11,)),
            pltpu.SemaphoreType.DMA((count,)),
        ],
        compiler_params=params(ROOM),
        name="image_rows",
    )(
        band_cutoff,
        kernel_weight,
        dose_scale,
        packed,
        both.astype(bf16),
        y_rows,
        socs_kernels,
        x_wave,
        up,
        target,
        y_cols,
        both.T.astype(bf16),
    )


def call_spread(folded, tables, slope):
    count, cols_here = slope.shape
    return pl.pallas_call(
        spread_kernel,
        out_shape=jax.ShapeDtypeStruct((count - 8, cols_here), f32),
        in_specs=[vmem] * 3,
        out_specs=vmem,
        compiler_params=params(40),
        name="mask_gradient",
    )(folded, tables, slope)


def local(
    mask_level, socs_kernels, band_cutoff, kernel_weight, dose_scale, shape_corner, shape_extent
):
    width = mask_level.shape[1]
    band = socs_kernels.shape[3]
    pencils = lax.axis_size("px")
    conds = lax.axis_size("cond")
    pieces = (pencils, band * band // LANES // pencils, LANES)
    table = basis_tables(band, width)

    packed = call_mask(mask_level, table, pieces)
    piece = collect(packed)
    target, y_rows, y_cols, tables, slope = call_prepare(
        shape_corner, shape_extent, piece, mask_level, table, pencils, conds
    )
    packed = hand_out(piece, pieces)
    folded = call_field(
        band_cutoff, kernel_weight, dose_scale, packed, socs_kernels, target, y_rows, y_cols, width
    )
    piece = collect(folded)
    others = [
        lax.ppermute(piece, "cond", [(i, (i + d) % conds) for i in range(conds)])
        for d in range(1, conds)
    ]
    piece = functools.reduce(jnp.add, others, piece)
    folded = hand_out(piece, pieces)
    return call_spread(folded, tables, slope)


def collect(packed):
    arrived = lax.all_to_all(packed, "px", split_axis=0, concat_axis=0, tiled=True)
    return jnp.sum(arrived, axis=0)


def hand_out(piece, pieces):
    outgoing = jnp.broadcast_to(piece[None], pieces)
    return lax.all_to_all(outgoing, "px", split_axis=0, concat_axis=0, tiled=True)


def solution(mesh):
    in_specs = (
        P("px", None),
        P("cond", None, None, None, None),
        P("cond", None),
        P("cond", None),
        P("cond"),
        P(),
        P(),
    )
    out_specs = P("px", "cond")
    return jax.shard_map(local, mesh=mesh, in_specs=in_specs, out_specs=out_specs, check_vma=False)
```

```python
import functools
import math

import jax
import jax.numpy as jnp
import numpy as np
from jax import lax
from jax.experimental import pallas as pl
from jax.experimental.pallas import tpu as pltpu
from jax.sharding import PartitionSpec as P

IMAGE = 2048
LANES = 128
SLOTS = 2
ROOM = 60
AHEAD = 4
steepness = 6.0
threshold = 0.3
f32 = jnp.float32
bf16 = jnp.bfloat16


def basis_slots(band):
    half = band // 2
    even = np.arange(0, half, 2)
    odd = np.arange(1, half, 2)
    freq = np.concatenate([even, even[1:], [half], odd, odd])
    is_sin = np.concatenate([0 * even, 1 + 0 * even[1:], [0], 0 * odd, 1 + 0 * odd]) > 0
    return freq, is_sin


def basis_tables(band, width):
    freq, is_sin = basis_slots(band)
    fine = 2.0 * np.pi * ((np.arange(LANES)[:, None] * freq[None]) % width) / width
    big = 2.0 * np.pi * ((LANES * np.arange(width // LANES)[:, None] * freq[None]) % width) / width
    first = np.where(is_sin, np.sin(big), np.cos(big))
    second = np.where(is_sin, np.cos(big), -np.sin(big))
    edge = np.sin(2.0 * np.pi * ((np.arange(LANES) * (band // 2)) % width) / width)
    edge = np.tile(edge, (8, band // LANES))
    table = np.concatenate([np.cos(fine), np.sin(fine), first, second, edge], axis=0)
    return table.astype(np.float32)


def fold_table(band):
    half = band // 2
    freq, is_sin = basis_slots(band)
    both = np.zeros((2 * band, band), np.float32)
    for slot in range(band):
        places = [half - freq[slot]] if freq[slot] == half else [half - freq[slot], half + freq[slot]]
        for place in places:
            if is_sin[slot]:
                both[band + place, slot] = -1.0 if place > half else 1.0
            else:
                both[place, slot] = 1.0
    return both


def wave(places, band, period):
    offsets = np.arange(band) - band // 2
    angle = 2.0 * np.pi * ((places[:, None] * offsets[None, :]) % period) / period
    return np.cos(angle), np.sin(angle)


def resample_table(band, image):
    assert image == 8 * band
    base = np.arange(image)
    row = np.ones(image)
    for freq in range(1, band):
        row += 2.0 * np.cos(2.0 * np.pi * ((base * freq) % image) / image)
    row /= 2 * band
    place = 4 * np.arange(band)[:, None] + 2
    odd = 2 * np.arange(2 * band)[None, :] + 1
    near, far = row[(odd - place) % image], row[(odd + place) % image]
    fourth = 4 * np.arange(2 * band)[None, :]
    direct = [row[(fourth - place) % image], row[(fourth + place) % image]]
    return np.concatenate([(near + far) / 2, (near - far) / 2, *direct], axis=0)


def column_runs(band, image):
    return (
        (0, band, 2, 4),
        (band, band, image - 2, -4),
        (2 * band, 2 * band, 1, 2),
        (4 * band, 2 * band, image - 1, -2),
        (6 * band, 2 * band, 0, 4),
    )


def halves(table):
    table = np.asarray(table, np.float32)
    top = table.astype(bf16)
    rest = (table - top.astype(np.float32)).astype(bf16)
    return top, rest


def split(value):
    top = value.astype(bf16)
    return top, (value - top.astype(f32)).astype(bf16)


def dot(left, right, left_dim=1, right_dim=0):
    return lax.dot_general(
        left, right, (((left_dim,), (right_dim,)), ((), ())), preferred_element_type=f32
    )


def dot_split(left, right, left_dim=1, right_dim=0):
    go = functools.partial(dot, left_dim=left_dim, right_dim=right_dim)
    return go(left[0], right[0]) + (go(left[1], right[0]) + go(left[0], right[1]))


def basis_rows(table, start, blocks):
    places = (table.shape[0] - 2 * LANES - 8) // 2
    parts = []
    for block in range(blocks):
        a = table[pl.ds(2 * LANES + start + block, 1), :]
        b = table[pl.ds(2 * LANES + places + start + block, 1), :]
        parts.append(a * table[:LANES, :] + b * table[LANES : 2 * LANES, :])
    return parts[0] if blocks == 1 else jnp.concatenate(parts, axis=0)


def edges(table):
    last = table.shape[0] - 8
    half = table.shape[1] // 2
    return table[last : last + 1, :LANES], table[LANES : 2 * LANES, half - 1 : half]


def put(array, row, column, value):
    rows = lax.broadcasted_iota(jnp.int32, array.shape, 0)
    columns = lax.broadcasted_iota(jnp.int32, array.shape, 1)
    return jnp.where((rows == row) & (columns == column), value, array)


def store_pieces(out, array):
    band = array.shape[1]
    pieces = [array[:, place : place + LANES] for place in range(0, band, LANES)]
    flat = pieces[0] if len(pieces) == 1 else jnp.concatenate(pieces, axis=0)
    out[...] = flat.reshape(out.shape)


def load_pieces(ref, band):
    flat = ref[...].reshape(band * band // LANES, LANES)
    pieces = [flat[place : place + band] for place in range(0, flat.shape[0], band)]
    return pieces[0] if len(pieces) == 1 else jnp.concatenate(pieces, axis=1)


def mask_kernel(mask_hbm, table_hbm, out, mask, table, even, odd, sems):
    count, rows_here, chunk = mask.shape
    band = even.shape[1] // 2 * 2
    half = band // 2
    blocks = chunk // LANES
    pairs = count // 2
    order = [place + side * pairs for place in range(pairs) for side in range(2)]

    def copy(place):
        columns = pl.ds(place * chunk, chunk)
        return pltpu.make_async_copy(mask_hbm.at[:, columns], mask.at[place], sems.at[place])

    copy_table = pltpu.make_async_copy(table_hbm, table, sems.at[count])
    copy(order[0]).start()
    copy(order[1]).start()
    copy_table.start()
    for place in order[2:]:
        copy(place).start()
    copy_table.wait()
    line = jnp.zeros((1, LANES), f32)
    for place in range(pairs):
        copy(place).wait()
        copy(place + pairs).wait()
        near = jnp.tanh(mask[place])
        far = jnp.tanh(mask[place + pairs])
        hi, lo = split(basis_rows(table, place * blocks, blocks))
        for total, value, columns in (
            (even, near + far, slice(0, half)),
            (odd, near - far, slice(half, band)),
        ):
            weights = jnp.concatenate([hi[:, columns], lo[:, columns]], axis=1)
            product = dot(jnp.concatenate(split(value), axis=0), weights)
            if place == 0:
                total[...] = product
            else:
                total[...] += product
        both_sum = jnp.sum(near + far, axis=0, keepdims=True)
        for start in range(0, chunk, LANES):
            line += both_sum[:, start : start + LANES]
    parts = []
    for total in (even, odd):
        part = total[:rows_here, :] + total[rows_here:, :]
        parts.append(part[:, :half] + part[:, half:])
    row_part = jnp.concatenate(parts, axis=1)
    rows = split(basis_rows(table, lax.axis_index("px"), 1))
    packed = dot_split(rows, split(row_part), 0, 0)
    edge_row, edge_col = edges(table)
    edge_u = jnp.sum(edge_col * row_part[:, 0:1])
    edge_v = jnp.sum(edge_row * line)
    packed = put(put(packed, half - 1, 1, edge_u), 1, half - 1, edge_v)
    store_pieces(out, packed)


def prepare_kernel(
    corner,
    extent,
    y_big,
    y_fine,
    after,
    mask_hbm,
    target,
    y_rows,
    y_cols,
    slope,
    sem,
):
    band = y_fine.shape[2]
    rows_here, image = target.shape
    cols_here = slope.shape[1]
    place_px = lax.axis_index("px")
    place_cond = lax.axis_index("cond")
    mine = pl.ds(pl.multiple_of(place_cond * cols_here, cols_here), cols_here)
    copy_mask = pltpu.make_async_copy(mask_hbm.at[:, mine], slope, sem)
    copy_mask.start()

    rects = corner.shape[1]
    top = corner[0:1, :]
    bottom = top + extent[0:1, :]
    left = corner[1:2, :]
    right = left + extent[1:2, :]
    places = place_px * rows_here + lax.broadcasted_iota(jnp.int32, (rows_here, rects), 0)
    rows_in = jnp.where((places >= top) & (places < bottom), 1.0, 0.0).astype(bf16)
    for start, count, first, stride in column_runs(band, image):
        places = first + stride * lax.broadcasted_iota(jnp.int32, (count, rects), 0)
        cols_in = jnp.where((places >= left) & (places < right), 1.0, 0.0).astype(bf16)
        target[:, start : start + count] = jnp.minimum(dot(rows_in, cols_in, 1, 1), 1.0)

    big_cos = y_big[0, pl.ds(place_px, 1), :]
    big_sin = y_big[1, pl.ds(place_px, 1), :]
    cos_y = (big_cos * y_fine[0] - big_sin * y_fine[1]) * (1.0 / band)
    sin_y = (big_sin * y_fine[0] + big_cos * y_fine[1]) * (1.0 / band)
    waves = jnp.concatenate(
        [
            jnp.concatenate([cos_y, 0.0 - sin_y], axis=1),
            jnp.concatenate([sin_y, cos_y], axis=1),
        ],
        axis=0,
    )
    waves_hi, waves_lo = split(waves)
    y_rows[...] = jnp.concatenate([waves_hi, waves_lo], axis=0)
    waves_hi, waves_lo = waves_hi.astype(f32), waves_lo.astype(f32)
    stacked = jnp.concatenate([waves_hi, waves_hi, waves_lo], axis=0)
    y_cols[...] = jnp.transpose(stacked).astype(bf16)

    copy_mask.wait()
    for start in range(0, cols_here, LANES):
        here = pl.ds(start, LANES)
        transmit = jnp.tanh(slope[:, here])
        slope[:, here] = 1.0 - transmit * transmit


def field_kernel(
    cutoff_hbm,
    weight_hbm,
    dose_hbm,
    packed_hbm,
    both_hbm,
    y_rows_hbm,
    kernels,
    x_hbm,
    up_hbm,
    target_hbm,
    y_cols_hbm,
    both_t_hbm,
    out,
    cutoff,
    weight,
    dose,
    packed,
    both,
    y_rows,
    kern,
    x_wave,
    up,
    target,
    y_cols,
    both_t,
    spec,
    radius,
    prod_hi,
    prod_lo,
    wide_hi,
    wide_lo,
    deep_hi,
    deep_lo,
    cs,
    back,
    gs,
    sems,
    kern_sems,
    *,
    width,
):
    count, _, band, _ = kern.shape
    rows_here, image = target.shape
    half = band // 2
    total_rows = count * rows_here
    part = 64
    pairs = (
        (packed_hbm, packed),
        (cutoff_hbm, cutoff),
        (weight_hbm, weight),
        (dose_hbm, dose),
        (both_hbm, both),
        (y_rows_hbm, y_rows),
        (x_hbm, x_wave),
        (up_hbm, up),
        (target_hbm, target),
        (y_cols_hbm, y_cols),
        (both_t_hbm, both_t),
    )
    copies = [pltpu.make_async_copy(*pair, sems.at[place]) for place, pair in enumerate(pairs)]
    copy_x, copy_up, copy_target, copy_y_cols, copy_both_t = copies[6:]

    def copy(place):
        return pltpu.make_async_copy(kernels.at[0, place], kern.at[place], kern_sems.at[place])

    for early in copies[:6]:
        early.start()
    later = [copy(place) for place in range(count)] + copies[6:]
    for item in later[:AHEAD]:
        item.start()
    fu = lax.broadcasted_iota(jnp.int32, (band, band), 0) - half
    fv = lax.broadcasted_iota(jnp.int32, (band, band), 1) - half
    radius[...] = fu * fu + fv * fv
    for early in copies[:6]:
        early.wait()

    box = load_pieces(packed, band)
    edge_u = box[half - 1 : half, 1:2] * (1.0 / width)
    edge_v = box[1:2, half - 1 : half] * (1.0 / width)
    box_hi, box_lo = split(box * (1.0 / width))
    opened = dot(both[...], box_hi) + dot(both[...], box_lo)
    box_hi, box_lo = split(opened)
    opened = dot(box_hi, both[...], 1, 1) + dot(box_lo, both[...], 1, 1)
    spec_im = opened[band:, :band] + opened[:band, band:]
    spec[0] = opened[:band, :band] - opened[band:, band:]
    at_u = (fu == -half) & (fv == 0)
    at_v = (fu == 0) & (fv == -half)
    spec[1] = spec_im + jnp.where(at_u, edge_u, 0.0) + jnp.where(at_v, edge_v, 0.0)

    for place in range(count):
        copy(place).wait()
        if place + AHEAD < len(later):
            later[place + AHEAD].start()
        limit = cutoff[0, place] * cutoff[0, place]
        slot = place % prod_hi.shape[0]
        for start in range(0, band, part):
            here = pl.ds(start, part)
            there = pl.ds(band + start, part)
            inside = radius[here, :] <= limit
            k_re = jnp.where(inside, kern[place, 0, here, :], 0.0)
            k_im = jnp.where(inside, kern[place, 1, here, :], 0.0)
            kern[place, 0, here, :] = k_re
            kern[place, 1, here, :] = k_im
            s_re = spec[0, here, :]
            s_im = spec[1, here, :]
            re_hi, re_lo = split(k_re * s_re - k_im * s_im)
            im_hi, im_lo = split(k_re * s_im + k_im * s_re)
            prod_hi[slot, here, :] = re_hi
            prod_lo[slot, here, :] = re_lo
            prod_hi[slot, there, :] = im_hi
            prod_lo[slot, there, :] = im_lo
        main = dot(y_rows[...], prod_hi[slot])
        rest = dot(y_rows[: 2 * rows_here, :], prod_lo[slot])
        hi, lo = split(main[: 2 * rows_here] + (main[2 * rows_here :] + rest))
        here = pl.ds(place * rows_here, rows_here)
        there = pl.ds(total_rows + place * rows_here, rows_here)
        wide_hi[here, :] = hi[:rows_here]
        wide_lo[here, :] = lo[:rows_here]
        wide_hi[there, :] = hi[rows_here:]
        wide_lo[there, :] = lo[rows_here:]

    for item in later[count + AHEAD :]:
        item.start()
    copy_x.wait()
    cs[...] = dot_split((wide_hi[...], wide_lo[...]), (x_wave[0], x_wave[1]))

    def fields(place):
        here = pl.ds(place * rows_here, rows_here)
        there = pl.ds(total_rows + place * rows_here, rows_here)
        c_re = cs[here, :band]
        s_re = cs[here, band:]
        c_im = cs[there, :band]
        s_im = cs[there, band:]
        return (c_re - s_im, c_im + s_re, c_re + s_im, c_im - s_re), here, there

    plus = jnp.zeros((rows_here, band), f32)
    minus = jnp.zeros((rows_here, band), f32)
    for place in range(count):
        (p_re, p_im, m_re, m_im), _, _ = fields(place)
        scale = weight[0, place]
        plus += scale * (p_re * p_re + p_im * p_im)
        minus += scale * (m_re * m_re + m_im * m_im)
    dose_here = dose[0]
    scale = 2.0 * (width / band) * steepness * dose_here

    def slope_of(intensity, start):
        level = steepness * (dose_here * intensity - threshold)
        resist = 1.0 / (1.0 + jnp.exp(0.0 - level))
        aim = target[:, start : start + intensity.shape[1]]
        return scale * (resist - aim) * resist * (1.0 - resist)

    def resample(value, rows, transposed):
        hi, lo = split(value)
        dim = 1 if transposed else 0
        main = dot(jnp.concatenate([hi, lo], axis=0), up[0, rows, :], 1, dim)
        rest = dot(hi, up[1, rows, :], 1, dim)
        return main[:rows_here] + (main[rows_here:] + rest)

    sums, gaps, whole_rows = slice(0, band), slice(band, 2 * band), slice(2 * band, 4 * band)
    copy_up.wait()
    copy_target.wait()
    sum_part = resample(plus + minus, sums, False)
    gap_part = resample(plus - minus, gaps, False)
    fourth = resample(jnp.concatenate([plus, minus], axis=1), whole_rows, False)
    slope_plus = slope_of(plus, 0)
    slope_minus = slope_of(minus, band)
    right = slope_of(sum_part + gap_part, 2 * band)
    left = slope_of(sum_part - gap_part, 4 * band)
    fourth = resample(slope_of(fourth, 6 * band), whole_rows, True)
    sum_part = resample(right + left, sums, True)
    gap_part = resample(right - left, gaps, True)
    slope_plus = 2.0 * (slope_plus + (sum_part + gap_part) + fourth[:, :band])
    slope_minus = 2.0 * (slope_minus + (sum_part - gap_part) + fourth[:, band:])

    for place in range(count):
        (p_re, p_im, m_re, m_im), here, there = fields(place)
        scale = weight[0, place]
        plus = scale * slope_plus
        minus = scale * slope_minus
        p_re, p_im, m_re, m_im = plus * p_re, plus * p_im, minus * m_re, minus * m_im
        for rows, columns, value in (
            (here, slice(0, band), p_re + m_re),
            (here, slice(band, 2 * band), p_im - m_im),
            (there, slice(0, band), p_im + m_im),
            (there, slice(band, 2 * band), m_re - p_re),
        ):
            hi, lo = split(value)
            deep_hi[rows, columns] = hi
            deep_lo[rows, columns] = lo
    back[...] = dot_split((deep_hi[...], deep_lo[...]), (x_wave[0], x_wave[1]), 1, 1)

    copy_y_cols.wait()
    copy_both_t.wait()
    for place in range(count):
        here = pl.ds(place * rows_here, rows_here)
        there = pl.ds(total_rows + place * rows_here, rows_here)
        hi, lo = split(jnp.concatenate([back[here, :], back[there, :]], axis=0))
        grad = dot(y_cols[...], jnp.concatenate([hi, lo, hi], axis=0))
        for start in range(0, band, part):
            here = pl.ds(start, part)
            k_re = kern[place, 0, here, :]
            k_im = kern[place, 1, here, :]
            g_re = grad[start : start + part]
            g_im = grad[band + start : band + start + part]
            if place == 0:
                gs[0, here, :] = k_re * g_re + k_im * g_im
                gs[1, here, :] = k_re * g_im - k_im * g_re
            else:
                gs[0, here, :] += k_re * g_re + k_im * g_im
                gs[1, here, :] += k_re * g_im - k_im * g_re
    g_re = gs[0]
    g_im = gs[1]
    edge_u = g_im[0:1, half : half + 1]
    edge_v = g_im[half : half + 1, 0:1]
    re_hi, re_lo = split(g_re)
    im_hi, im_lo = split(g_im)
    even, odd = both_t[:, :band], both_t[:, band:]
    left = dot(even, re_hi) + dot(even, re_lo) + dot(odd, im_hi) + dot(odd, im_lo)
    right = dot(even, im_hi) + dot(even, im_lo) - dot(odd, re_hi) - dot(odd, re_lo)
    l_hi, l_lo = split(left)
    r_hi, r_lo = split(right)
    even, odd = both[:band, :], both[band:, :]
    folded = dot(l_hi, even) + dot(l_lo, even) + dot(r_hi, odd) + dot(r_lo, odd)
    store_pieces(out, put(put(folded, half - 1, 1, edge_u), 1, half - 1, edge_v))


def spread_kernel(packed, table, slope, out):
    count, cols_here = out.shape
    band = table.shape[1]
    half = band // 2
    step = min(512, cols_here)
    blocks = step // LANES
    width = (table.shape[0] - 2 * LANES - 8) // 2 * LANES
    first_block = lax.axis_index("cond") * (cols_here // LANES)
    box = load_pieces(packed, band) * (1.0 / width)
    edge_u = box[half - 1 : half, 1:2]
    edge_v = box[1:2, half - 1 : half]
    box = put(put(box, half - 1, 1, 0.0), 1, half - 1, 0.0)
    mixed_hi, mixed_lo = split(
        dot_split(split(basis_rows(table, lax.axis_index("px"), 1)), split(box))
    )
    mixed = jnp.concatenate([mixed_hi, mixed_lo], axis=0)
    edge_row, edge_col = edges(table)
    side = edge_u * edge_col + edge_v * edge_row
    for start in range(0, cols_here, step):
        hi, lo = split(basis_rows(table, first_block + start // LANES, blocks))
        main = dot(mixed, hi, 1, 1)
        rest = dot(mixed_hi, lo, 1, 1)
        grad = main[:count] + (main[count:] + rest)
        for inner in range(0, step, LANES):
            there = pl.ds(start + inner, LANES)
            out[:, there] = (grad[:, inner : inner + LANES] + side) * slope[:, there]


def params(mebibytes):
    return pltpu.CompilerParams(vmem_limit_bytes=mebibytes * 1024 * 1024)


vmem = pl.BlockSpec(memory_space=pltpu.VMEM)
anywhere = pl.BlockSpec(memory_space=pl.ANY)


def call_mask(mask_level, table, pieces):
    rows_here, width = mask_level.shape
    band = table.shape[1]
    chunk = min(512, width // 4)
    steps = width // chunk
    return pl.pallas_call(
        mask_kernel,
        out_shape=jax.ShapeDtypeStruct(pieces, f32),
        in_specs=[anywhere, anywhere],
        out_specs=vmem,
        scratch_shapes=[
            pltpu.VMEM((steps, rows_here, chunk), f32),
            pltpu.VMEM(table.shape, f32),
            pltpu.VMEM((2 * rows_here, band), f32),
            pltpu.VMEM((2 * rows_here, band), f32),
            pltpu.SemaphoreType.DMA((steps + 1,)),
        ],
        compiler_params=params(ROOM),
        name="mask_rows",
    )(mask_level, table)


def call_prepare(shape_corner, shape_extent, after, mask_level, band, pencils, conds):
    rows_here, width = mask_level.shape
    image_rows = IMAGE // pencils
    cols_here = width // conds
    y_big = np.stack(wave(image_rows * np.arange(pencils), band, IMAGE)).astype(np.float32)
    y_fine = np.stack(wave(np.arange(image_rows), band, IMAGE)).astype(np.float32)
    shapes = [
        ((image_rows, IMAGE), f32),
        ((4 * image_rows, 2 * band), bf16),
        ((2 * band, 6 * image_rows), bf16),
        ((rows_here, cols_here), f32),
    ]
    return pl.pallas_call(
        prepare_kernel,
        out_shape=[jax.ShapeDtypeStruct(*shape) for shape in shapes],
        in_specs=[vmem] * 4 + [anywhere] * 2,
        out_specs=[vmem] * len(shapes),
        scratch_shapes=[pltpu.SemaphoreType.DMA],
        compiler_params=params(ROOM),
        cost_estimate=pl.CostEstimate(flops=10**9, bytes_accessed=2 * 10**7, transcendentals=10**6),
        name="prepare",
    )(shape_corner.T, shape_extent.T, y_big, y_fine, after, mask_level)


def call_field(
    band_cutoff, kernel_weight, dose_scale, packed, socs_kernels, target, y_rows, y_cols, width
):
    _, count, _, band, _ = socs_kernels.shape
    image_rows = target.shape[0]
    both = fold_table(band)
    x_cos, x_sin = wave(2 * np.arange(band) + 1, band, 4 * band)
    x_wave = np.stack(halves(np.concatenate([x_cos.T, x_sin.T], axis=1)))
    up = np.stack(halves(resample_table(band, IMAGE)))
    deep = 2 * count * image_rows
    return pl.pallas_call(
        functools.partial(field_kernel, width=width),
        out_shape=jax.ShapeDtypeStruct(packed.shape, f32),
        in_specs=[anywhere] * 12,
        out_specs=vmem,
        scratch_shapes=[
            pltpu.SMEM(band_cutoff.shape, jnp.int32),
            pltpu.SMEM(kernel_weight.shape, f32),
            pltpu.SMEM(dose_scale.shape, f32),
            pltpu.VMEM(packed.shape, f32),
            pltpu.VMEM(both.shape, bf16),
            pltpu.VMEM(y_rows.shape, bf16),
            pltpu.VMEM((count, 2, band, band), f32),
            pltpu.VMEM(x_wave.shape, bf16),
            pltpu.VMEM(up.shape, bf16),
            pltpu.VMEM(target.shape, f32),
            pltpu.VMEM(y_cols.shape, bf16),
            pltpu.VMEM(both.T.shape, bf16),
            pltpu.VMEM((2, band, band), f32),
            pltpu.VMEM((band, band), jnp.int32),
            pltpu.VMEM((SLOTS, 2 * band, band), bf16),
            pltpu.VMEM((SLOTS, 2 * band, band), bf16),
            pltpu.VMEM((deep, band), bf16),
            pltpu.VMEM((deep, band), bf16),
            pltpu.VMEM((deep, 2 * band), bf16),
            pltpu.VMEM((deep, 2 * band), bf16),
            pltpu.VMEM((deep, 2 * band), f32),
            pltpu.VMEM((deep, band), f32),
            pltpu.VMEM((2, band, band), f32),
            pltpu.SemaphoreType.DMA((11,)),
            pltpu.SemaphoreType.DMA((count,)),
        ],
        compiler_params=params(ROOM),
        name="image_rows",
    )(
        band_cutoff,
        kernel_weight,
        dose_scale,
        packed,
        both.astype(bf16),
        y_rows,
        socs_kernels,
        x_wave,
        up,
        target,
        y_cols,
        both.T.astype(bf16),
    )


def call_spread(folded, slope, table):
    return pl.pallas_call(
        spread_kernel,
        out_shape=jax.ShapeDtypeStruct(slope.shape, f32),
        in_specs=[vmem] * 3,
        out_specs=vmem,
        compiler_params=params(40),
        name="mask_gradient",
    )(folded, table, slope)


def local(
    mask_level, socs_kernels, band_cutoff, kernel_weight, dose_scale, shape_corner, shape_extent
):
    width = mask_level.shape[1]
    band = socs_kernels.shape[3]
    pencils = lax.axis_size("px")
    conds = lax.axis_size("cond")
    pieces = (pencils, band * band // LANES // pencils, LANES)
    table = basis_tables(band, width)

    packed = call_mask(mask_level, table, pieces)
    piece = collect(packed)
    target, y_rows, y_cols, slope = call_prepare(
        shape_corner, shape_extent, piece, mask_level, band, pencils, conds
    )
    packed = hand_out(piece, pieces)
    folded = call_field(
        band_cutoff, kernel_weight, dose_scale, packed, socs_kernels, target, y_rows, y_cols, width
    )
    piece = collect(folded)
    others = [
        lax.ppermute(piece, "cond", [(i, (i + d) % conds) for i in range(conds)])
        for d in range(1, conds)
    ]
    piece = functools.reduce(jnp.add, others, piece)
    folded = hand_out(piece, pieces)
    return call_spread(folded, slope, table)


def collect(packed):
    arrived = lax.all_to_all(packed, "px", split_axis=0, concat_axis=0, tiled=True)
    return jnp.sum(arrived, axis=0)


def hand_out(piece, pieces):
    outgoing = jnp.broadcast_to(piece[None], pieces)
    return lax.all_to_all(outgoing, "px", split_axis=0, concat_axis=0, tiled=True)


def solution(mesh):
    in_specs = (
        P("px", None),
        P("cond", None, None, None, None),
        P("cond", None),
        P("cond", None),
        P("cond"),
        P(),
        P(),
    )
    out_specs = P("px", "cond")
    return jax.shard_map(local, mesh=mesh, in_specs=in_specs, out_specs=out_specs, check_vma=False)
```

```python
import functools
import math

import jax
import jax.numpy as jnp
import numpy as np
from jax import lax
from jax.experimental import pallas as pl
from jax.experimental.pallas import tpu as pltpu
from jax.sharding import PartitionSpec as P

IMAGE = 2048
LANES = 128
SLOTS = 4
ROOM = 60
AHEAD = 4
steepness = 6.0
threshold = 0.3
f32 = jnp.float32
bf16 = jnp.bfloat16


def basis_slots(band):
    half = band // 2
    even = np.arange(0, half, 2)
    odd = np.arange(1, half, 2)
    freq = np.concatenate([even, even[1:], [half], odd, odd])
    is_sin = np.concatenate([0 * even, 1 + 0 * even[1:], [0], 0 * odd, 1 + 0 * odd]) > 0
    return freq, is_sin


def basis_tables(band, width):
    freq, is_sin = basis_slots(band)
    fine = 2.0 * np.pi * ((np.arange(LANES)[:, None] * freq[None]) % width) / width
    big = 2.0 * np.pi * ((LANES * np.arange(width // LANES)[:, None] * freq[None]) % width) / width
    first = np.where(is_sin, np.sin(big), np.cos(big))
    second = np.where(is_sin, np.cos(big), -np.sin(big))
    edge = np.sin(2.0 * np.pi * ((np.arange(LANES) * (band // 2)) % width) / width)
    edge = np.tile(edge, (8, band // LANES))
    table = np.concatenate([np.cos(fine), np.sin(fine), first, second, edge], axis=0)
    return table.astype(np.float32)


def fold_table(band):
    half = band // 2
    freq, is_sin = basis_slots(band)
    both = np.zeros((2 * band, band), np.float32)
    for slot in range(band):
        places = [half - freq[slot]] if freq[slot] == half else [half - freq[slot], half + freq[slot]]
        for place in places:
            if is_sin[slot]:
                both[band + place, slot] = -1.0 if place > half else 1.0
            else:
                both[place, slot] = 1.0
    return both


def wave(places, band, period):
    offsets = np.arange(band) - band // 2
    angle = 2.0 * np.pi * ((places[:, None] * offsets[None, :]) % period) / period
    return np.cos(angle), np.sin(angle)


def resample_table(band, image):
    assert image == 8 * band
    base = np.arange(image)
    row = np.ones(image)
    for freq in range(1, band):
        row += 2.0 * np.cos(2.0 * np.pi * ((base * freq) % image) / image)
    row /= 2 * band
    place = 4 * np.arange(band)[:, None] + 2
    odd = 2 * np.arange(2 * band)[None, :] + 1
    near, far = row[(odd - place) % image], row[(odd + place) % image]
    fourth = 4 * np.arange(2 * band)[None, :]
    direct = [row[(fourth - place) % image], row[(fourth + place) % image]]
    return np.concatenate([(near + far) / 2, (near - far) / 2, *direct], axis=0)


def column_runs(band, image):
    return (
        (0, band, 2, 4),
        (band, band, image - 2, -4),
        (2 * band, 2 * band, 1, 2),
        (4 * band, 2 * band, image - 1, -2),
        (6 * band, 2 * band, 0, 4),
    )


def halves(table):
    table = np.asarray(table, np.float32)
    top = table.astype(bf16)
    rest = (table - top.astype(np.float32)).astype(bf16)
    return top, rest


def split(value):
    top = value.astype(bf16)
    return top, (value - top.astype(f32)).astype(bf16)


def dot(left, right, left_dim=1, right_dim=0):
    return lax.dot_general(
        left, right, (((left_dim,), (right_dim,)), ((), ())), preferred_element_type=f32
    )


def dot_split(left, right, left_dim=1, right_dim=0):
    go = functools.partial(dot, left_dim=left_dim, right_dim=right_dim)
    return go(left[0], right[0]) + (go(left[1], right[0]) + go(left[0], right[1]))


def basis_rows(table, start, blocks):
    places = (table.shape[0] - 2 * LANES - 8) // 2
    parts = []
    for block in range(blocks):
        a = table[pl.ds(2 * LANES + start + block, 1), :]
        b = table[pl.ds(2 * LANES + places + start + block, 1), :]
        parts.append(a * table[:LANES, :] + b * table[LANES : 2 * LANES, :])
    return parts[0] if blocks == 1 else jnp.concatenate(parts, axis=0)


def edges(table):
    last = table.shape[0] - 8
    half = table.shape[1] // 2
    return table[last : last + 1, :LANES], table[LANES : 2 * LANES, half - 1 : half]


def put(array, row, column, value):
    rows = lax.broadcasted_iota(jnp.int32, array.shape, 0)
    columns = lax.broadcasted_iota(jnp.int32, array.shape, 1)
    return jnp.where((rows == row) & (columns == column), value, array)


def store_pieces(out, array):
    band = array.shape[1]
    pieces = [array[:, place : place + LANES] for place in range(0, band, LANES)]
    flat = pieces[0] if len(pieces) == 1 else jnp.concatenate(pieces, axis=0)
    out[...] = flat.reshape(out.shape)


def load_pieces(ref, band):
    flat = ref[...].reshape(band * band // LANES, LANES)
    pieces = [flat[place : place + band] for place in range(0, flat.shape[0], band)]
    return pieces[0] if len(pieces) == 1 else jnp.concatenate(pieces, axis=1)


def mask_kernel(mask_hbm, table_hbm, out, mask, table, even, odd, sems):
    count, rows_here, chunk = mask.shape
    band = even.shape[1] // 2 * 2
    half = band // 2
    blocks = chunk // LANES
    pairs = count // 2
    order = [place + side * pairs for place in range(pairs) for side in range(2)]

    def copy(place):
        columns = pl.ds(place * chunk, chunk)
        return pltpu.make_async_copy(mask_hbm.at[:, columns], mask.at[place], sems.at[place])

    copy_table = pltpu.make_async_copy(table_hbm, table, sems.at[count])
    copy(order[0]).start()
    copy(order[1]).start()
    copy_table.start()
    for place in order[2:]:
        copy(place).start()
    copy_table.wait()
    line = jnp.zeros((1, LANES), f32)
    for place in range(pairs):
        copy(place).wait()
        copy(place + pairs).wait()
        near = jnp.tanh(mask[place])
        far = jnp.tanh(mask[place + pairs])
        hi, lo = split(basis_rows(table, place * blocks, blocks))
        for total, value, columns in (
            (even, near + far, slice(0, half)),
            (odd, near - far, slice(half, band)),
        ):
            weights = jnp.concatenate([hi[:, columns], lo[:, columns]], axis=1)
            product = dot(jnp.concatenate(split(value), axis=0), weights)
            if place == 0:
                total[...] = product
            else:
                total[...] += product
        both_sum = jnp.sum(near + far, axis=0, keepdims=True)
        for start in range(0, chunk, LANES):
            line += both_sum[:, start : start + LANES]
    parts = []
    for total in (even, odd):
        part = total[:rows_here, :] + total[rows_here:, :]
        parts.append(part[:, :half] + part[:, half:])
    row_part = jnp.concatenate(parts, axis=1)
    rows = split(basis_rows(table, lax.axis_index("px"), 1))
    packed = dot_split(rows, split(row_part), 0, 0)
    edge_row, edge_col = edges(table)
    edge_u = jnp.sum(edge_col * row_part[:, 0:1])
    edge_v = jnp.sum(edge_row * line)
    packed = put(put(packed, half - 1, 1, edge_u), 1, half - 1, edge_v)
    store_pieces(out, packed)


def prepare_kernel(
    corner,
    extent,
    y_big,
    y_fine,
    after,
    mask_hbm,
    target,
    y_rows,
    y_cols,
    slope,
    sem,
):
    band = y_fine.shape[2]
    rows_here, image = target.shape
    cols_here = slope.shape[1]
    place_px = lax.axis_index("px")
    place_cond = lax.axis_index("cond")
    mine = pl.ds(pl.multiple_of(place_cond * cols_here, cols_here), cols_here)
    copy_mask = pltpu.make_async_copy(mask_hbm.at[:, mine], slope, sem)
    copy_mask.start()

    rects = corner.shape[1]
    top = corner[0:1, :]
    bottom = top + extent[0:1, :]
    left = corner[1:2, :]
    right = left + extent[1:2, :]
    places = place_px * rows_here + lax.broadcasted_iota(jnp.int32, (rows_here, rects), 0)
    rows_in = jnp.where((places >= top) & (places < bottom), 1.0, 0.0).astype(bf16)
    for start, count, first, stride in column_runs(band, image):
        places = first + stride * lax.broadcasted_iota(jnp.int32, (count, rects), 0)
        cols_in = jnp.where((places >= left) & (places < right), 1.0, 0.0).astype(bf16)
        target[:, start : start + count] = jnp.minimum(dot(rows_in, cols_in, 1, 1), 1.0)

    big_cos = y_big[0, pl.ds(place_px, 1), :]
    big_sin = y_big[1, pl.ds(place_px, 1), :]
    cos_y = (big_cos * y_fine[0] - big_sin * y_fine[1]) * (1.0 / band)
    sin_y = (big_sin * y_fine[0] + big_cos * y_fine[1]) * (1.0 / band)
    waves = jnp.concatenate(
        [
            jnp.concatenate([cos_y, 0.0 - sin_y], axis=1),
            jnp.concatenate([sin_y, cos_y], axis=1),
        ],
        axis=0,
    )
    waves_hi, waves_lo = split(waves)
    y_rows[...] = jnp.concatenate([waves_hi, waves_lo], axis=0)
    waves_hi, waves_lo = waves_hi.astype(f32), waves_lo.astype(f32)
    stacked = jnp.concatenate([waves_hi, waves_hi, waves_lo], axis=0)
    y_cols[...] = jnp.transpose(stacked).astype(bf16)

    copy_mask.wait()
    for start in range(0, cols_here, LANES):
        here = pl.ds(start, LANES)
        transmit = jnp.tanh(slope[:, here])
        slope[:, here] = 1.0 - transmit * transmit


def field_kernel(
    cutoff_hbm,
    weight_hbm,
    dose_hbm,
    packed_hbm,
    both_hbm,
    y_rows_hbm,
    kernels,
    x_hbm,
    up_hbm,
    target_hbm,
    y_cols_hbm,
    both_t_hbm,
    out,
    cutoff,
    weight,
    dose,
    packed,
    both,
    y_rows,
    kern,
    x_wave,
    up,
    target,
    y_cols,
    both_t,
    spec,
    radius,
    prod_hi,
    prod_lo,
    wide_hi,
    wide_lo,
    deep_hi,
    deep_lo,
    cs,
    back,
    gs,
    sems,
    kern_sems,
    *,
    width,
):
    count, _, band, _ = kern.shape
    rows_here, image = target.shape
    half = band // 2
    total_rows = count * rows_here
    part = 64
    pairs = (
        (packed_hbm, packed),
        (cutoff_hbm, cutoff),
        (weight_hbm, weight),
        (dose_hbm, dose),
        (both_hbm, both),
        (y_rows_hbm, y_rows),
        (x_hbm, x_wave),
        (up_hbm, up),
        (target_hbm, target),
        (y_cols_hbm, y_cols),
        (both_t_hbm, both_t),
    )
    copies = [pltpu.make_async_copy(*pair, sems.at[place]) for place, pair in enumerate(pairs)]
    copy_x, copy_up, copy_target, copy_y_cols, copy_both_t = copies[6:]

    def copy(place):
        return pltpu.make_async_copy(kernels.at[0, place], kern.at[place], kern_sems.at[place])

    for early in copies[:6]:
        early.start()
    later = [copy(place) for place in range(count)] + copies[6:]
    for item in later[:AHEAD]:
        item.start()
    fu = lax.broadcasted_iota(jnp.int32, (band, band), 0) - half
    fv = lax.broadcasted_iota(jnp.int32, (band, band), 1) - half
    radius[...] = fu * fu + fv * fv
    for early in copies[:6]:
        early.wait()

    box = load_pieces(packed, band)
    edge_u = box[half - 1 : half, 1:2] * (1.0 / width)
    edge_v = box[1:2, half - 1 : half] * (1.0 / width)
    box_hi, box_lo = split(box * (1.0 / width))
    opened = dot(both[...], box_hi) + dot(both[...], box_lo)
    box_hi, box_lo = split(opened)
    opened = dot(box_hi, both[...], 1, 1) + dot(box_lo, both[...], 1, 1)
    spec_im = opened[band:, :band] + opened[:band, band:]
    spec[0] = opened[:band, :band] - opened[band:, band:]
    at_u = (fu == -half) & (fv == 0)
    at_v = (fu == 0) & (fv == -half)
    spec[1] = spec_im + jnp.where(at_u, edge_u, 0.0) + jnp.where(at_v, edge_v, 0.0)

    for place in range(count):
        copy(place).wait()
        if place + AHEAD < len(later):
            later[place + AHEAD].start()
        limit = cutoff[0, place] * cutoff[0, place]
        slot = place % prod_hi.shape[0]
        for start in range(0, band, part):
            here = pl.ds(start, part)
            there = pl.ds(band + start, part)
            inside = radius[here, :] <= limit
            k_re = jnp.where(inside, kern[place, 0, here, :], 0.0)
            k_im = jnp.where(inside, kern[place, 1, here, :], 0.0)
            kern[place, 0, here, :] = k_re
            kern[place, 1, here, :] = k_im
            s_re = spec[0, here, :]
            s_im = spec[1, here, :]
            re_hi, re_lo = split(k_re * s_re - k_im * s_im)
            im_hi, im_lo = split(k_re * s_im + k_im * s_re)
            prod_hi[slot, here, :] = re_hi
            prod_lo[slot, here, :] = re_lo
            prod_hi[slot, there, :] = im_hi
            prod_lo[slot, there, :] = im_lo
        main = dot(y_rows[...], prod_hi[slot])
        rest = dot(y_rows[: 2 * rows_here, :], prod_lo[slot])
        hi, lo = split(main[: 2 * rows_here] + (main[2 * rows_here :] + rest))
        here = pl.ds(place * rows_here, rows_here)
        there = pl.ds(total_rows + place * rows_here, rows_here)
        wide_hi[here, :] = hi[:rows_here]
        wide_lo[here, :] = lo[:rows_here]
        wide_hi[there, :] = hi[rows_here:]
        wide_lo[there, :] = lo[rows_here:]

    for item in later[count + AHEAD :]:
        item.start()
    copy_x.wait()
    cs[...] = dot_split((wide_hi[...], wide_lo[...]), (x_wave[0], x_wave[1]))

    def fields(place):
        here = pl.ds(place * rows_here, rows_here)
        there = pl.ds(total_rows + place * rows_here, rows_here)
        c_re = cs[here, :band]
        s_re = cs[here, band:]
        c_im = cs[there, :band]
        s_im = cs[there, band:]
        return (c_re - s_im, c_im + s_re, c_re + s_im, c_im - s_re), here, there

    plus = jnp.zeros((rows_here, band), f32)
    minus = jnp.zeros((rows_here, band), f32)
    for place in range(count):
        (p_re, p_im, m_re, m_im), _, _ = fields(place)
        scale = weight[0, place]
        plus += scale * (p_re * p_re + p_im * p_im)
        minus += scale * (m_re * m_re + m_im * m_im)
    dose_here = dose[0]
    scale = 2.0 * (width / band) * steepness * dose_here

    def slope_of(intensity, start):
        level = steepness * (dose_here * intensity - threshold)
        resist = 1.0 / (1.0 + jnp.exp(0.0 - level))
        aim = target[:, start : start + intensity.shape[1]]
        return scale * (resist - aim) * resist * (1.0 - resist)

    def resample(value, rows, transposed):
        hi, lo = split(value)
        dim = 1 if transposed else 0
        main = dot(jnp.concatenate([hi, lo], axis=0), up[0, rows, :], 1, dim)
        rest = dot(hi, up[1, rows, :], 1, dim)
        return main[:rows_here] + (main[rows_here:] + rest)

    sums, gaps, whole_rows = slice(0, band), slice(band, 2 * band), slice(2 * band, 4 * band)
    copy_up.wait()
    copy_target.wait()
    sum_part = resample(plus + minus, sums, False)
    gap_part = resample(plus - minus, gaps, False)
    fourth = resample(jnp.concatenate([plus, minus], axis=1), whole_rows, False)
    slope_plus = slope_of(plus, 0)
    slope_minus = slope_of(minus, band)
    right = slope_of(sum_part + gap_part, 2 * band)
    left = slope_of(sum_part - gap_part, 4 * band)
    fourth = resample(slope_of(fourth, 6 * band), whole_rows, True)
    sum_part = resample(right + left, sums, True)
    gap_part = resample(right - left, gaps, True)
    slope_plus = 2.0 * (slope_plus + (sum_part + gap_part) + fourth[:, :band])
    slope_minus = 2.0 * (slope_minus + (sum_part - gap_part) + fourth[:, band:])

    for place in range(count):
        (p_re, p_im, m_re, m_im), here, there = fields(place)
        scale = weight[0, place]
        plus = scale * slope_plus
        minus = scale * slope_minus
        p_re, p_im, m_re, m_im = plus * p_re, plus * p_im, minus * m_re, minus * m_im
        for rows, columns, value in (
            (here, slice(0, band), p_re + m_re),
            (here, slice(band, 2 * band), p_im - m_im),
            (there, slice(0, band), p_im + m_im),
            (there, slice(band, 2 * band), m_re - p_re),
        ):
            hi, lo = split(value)
            deep_hi[rows, columns] = hi
            deep_lo[rows, columns] = lo
    back[...] = dot_split((deep_hi[...], deep_lo[...]), (x_wave[0], x_wave[1]), 1, 1)

    copy_y_cols.wait()
    copy_both_t.wait()
    for place in range(count):
        here = pl.ds(place * rows_here, rows_here)
        there = pl.ds(total_rows + place * rows_here, rows_here)
        hi, lo = split(jnp.concatenate([back[here, :], back[there, :]], axis=0))
        grad = dot(y_cols[...], jnp.concatenate([hi, lo, hi], axis=0))
        for start in range(0, band, part):
            here = pl.ds(start, part)
            k_re = kern[place, 0, here, :]
            k_im = kern[place, 1, here, :]
            g_re = grad[start : start + part]
            g_im = grad[band + start : band + start + part]
            if place == 0:
                gs[0, here, :] = k_re * g_re + k_im * g_im
                gs[1, here, :] = k_re * g_im - k_im * g_re
            else:
                gs[0, here, :] += k_re * g_re + k_im * g_im
                gs[1, here, :] += k_re * g_im - k_im * g_re
    g_re = gs[0]
    g_im = gs[1]
    edge_u = g_im[0:1, half : half + 1]
    edge_v = g_im[half : half + 1, 0:1]
    re_hi, re_lo = split(g_re)
    im_hi, im_lo = split(g_im)
    even, odd = both_t[:, :band], both_t[:, band:]
    left = dot(even, re_hi) + dot(even, re_lo) + dot(odd, im_hi) + dot(odd, im_lo)
    right = dot(even, im_hi) + dot(even, im_lo) - dot(odd, re_hi) - dot(odd, re_lo)
    l_hi, l_lo = split(left)
    r_hi, r_lo = split(right)
    even, odd = both[:band, :], both[band:, :]
    folded = dot(l_hi, even) + dot(l_lo, even) + dot(r_hi, odd) + dot(r_lo, odd)
    store_pieces(out, put(put(folded, half - 1, 1, edge_u), 1, half - 1, edge_v))


def spread_kernel(packed, table, slope, out):
    count, cols_here = out.shape
    band = table.shape[1]
    half = band // 2
    step = min(512, cols_here)
    blocks = step // LANES
    width = (table.shape[0] - 2 * LANES - 8) // 2 * LANES
    first_block = lax.axis_index("cond") * (cols_here // LANES)
    box = load_pieces(packed, band) * (1.0 / width)
    edge_u = box[half - 1 : half, 1:2]
    edge_v = box[1:2, half - 1 : half]
    box = put(put(box, half - 1, 1, 0.0), 1, half - 1, 0.0)
    mixed_hi, mixed_lo = split(
        dot_split(split(basis_rows(table, lax.axis_index("px"), 1)), split(box))
    )
    mixed = jnp.concatenate([mixed_hi, mixed_lo], axis=0)
    edge_row, edge_col = edges(table)
    side = edge_u * edge_col + edge_v * edge_row
    for start in range(0, cols_here, step):
        hi, lo = split(basis_rows(table, first_block + start // LANES, blocks))
        main = dot(mixed, hi, 1, 1)
        rest = dot(mixed_hi, lo, 1, 1)
        grad = main[:count] + (main[count:] + rest)
        for inner in range(0, step, LANES):
            there = pl.ds(start + inner, LANES)
            out[:, there] = (grad[:, inner : inner + LANES] + side) * slope[:, there]


def params(mebibytes):
    return pltpu.CompilerParams(vmem_limit_bytes=mebibytes * 1024 * 1024)


vmem = pl.BlockSpec(memory_space=pltpu.VMEM)
anywhere = pl.BlockSpec(memory_space=pl.ANY)


def call_mask(mask_level, table, pieces):
    rows_here, width = mask_level.shape
    band = table.shape[1]
    chunk = min(1024, width // 4)
    steps = width // chunk
    return pl.pallas_call(
        mask_kernel,
        out_shape=jax.ShapeDtypeStruct(pieces, f32),
        in_specs=[anywhere, anywhere],
        out_specs=vmem,
        scratch_shapes=[
            pltpu.VMEM((steps, rows_here, chunk), f32),
            pltpu.VMEM(table.shape, f32),
            pltpu.VMEM((2 * rows_here, band), f32),
            pltpu.VMEM((2 * rows_here, band), f32),
            pltpu.SemaphoreType.DMA((steps + 1,)),
        ],
        compiler_params=params(ROOM),
        name="mask_rows",
    )(mask_level, table)


def call_prepare(shape_corner, shape_extent, after, mask_level, band, pencils, conds):
    rows_here, width = mask_level.shape
    image_rows = IMAGE // pencils
    cols_here = width // conds
    y_big = np.stack(wave(image_rows * np.arange(pencils), band, IMAGE)).astype(np.float32)
    y_fine = np.stack(wave(np.arange(image_rows), band, IMAGE)).astype(np.float32)
    shapes = [
        ((image_rows, IMAGE), f32),
        ((4 * image_rows, 2 * band), bf16),
        ((2 * band, 6 * image_rows), bf16),
        ((rows_here, cols_here), f32),
    ]
    return pl.pallas_call(
        prepare_kernel,
        out_shape=[jax.ShapeDtypeStruct(*shape) for shape in shapes],
        in_specs=[vmem] * 4 + [anywhere] * 2,
        out_specs=[vmem] * len(shapes),
        scratch_shapes=[pltpu.SemaphoreType.DMA],
        compiler_params=params(ROOM),
        cost_estimate=pl.CostEstimate(flops=10**9, bytes_accessed=2 * 10**7, transcendentals=10**6),
        name="prepare",
    )(shape_corner.T, shape_extent.T, y_big, y_fine, after, mask_level)


def call_field(
    band_cutoff, kernel_weight, dose_scale, packed, socs_kernels, target, y_rows, y_cols, width
):
    _, count, _, band, _ = socs_kernels.shape
    image_rows = target.shape[0]
    both = fold_table(band)
    x_cos, x_sin = wave(2 * np.arange(band) + 1, band, 4 * band)
    x_wave = np.stack(halves(np.concatenate([x_cos.T, x_sin.T], axis=1)))
    up = np.stack(halves(resample_table(band, IMAGE)))
    deep = 2 * count * image_rows
    return pl.pallas_call(
        functools.partial(field_kernel, width=width),
        out_shape=jax.ShapeDtypeStruct(packed.shape, f32),
        in_specs=[anywhere] * 12,
        out_specs=vmem,
        scratch_shapes=[
            pltpu.SMEM(band_cutoff.shape, jnp.int32),
            pltpu.SMEM(kernel_weight.shape, f32),
            pltpu.SMEM(dose_scale.shape, f32),
            pltpu.VMEM(packed.shape, f32),
            pltpu.VMEM(both.shape, bf16),
            pltpu.VMEM(y_rows.shape, bf16),
            pltpu.VMEM((count, 2, band, band), f32),
            pltpu.VMEM(x_wave.shape, bf16),
            pltpu.VMEM(up.shape, bf16),
            pltpu.VMEM(target.shape, f32),
            pltpu.VMEM(y_cols.shape, bf16),
            pltpu.VMEM(both.T.shape, bf16),
            pltpu.VMEM((2, band, band), f32),
            pltpu.VMEM((band, band), jnp.int32),
            pltpu.VMEM((SLOTS, 2 * band, band), bf16),
            pltpu.VMEM((SLOTS, 2 * band, band), bf16),
            pltpu.VMEM((deep, band), bf16),
            pltpu.VMEM((deep, band), bf16),
            pltpu.VMEM((deep, 2 * band), bf16),
            pltpu.VMEM((deep, 2 * band), bf16),
            pltpu.VMEM((deep, 2 * band), f32),
            pltpu.VMEM((deep, band), f32),
            pltpu.VMEM((2, band, band), f32),
            pltpu.SemaphoreType.DMA((11,)),
            pltpu.SemaphoreType.DMA((count,)),
        ],
        compiler_params=params(ROOM),
        name="image_rows",
    )(
        band_cutoff,
        kernel_weight,
        dose_scale,
        packed,
        both.astype(bf16),
        y_rows,
        socs_kernels,
        x_wave,
        up,
        target,
        y_cols,
        both.T.astype(bf16),
    )


def call_spread(folded, slope, table):
    return pl.pallas_call(
        spread_kernel,
        out_shape=jax.ShapeDtypeStruct(slope.shape, f32),
        in_specs=[vmem] * 3,
        out_specs=vmem,
        compiler_params=params(40),
        name="mask_gradient",
    )(folded, table, slope)


def local(
    mask_level, socs_kernels, band_cutoff, kernel_weight, dose_scale, shape_corner, shape_extent
):
    width = mask_level.shape[1]
    band = socs_kernels.shape[3]
    pencils = lax.axis_size("px")
    conds = lax.axis_size("cond")
    pieces = (pencils, band * band // LANES // pencils, LANES)
    table = basis_tables(band, width)

    packed = call_mask(mask_level, table, pieces)
    piece = collect(packed)
    target, y_rows, y_cols, slope = call_prepare(
        shape_corner, shape_extent, piece, mask_level, band, pencils, conds
    )
    packed = hand_out(piece, pieces)
    folded = call_field(
        band_cutoff, kernel_weight, dose_scale, packed, socs_kernels, target, y_rows, y_cols, width
    )
    piece = collect(folded)
    others = [
        lax.ppermute(piece, "cond", [(i, (i + d) % conds) for i in range(conds)])
        for d in range(1, conds)
    ]
    piece = functools.reduce(jnp.add, others, piece)
    folded = hand_out(piece, pieces)
    return call_spread(folded, slope, table)


def collect(packed):
    arrived = lax.all_to_all(packed, "px", split_axis=0, concat_axis=0, tiled=True)
    return jnp.sum(arrived, axis=0)


def hand_out(piece, pieces):
    outgoing = jnp.broadcast_to(piece[None], pieces)
    return lax.all_to_all(outgoing, "px", split_axis=0, concat_axis=0, tiled=True)


def solution(mesh):
    in_specs = (
        P("px", None),
        P("cond", None, None, None, None),
        P("cond", None),
        P("cond", None),
        P("cond"),
        P(),
        P(),
    )
    out_specs = P("px", "cond")
    return jax.shard_map(local, mesh=mesh, in_specs=in_specs, out_specs=out_specs, check_vma=False)
```
